256 devices in a mesh: depth: 16 (over y, x_lo, core), height: 16 (over z, x_hi).
Axes of the slice: x: 4 (x_hi: 2, x_lo: 2; x = x_hi * 2 + x_lo), y: 4, z: 8, core: 2. Of those that a mesh axis runs over, the one named last changes fastest.
Arguments:
- bottom: bfloat16 [16, 16, 32, 320], P('depth', None, None, 'height'), may hold values from -6 to 6
- skip: bfloat16 [32, 32, 64, 128], P('depth', 'height'), may hold values from -6 to 6
- upconv_kernel: bfloat16 [3, 3, 3, 320, 128], replicated, may hold values from -0.1875 to 0.1875
- w_first: bfloat16 [3, 3, 3, 256, 128], replicated, may hold values from -0.078125 to 0.078125
- w_second: bfloat16 [3, 3, 3, 128, 128], replicated, may hold values from -0.109375 to 0.109375
- cotangent: bfloat16 [32, 32, 64, 128], P('depth', 'height'), may hold values from -6 to 6
Outputs:
- result: bfloat16 [32, 32, 64, 128], P('depth', 'height')
- coarse_input_gradient: bfloat16 [16, 16, 32, 320], P('depth', None, None, 'height')
- grad_skip: bfloat16 [32, 32, 64, 128], P('depth', 'height')
- g_up: float32 [3, 3, 3, 320, 128], P(None, None, None, 'height', 'depth')
- g_first: float32 [3, 3, 3, 256, 128], P(None, None, None, 'height', 'depth')
- g_second: float32 [3, 3, 3, 128, 128], P(None, None, None, 'height', 'depth')
The draws below stay inside these ranges and needn't reach their ends.
All inputs are finite; a program needn't handle non-finite values.
Results may differ from the reference program's by a relative error of at most 0.015.
Values may be sent and summed in bfloat16 or wider, within the bound.
A program may use at most 192 MiB of HBM per device.

```python
import math
import jax
import jax.numpy as jnp
from jax import lax

CB = 320
CU = 128
CS = 128
CO = 128
GW = 64
CC = 256
GD = 32
GH = 32
VOXELS = 65536


def with_spikes(drawn, rng, source, target, blocks, factor):
    owner, partner = [(jnp.arange(drawn.shape[position]) // (drawn.shape[position] // blocks)).reshape([-1 if axis == position else 1 for axis in range(drawn.ndim)]) for position in (source, target)]
    chosen = jax.random.permutation(rng, blocks)[partner]
    strong = (owner == chosen) | (owner == (partner + blocks // 2) % blocks)
    return jnp.where(strong, factor * drawn, drawn)


def level_of(stream_key, extent, pieces, smallest, top_value):
    level, own = 1.0, jax.random.fold_in(stream_key, 6)
    for dim, shards_of in pieces:
        draws = jnp.exp(jax.random.uniform(jax.random.fold_in(own, dim), (shards_of,), jnp.float32, smallest / len(pieces), top_value / len(pieces)))
        level = level * jnp.repeat(draws, extent[dim] // shards_of).reshape([-1 if axis == dim else 1 for axis in range(len(extent))])
    return level


def noise(own_key, extent, width, reach, cuts=(), dtype=jnp.bfloat16):
    loudness = level_of(own_key, extent, cuts, -0.22, 0.18) if cuts else 1.0
    entries = jax.random.normal(own_key, extent, jnp.float32) * width * loudness
    return jnp.minimum(jnp.maximum(entries, -reach), reach).astype(dtype)


def heavy_noise(key, shape, spread, limit, cuts, heavy, held_as=jnp.bfloat16):
    drawn = spread * jax.random.normal(key, shape, jnp.float32)
    if cuts:
        drawn = drawn * level_of(key, shape, cuts, -0.22, 0.18)
    return jnp.clip(with_spikes(drawn, jax.random.fold_in(key, 3), *heavy), -limit, limit).astype(held_as)


def setup_inputs(seed: int = 0) -> dict:
    key_of = jax.random.split(jax.random.key(seed), 7)
    return {
        "bottom": noise(key_of[0], (GD // 2, GH // 2, GW // 2, CB), 1.0, 6.0, ((0, 16), (3, 16))),
        "skip": noise(key_of[1], (GD, GH, GW, CS), 1.0, 6.0, ((0, 16), (1, 16))),
        "upconv_kernel": noise(key_of[2], (3, 3, 3, CB, CU), (27 * CB // 8) ** -0.5, 0.1875),
        "w_first": noise(key_of[3], (3, 3, 3, CC, CO), (27 * CC) ** -0.5, 0.078125),
        "w_second": noise(key_of[4], (3, 3, 3, CO, CO), (27 * CO) ** -0.5, 0.109375),
        "cotangent": heavy_noise(key_of[5], (GD, GH, GW, CO), 1.0, 6.0, ((0, 16), (1, 16)), (0, 3, 16, 2.0)),
    }


TAP_TABLE = (((1, 0),), ((2, 0), (0, 1)))

def mult(left, right, contract):
    return lax.dot_general(left.astype(jnp.float32), right.astype(jnp.float32), (contract, ((), ())), precision=lax.Precision.HIGHEST)

def upsample(widened_volume, weight_tensor):
    coarse = (widened_volume.shape[0] - 1, widened_volume.shape[1] - 1, widened_volume.shape[2] - 1)
    chans = widened_volume.shape[3]
    outer = []
    for phase_d in range(2):
        middle = []
        for phase_h in range(2):
            inner = []
            for phase_w in range(2):
                summed = None
                for tap_d, shift_d in TAP_TABLE[phase_d]:
                    for tap_h, shift_h in TAP_TABLE[phase_h]:
                        for tap_w, shift_w in TAP_TABLE[phase_w]:
                            sliced = widened_volume[shift_d:shift_d + coarse[0], shift_h:shift_h + coarse[1], shift_w:shift_w + coarse[2]]
                            product = mult(sliced.reshape(-1, chans), weight_tensor[tap_d, tap_h, tap_w], ((1,), (0,)))
                            summed = product if summed is None else summed + product
                inner.append(summed)
            middle.append(jnp.stack(inner))
        outer.append(jnp.stack(middle))
    outc = weight_tensor.shape[4]
    stacked = jnp.stack(outer).reshape(2, 2, 2, coarse[0], coarse[1], coarse[2], outc)
    stacked = stacked.transpose(3, 0, 4, 1, 5, 2, 6)
    return stacked.reshape(2 * coarse[0], 2 * coarse[1], 2 * coarse[2], outc)

def reduce_resolution(widened_volume, weight_tensor):
    coarse = ((widened_volume.shape[0] - 1) // 2, (widened_volume.shape[1] - 1) // 2, (widened_volume.shape[2] - 1) // 2)
    chans = widened_volume.shape[3]
    summed = None
    for tap_d in range(3):
        for tap_h in range(3):
            for tap_w in range(3):
                sliced = widened_volume[tap_d:tap_d + 2 * coarse[0]:2, tap_h:tap_h + 2 * coarse[1]:2, tap_w:tap_w + 2 * coarse[2]:2]
                product = mult(sliced.reshape(-1, chans), weight_tensor[tap_d, tap_h, tap_w], ((1,), (1,)))
                summed = product if summed is None else summed + product
    return summed.reshape(coarse + (weight_tensor.shape[3],))

def up_weight_grad(coarse_in, widened_volume):
    shape = coarse_in.shape
    flat_in = coarse_in.reshape(-1, shape[3])
    listed = []
    for tap_d in range(3):
        for tap_h in range(3):
            for tap_w in range(3):
                sliced = widened_volume[tap_d:tap_d + 2 * shape[0]:2, tap_h:tap_h + 2 * shape[1]:2, tap_w:tap_w + 2 * shape[2]:2]
                listed.append(mult(flat_in, sliced.reshape(-1, widened_volume.shape[3]), ((0,), (0,))))
    return jnp.stack(listed).reshape(3, 3, 3, shape[3], widened_volume.shape[3])

def conv_same(padded, weight_tensor):
    cells = (padded.shape[0] - 2, padded.shape[1] - 2, padded.shape[2] - 2)
    chans = padded.shape[3]
    summed = None
    for tap_d in range(3):
        for tap_h in range(3):
            for tap_w in range(3):
                sliced = padded[tap_d:tap_d + cells[0], tap_h:tap_h + cells[1], tap_w:tap_w + cells[2]]
                product = mult(sliced.reshape(-1, chans), weight_tensor[tap_d, tap_h, tap_w], ((1,), (0,)))
                summed = product if summed is None else summed + product
    return summed.reshape(cells + (weight_tensor.shape[4],))

def conv_back(padded, weight_tensor):
    cells = (padded.shape[0] - 2, padded.shape[1] - 2, padded.shape[2] - 2)
    chans = padded.shape[3]
    summed = None
    for tap_d in range(3):
        for tap_h in range(3):
            for tap_w in range(3):
                sliced = padded[2 - tap_d:2 - tap_d + cells[0], 2 - tap_h:2 - tap_h + cells[1], 2 - tap_w:2 - tap_w + cells[2]]
                product = mult(sliced.reshape(-1, chans), weight_tensor[tap_d, tap_h, tap_w], ((1,), (1,)))
                summed = product if summed is None else summed + product
    return summed.reshape(cells + (weight_tensor.shape[3],))

def conv_weight(padded, error):
    cells = error.shape[:3]
    flat_err = error.reshape(-1, error.shape[3])
    listed = []
    for tap_d in range(3):
        for tap_h in range(3):
            for tap_w in range(3):
                sliced = padded[tap_d:tap_d + cells[0], tap_h:tap_h + cells[1], tap_w:tap_w + cells[2]]
                listed.append(mult(sliced.reshape(-1, padded.shape[3]), flat_err, ((0,), (0,))))
    return jnp.stack(listed).reshape(3, 3, 3, padded.shape[3], error.shape[3])

def slope(values):
    sig = jax.nn.sigmoid(values)
    return sig * (1.0 + values * (1.0 - sig))

def pad_all(field):
    return jnp.pad(field, ((1, 1), (1, 1), (1, 1), (0, 0)))

def reference(bottom, skip, upconv_kernel, w_first, w_second, cotangent):
    factor = 1.0 / math.sqrt(VOXELS)
    widened_volume = jnp.pad(bottom, ((0, 1), (0, 1), (0, 1), (0, 0)))
    upsampled = upsample(widened_volume, upconv_kernel).astype(jnp.bfloat16)
    joined = jnp.concatenate([upsampled, skip], 3)
    joined_pad = pad_all(joined)
    first_pre = conv_same(joined_pad, w_first)
    hidden = jax.nn.silu(first_pre).astype(jnp.bfloat16)
    hidden_pad = pad_all(hidden)
    second_pre = conv_same(hidden_pad, w_second)
    result = jax.nn.silu(second_pre).astype(jnp.bfloat16)
    err_second = (cotangent.astype(jnp.float32) * slope(second_pre)).astype(jnp.bfloat16)
    back_hidden = conv_back(pad_all(err_second), w_second)
    err_first = (back_hidden * slope(first_pre)).astype(jnp.bfloat16)
    back_joined = conv_back(pad_all(err_first), w_first)
    back_up = back_joined[..., :CU].astype(jnp.bfloat16)
    grad_skip = back_joined[..., CU:].astype(jnp.bfloat16)
    lower_level = jnp.pad(back_up, ((1, 0), (1, 0), (1, 0), (0, 0)))
    coarse_input_gradient = reduce_resolution(lower_level, upconv_kernel).astype(jnp.bfloat16)
    g_second = conv_weight(hidden_pad, err_second) * factor
    g_first = conv_weight(joined_pad, err_first) * factor
    g_up = up_weight_grad(bottom, lower_level) * factor
    return (result, coarse_input_gradient, grad_skip, g_up, g_first, g_second)
```

```python
import functools
import math

import jax
import jax.numpy as jnp
from jax import lax
from jax.experimental import pallas as pl
from jax.experimental.pallas import tpu as pltpu
from jax.sharding import PartitionSpec as P

MESH = pl.DeviceIdType.MESH
F32 = jnp.float32
BF16 = jnp.bfloat16
GRID9 = [(a, b) for a in range(3) for b in range(3)]
OTHERS = [(a, b) for a in (-1, 0, 1) for b in (-1, 0, 1) if (a, b) != (0, 0)]
NT = (((1,), (1,)), ((), ()))
PARITY_SHIFT = {0: (1, 1), 1: (0, 0), 2: (1, 0)}


def round_up(value, unit):
    return -(-value // unit) * unit


def remote(src, dst, send, recv, target):
    return pltpu.make_async_remote_copy(
        src_ref=src, dst_ref=dst, send_sem=send, recv_sem=recv, device_id=target, device_id_type=MESH
    )


class Spread:
    def __init__(self, me, count, target, source, slot, send, recv):
        self.me, self.count, self.target = me, count, target
        self.source, self.slot, self.send, self.recv = source, slot, send, recv

    def each(self, act):
        def step(j, carry):
            act(j)
            return carry

        lax.fori_loop(1, self.count, step, 0)

    def outgoing(self, j):
        peer = lax.rem(self.me + j, self.count)
        return remote(
            self.source(peer), self.slot(self.me), self.send.at[peer], self.recv.at[self.me], self.target(peer)
        )

    def incoming(self, j):
        peer = lax.rem(self.me + self.count - j, self.count)
        return remote(
            self.source(peer), self.slot(peer), self.send.at[peer], self.recv.at[peer], self.target(peer)
        )

    def start(self):
        self.each(lambda j: self.outgoing(j).start())

    def wait_recv(self):
        self.each(lambda j: self.incoming(j).wait_recv())

    def wait_send(self):
        self.each(lambda j: self.outgoing(j).wait_send())


def shift_rows(value, by, period):
    rows = value.shape[0]
    row = lax.broadcasted_iota(jnp.int32, value.shape, 0) % period
    edge = 0 if by > 0 else period - 1
    return jnp.where(row == edge, 0.0, pltpu.roll(value, by % rows, 0))


def shift_lanes(value, by, period):
    lanes = value.shape[1]
    lane = lax.broadcasted_iota(jnp.int32, value.shape, 1) % period
    edge = 0 if by > 0 else period - 1
    return jnp.where(lane == edge, 0.0, pltpu.roll(value, by % lanes, 1))


def slope(values):
    sig = jax.nn.sigmoid(values)
    return sig * (1.0 + values * (1.0 - sig))


def dot(a, b, dims=(((1,), (0,)), ((), ()))):
    return lax.dot_general(a, b, dims, preferred_element_type=F32)


def body(
    nd, nh, factor,
    bottom, skip, upw_hbm, w1_hbm, w2_hbm, cot_hbm,
    result, cgrad, gskip, gup, gfirst, gsecond,
    upw, w1, w2, cot, brecv, bg, up32, joined, jg, fp, hid, hg, e2, e1, et2s, et2r, et1s, et1r,
    bu32, bu, buts, butr, cgs, cgr, vt0, vt1, acc1, acc2, gs2, gr2, gs1, gr1, gsu, gru,
    ssem, rsem, hs, hr, loc,
):
    d = lax.axis_index("depth")
    h = lax.axis_index("height")
    cb = bottom.shape[3]
    cw = bottom.shape[2]
    cu = upw.shape[2]
    no = cu // nd
    taps = 27

    weights = [
        pltpu.make_async_copy(upw_hbm, upw, loc.at[0]),
        pltpu.make_async_copy(w1_hbm, w1, loc.at[1]),
        pltpu.make_async_copy(w2_hbm, w2, loc.at[2]),
        pltpu.make_async_copy(cot_hbm, cot, loc.at[3]),
    ]
    own_skip = pltpu.make_async_copy(skip, joined.at[pl.ds(1, 2), pl.ds(1, 2), :, pl.ds(cu, cu)], loc.at[4])
    first_row = lambda p: jnp.clip(p - 1, 0, nh - 3)
    own_rows = pltpu.make_async_copy(bottom.at[0, pl.ds(first_row(h), 3)], brecv.at[h], loc.at[5])

    joined[...] = jnp.zeros_like(joined)
    hid[...] = jnp.zeros_like(hid)
    e2[...] = jnp.zeros_like(e2)
    e1[...] = jnp.zeros_like(e1)
    bu[...] = jnp.zeros_like(bu)

    own_rows.start()
    own_skip.start()
    for copy in weights:
        copy.start()

    barrier = pltpu.get_barrier_semaphore()

    def greet_line(count, target):
        def step(j, carry):
            pl.semaphore_signal(barrier, inc=1, device_id=target(j), device_id_type=MESH)
            return carry

        lax.fori_loop(1, count, step, 0)

    greet_line(nh, lambda j: (d, lax.rem(h + j, nh)))
    greet_line(nd, lambda j: (lax.rem(d + j, nd), h))

    def there(dd, dh):
        ok = None
        for pos, step, count in ((d, dd, nd), (h, dh, nh)):
            if step:
                cond = pos > 0 if step < 0 else pos < count - 1
                ok = cond if ok is None else jnp.logical_and(ok, cond)
        return ok

    for dd in (-1, 1):
        for dh in (-1, 1):
            corner = (lax.rem(d + dd + nd, nd), lax.rem(h + dh + nh, nh))
            pl.semaphore_signal(barrier, inc=1, device_id=corner, device_id_type=MESH)
    pl.semaphore_wait(barrier, nd + nh + 2)

    def src_part(step):
        return {0: pl.ds(1, 2), 1: pl.ds(2, 1), -1: pl.ds(1, 1)}[step]

    def own_part(step):
        return {0: pl.ds(0, 2), 1: pl.ds(1, 1), -1: pl.ds(0, 1)}[step]

    def dst_part(step):
        return {0: pl.ds(1, 2), 1: pl.ds(0, 1), -1: pl.ds(3, 1)}[step]

    def halo(phase, copy_of, directions=OTHERS):
        def copies(dd, dh):
            slot = (dd + 1) * 3 + dh + 1
            src, dst = copy_of(dd, dh)
            return remote(src, dst, hs.at[phase, slot], hr.at[phase, slot], (d + dd, h + dh))

        def start():
            for dd, dh in directions:
                @pl.when(there(dd, dh))
                def _(dd=dd, dh=dh):
                    copies(dd, dh).start()

        def wait_recv():
            for dd, dh in directions:
                @pl.when(there(-dd, -dh))
                def _(dd=dd, dh=dh):
                    copies(dd, dh).wait_recv()

        def wait_send():
            for dd, dh in directions:
                @pl.when(there(dd, dh))
                def _(dd=dd, dh=dh):
                    copies(dd, dh).wait_send()

        return start, wait_recv, wait_send

    def field_halo(phase, field):
        return halo(
            phase,
            lambda dd, dh: (
                field.at[src_part(dd), src_part(dh)],
                field.at[dst_part(dd), dst_part(dh)],
            ),
        )

    along_h = lambda p: (d, p)
    along_d = lambda p: (p, h)

    def line_h(phase, source, slot):
        return Spread(h, nh, along_h, source, slot, ssem.at[phase], rsem.at[phase])

    def line_d(phase, source, slot):
        return Spread(d, nd, along_d, source, slot, ssem.at[phase], rsem.at[phase])

    sends = []
    rows_out = line_h(0, lambda p: bottom.at[0, pl.ds(first_row(p), 3)], lambda s: brecv.at[s])
    rows_out.start()
    skip_start, skip_recv, skip_send = halo(
        0,
        lambda dd, dh: (
            skip.at[own_part(dd), own_part(dh)],
            joined.at[dst_part(dd), dst_part(dh), :, pl.ds(cu, cu)],
        ),
    )
    skip_start()
    own_rows.wait()
    rows_out.wait_recv()
    for r in range(3):
        row = h - 1 + r
        here = jnp.logical_and(row >= 0, row < nh)
        at = jnp.clip(row - first_row(h), 0, 2)
        pieces = [brecv[c, at].astype(F32) for c in range(nh)]
        line = jnp.concatenate(pieces, axis=1)
        bg[d, r] = jnp.where(here, line, 0.0).astype(BF16)

    near_start, _, near_send = halo(
        1, lambda dd, dh: (bg.at[d, pl.ds(0, 1)], bg.at[d, pl.ds(0, 1)]), [(-1, 0), (1, 0)]
    )
    near_start()
    planes_out = line_d(1, lambda p: bg.at[d, pl.ds(1, 2)], lambda s: bg.at[s, pl.ds(1, 2)])
    planes_out.start()
    weights[0].wait()

    for dd in (-1, 1):
        @pl.when(there(dd, 0))
        def _(dd=dd):
            peer = d + dd
            slot = (-dd + 1) * 3 + 1
            remote(
                bg.at[peer, pl.ds(0, 1)], bg.at[peer, pl.ds(0, 1)], hs.at[1, slot], hr.at[1, slot], (peer, h)
            ).wait_recv()
    planes_out.wait_recv()

    coarse = []
    for s in range(3):
        plane = d - 1 + s
        here = jnp.logical_and(plane >= 0, plane < nd)
        value = bg[jnp.clip(plane, 0, nd - 1)]
        coarse.append(jnp.where(here, value, jnp.zeros_like(value)))
    coarse = jnp.stack(coarse)
    first_of = {0: 1, 1: 1, 2: 0}
    for gd in range(2):
        for gh in range(2):
            total = None
            for kd in ((1,), (0, 2))[gd]:
                for kh in ((1,), (0, 2))[gh]:
                    a, b = first_of[kd], first_of[kh]
                    lhs = coarse[a : a + 2, b : b + 2].reshape(4 * cw, -1)
                    t = kd * 9 + kh * 3
                    rhs = jnp.concatenate([upw[t], upw[t + 1], upw[t + 2]], axis=1)
                    part = dot(lhs, rhs)
                    total = part if total is None else total + part
            even = total[:, cu : 2 * cu]
            odd = total[:, 2 * cu :] + shift_rows(total[:, :cu], -1, cw)
            for i in range(2):
                for j in range(2):
                    at = (i * 2 + j) * cw
                    fd, fh = 2 * i + 1 - gd, 2 * j + 1 - gh
                    up32[fd, fh, pl.ds(0, cw, stride=2), :] = even[at : at + cw]
                    up32[fd, fh, pl.ds(1, cw, stride=2), :] = odd[at : at + cw]
    for fd in range(4):
        for fh in range(4):
            inside = None
            for pos, f, count in ((d, fd, nd), (h, fh, nh)):
                cond = None
                if f == 0:
                    cond = pos > 0
                if f == 3:
                    cond = pos < count - 1
                if cond is not None:
                    inside = cond if inside is None else jnp.logical_and(inside, cond)
            value = up32[fd, fh]
            if inside is not None:
                value = jnp.where(inside, value, 0.0)
            joined[fd, fh, :, 0:cu] = value.astype(BF16)

    own_skip.wait()
    skip_recv()
    weights[1].wait()
    cells = 4 * 2 * cw

    def conv(field, weight):
        chans = field.shape[3]
        lhs = jnp.concatenate(
            [field[a : a + 2, b : b + 2].reshape(cells, chans) for a, b in GRID9], axis=1
        )
        rhs = jnp.concatenate(
            [
                jnp.concatenate([weight[(a * 3 + b) * 3 + c] for c in range(3)], axis=1)
                for a, b in GRID9
            ],
            axis=0,
        )
        y = dot(lhs, rhs)
        n = weight.shape[2]
        return shift_rows(y[:, :n], 1, 2 * cw) + y[:, n : 2 * n] + shift_rows(y[:, 2 * n :], -1, 2 * cw)

    def conv_back(field, weight):
        chans = field.shape[3]
        lhs = jnp.concatenate(
            [field[2 - a : 4 - a, 2 - b : 4 - b].reshape(cells, chans) for a, b in GRID9], axis=1
        )
        rhs = jnp.concatenate(
            [
                jnp.concatenate([weight[(a * 3 + b) * 3 + c] for a, b in GRID9], axis=1)
                for c in range(3)
            ],
            axis=0,
        )
        y = dot(lhs, rhs, NT)
        n = weight.shape[1]
        return shift_rows(y[:, :n], -1, 2 * cw) + y[:, n : 2 * n] + shift_rows(y[:, 2 * n :], 1, 2 * cw)

    first_pre = conv(joined, w1)
    fp[...] = first_pre
    hidden = (first_pre * jax.nn.sigmoid(first_pre)).astype(BF16)
    hid[1:3, 1:3] = hidden.reshape(2, 2, 2 * cw, cu)
    hid_start, hid_recv, hid_send = field_halo(2, hid)
    hid_start()
    hg[d] = hidden
    jg[d] = joined[1:3, 1:3].reshape(cells, 2 * cu)
    hid_out = line_d(2, lambda p: hg.at[d], lambda s: hg.at[s])
    joined_out = line_d(3, lambda p: jg.at[d], lambda s: jg.at[s])
    hid_out.start()

    weights[2].wait()
    weights[3].wait()
    hid_recv()
    second_pre = conv(hid, w2)
    result[...] = (second_pre * jax.nn.sigmoid(second_pre)).astype(BF16).reshape(2, 2, 2 * cw, cu)
    err2 = (cot[...].reshape(cells, cu).astype(F32) * slope(second_pre)).astype(BF16)
    e2[1:3, 1:3] = err2.reshape(2, 2, 2 * cw, cu)
    e2_start, e2_recv, e2_send = field_halo(3, e2)
    e2_start()
    joined_out.start()

    e2_recv()
    err1 = (conv_back(e2, w2) * slope(fp[...])).astype(BF16)
    e1[1:3, 1:3] = err1.reshape(2, 2, 2 * cw, cu)
    e1_start, e1_recv, e1_send = field_halo(4, e1)
    e1_start()

    def flip(field, phase, out, into):
        value = field[1:3].reshape(2 * cells, cu).astype(F32)
        out[...] = value.T
        into[d] = out[pl.ds(pl.multiple_of(d * no, no), no)]
        spread = line_d(
            phase, lambda p: out.at[pl.ds(pl.multiple_of(p * no, no), no)], lambda s: into.at[s]
        )
        spread.start()
        return spread

    e2_out = flip(e2, 4, et2s, et2r)

    e1_recv()
    back = conv_back(e1, w1)
    bu32[...] = back[:, :cu].reshape(2, 2, 2 * cw, cu)
    for i in range(2):
        for j in range(2):
            for par in range(2):
                bu[1 + i, 1 + j, par] = bu32[i, j, pl.ds(par, cw, stride=2), :].astype(BF16)
    bu_start, bu_recv, bu_send = halo(
        5,
        lambda dd, dh: (
            bu.at[pl.ds(2, 1) if dd else pl.ds(1, 2), pl.ds(2, 1) if dh else pl.ds(1, 2)],
            bu.at[pl.ds(0, 1) if dd else pl.ds(1, 2), pl.ds(0, 1) if dh else pl.ds(1, 2)],
        ),
        [(1, 0), (0, 1), (1, 1)],
    )
    bu_start()
    buts[...] = bu[1:3, 1:3].reshape(cells, cu).astype(F32).T
    butr[d] = buts[pl.ds(pl.multiple_of(d * no, no), no)]
    bu_out = line_d(
        5, lambda p: buts.at[pl.ds(pl.multiple_of(p * no, no), no)], lambda s: butr.at[s]
    )
    bu_out.start()
    e1_out = flip(e1, 6, et1s, et1r)
    gskip[...] = back[:, cu:].astype(BF16).reshape(2, 2, 2 * cw, cu)

    def weight_grad(into, gathered, acc):
        a0 = into[:, :, 0 * 128 : 1 * 128].reshape(nd * no, 128)
        b0 = into[:, :, 1 * 128 : 2 * 128].reshape(nd * no, 128)
        a1 = into[:, :, 2 * 128 : 3 * 128].reshape(nd * no, 128)
        b1 = into[:, :, 3 * 128 : 4 * 128].reshape(nd * no, 128)
        lane = lax.broadcasted_iota(jnp.int32, a0.shape, 1)
        zero = jnp.zeros((9 * no, 128), F32)
        for low, high, vt in ((a0, b0, vt0), (a1, b1, vt1)):
            vt[0] = zero
            vt[nd + 1] = zero
            mid = jnp.where(lane < 64, pltpu.roll(low, 64, 1), pltpu.roll(high, 64, 1))
            for kh, rows in enumerate((high, mid, low)):
                for kw in range(3):
                    value = rows if kw == 1 else shift_lanes(rows, kw - 1, 2 * cw)
                    at = (kh * 3 + kw) * no
                    vt[1 : nd + 1, at : at + no, :] = value.reshape(nd, no, 128)
        acc[...] = jnp.zeros_like(acc)

        def step(j, carry):
            lhs = jnp.concatenate(
                [
                    jnp.concatenate([vt1[j + 1], vt0[j + 2]], axis=1),
                    jnp.concatenate([vt0[j + 1], vt1[j + 1]], axis=1),
                    jnp.concatenate([vt1[j], vt0[j + 1]], axis=1),
                ],
                axis=0,
            ).astype(BF16)
            acc[...] += dot(lhs, gathered[j])
            return carry

        lax.fori_loop(0, nd, step, 0)
        return acc[...] * factor

    def flipped(value):
        rows, lanes = value.shape
        tall, wide = round_up(rows, 128), round_up(lanes, 128)
        if tall > rows:
            value = jnp.concatenate([value, jnp.zeros((tall - rows, lanes), F32)], axis=0)
        if wide > lanes:
            value = jnp.concatenate([value, jnp.zeros((tall, wide - lanes), F32)], axis=1)
        return value.T

    def scatter_rows(phase, value, chunk, out, into):
        turned = flipped(value)
        for c in range(nh):
            out[c, 0:chunk, :] = turned[c * chunk : (c + 1) * chunk]
        into[h] = out[h]
        spread = line_h(phase, lambda p: out.at[p], lambda s: into.at[s])
        spread.start()
        return spread

    e2_out.wait_recv()
    hid_out.wait_recv()
    g2_out = scatter_rows(7, weight_grad(et2r, hg, acc2), gsecond.shape[1], gs2, gr2)

    bu_recv()
    around = lambda par: [bu[a, b, par].reshape(cw, cu) for a, b in GRID9]
    lhs = jnp.concatenate(around(0) + around(1), axis=1)
    rhs = jnp.concatenate(
        [upw[(a * 3 + b) * 3 + 1] for a, b in GRID9] + [upw[(a * 3 + b) * 3 + 2] for a, b in GRID9], axis=1
    )
    same = dot(lhs, rhs, NT)
    lhs = jnp.concatenate(around(1), axis=1)
    rhs = jnp.concatenate([upw[(a * 3 + b) * 3] for a, b in GRID9], axis=1)
    block_grad = same + shift_rows(dot(lhs, rhs, NT), 1, cw)
    for c in range(nh):
        cgs[c] = block_grad[:, c * cb : (c + 1) * cb].astype(BF16)
    cgr[h] = cgs[h]
    cg_out = line_h(8, lambda p: cgs.at[p], lambda s: cgr.at[s])
    cg_out.start()

    bu_out.wait_recv()
    per = 128 // cw
    lane = lax.broadcasted_iota(jnp.int32, (no, 128), 1) // cw
    phases = {}
    for pd in range(2):
        for p in range(per):
            groups = []
            for g in range(nd // per):
                total = None
                for s in range(per):
                    piece = butr[g * per + s, :, pd * 128 : (pd + 1) * 128]
                    turn = ((s - p) * cw) % 128
                    piece = pltpu.roll(piece, turn, 1) if turn else piece
                    total = piece if total is None else jnp.where(lane == s, piece, total)
                groups.append(total)
            phases[pd, p // 2, p % 2] = jnp.concatenate(groups, axis=1) if len(groups) > 1 else groups[0]
    wide = lax.broadcasted_iota(jnp.int32, (no, nd * cw), 1)

    def tap_rows(kd, kh, kw):
        pd, sd = PARITY_SHIFT[kd]
        ph, _ = PARITY_SHIFT[kh]
        pw, sw = PARITY_SHIFT[kw]
        value = phases[pd, ph, pw]
        if sw:
            value = shift_lanes(value, 1, cw)
        if sd:
            value = jnp.where(wide < cw, 0.0, pltpu.roll(value, cw, 1))
        return value

    products = {}
    for sh, khs in ((0, (1, 2)), (1, (0,))):
        order = [(kd, kh, kw) for kh in khs for kd in range(3) for kw in range(3)]
        lhs = jnp.concatenate([tap_rows(*k) for k in order], axis=0).astype(BF16)
        rhs = bg[:, 1 + sh].reshape(nd * cw, -1)
        value = dot(lhs, rhs)
        for i, k in enumerate(order):
            products[k] = value[i * no : (i + 1) * no]
    grad_up = jnp.concatenate(
        [products[kd, kh, kw] for kd in range(3) for kh in range(3) for kw in range(3)], axis=0
    )
    gu_out = scatter_rows(9, grad_up * factor, cb, gsu, gru)

    e1_out.wait_recv()
    joined_out.wait_recv()
    g1_out = scatter_rows(10, weight_grad(et1r, jg, acc1), gfirst.shape[1], gs1, gr1)

    def finish(spread, into, out):
        spread.wait_recv()
        total = into[0]
        for s in range(1, nh):
            total = total + into[s]
        rows = out.shape[1]
        for t in range(taps):
            out[t] = total[:rows, t * no : (t + 1) * no]

    finish(g2_out, gr2, gsecond)
    cg_out.wait_recv()
    cgrad[...] = cgr[...]
    finish(gu_out, gru, gup)
    finish(g1_out, gr1, gfirst)

    for spread in (
        rows_out, planes_out, hid_out, joined_out, e2_out, e1_out, bu_out, g2_out, cg_out, gu_out, g1_out
    ):
        spread.wait_send()
    for wait in (skip_send, near_send, hid_send, e2_send, e1_send, bu_send):
        wait()


def per_device(nd, nh, bottom, skip, upconv_kernel, w_first, w_second, cotangent):
    cb, cw = bottom.shape[3], bottom.shape[2]
    cin, cu = upconv_kernel.shape[3:]
    fw = skip.shape[2]
    cj = w_first.shape[3]
    no = cu // nd
    rows = skip.shape[:2]
    factor = 1.0 / math.sqrt(rows[0] * nd * rows[1] * nh * fw)
    taps = round_up(27 * no, 128)
    ncj, nch = cj // nh, cu // nh
    v = pltpu.VMEM
    upw = upconv_kernel.reshape(27, cin, cu)
    w1 = w_first.reshape(27, cj, cu)
    w2 = w_second.reshape(27, cu, cu)
    cells = rows[0] * rows[1] * fw
    line = max(nd, nh)
    scratch = [
        v(upw.shape, BF16), v(w1.shape, BF16), v(w2.shape, BF16), v(cotangent.shape, BF16),
        v((nh, 3, cw, cb), BF16),
        v((nd, 3, cw, cin), BF16),
        v((4, 4, fw, cu), F32),
        v((4, 4, fw, cj), BF16),
        v((nd, cells, cj), BF16),
        v((cells, cu), F32),
        v((4, 4, fw, cu), BF16),
        v((nd, cells, cu), BF16),
        v((4, 4, fw, cu), BF16),
        v((4, 4, fw, cu), BF16),
        v((cu, 2 * cells), F32), v((nd, no, 2 * cells), F32),
        v((cu, 2 * cells), F32), v((nd, no, 2 * cells), F32),
        v((2, 2, fw, cu), F32),
        v((3, 3, 2, cw, cu), BF16),
        v((cu, cells), F32), v((nd, no, cells), F32),
        v((nh, cw, cb), BF16), v((nh, cw, cb), BF16),
        v((nd + 2, 9 * no, 128), F32), v((nd + 2, 9 * no, 128), F32),
        v((27 * no, cj), F32), v((27 * no, cu), F32),
        v((nh, round_up(nch, 8), taps), F32), v((nh, round_up(nch, 8), taps), F32),
        v((nh, round_up(ncj, 8), taps), F32), v((nh, round_up(ncj, 8), taps), F32),
        v((nh, round_up(cb, 8), taps), F32), v((nh, round_up(cb, 8), taps), F32),
        pltpu.SemaphoreType.DMA((11, line)), pltpu.SemaphoreType.DMA((11, line)),
        pltpu.SemaphoreType.DMA((6, 9)), pltpu.SemaphoreType.DMA((6, 9)),
        pltpu.SemaphoreType.DMA((6,)),
    ]
    outs = [
        jax.ShapeDtypeStruct(skip.shape, BF16),
        jax.ShapeDtypeStruct((nh, cw, cb), BF16),
        jax.ShapeDtypeStruct(skip.shape, BF16),
        jax.ShapeDtypeStruct((27, cb, no), F32),
        jax.ShapeDtypeStruct((27, ncj, no), F32),
        jax.ShapeDtypeStruct((27, nch, no), F32),
    ]
    result, cgrad, gskip, gup, gfirst, gsecond = pl.pallas_call(
        functools.partial(body, nd, nh, factor),
        out_shape=outs,
        in_specs=[pl.BlockSpec(memory_space=pl.ANY)] * 6,
        out_specs=[pl.BlockSpec(memory_space=pltpu.VMEM)] * 6,
        scratch_shapes=scratch,
        compiler_params=pltpu.CompilerParams(
            collective_id=0, has_side_effects=True, vmem_limit_bytes=56 * 1024 * 1024
        ),
        name="decoder",
    )(bottom, skip, upw, w1, w2, cotangent)
    return (
        result,
        cgrad[None],
        gskip,
        gup.reshape(3, 3, 3, cb, no),
        gfirst.reshape(3, 3, 3, ncj, no),
        gsecond.reshape(3, 3, 3, nch, no),
    )


def solution(mesh):
    return jax.shard_map(
        functools.partial(per_device, mesh.shape["depth"], mesh.shape["height"]),
        mesh=mesh,
        in_specs=(
            P("depth", None, None, "height"),
            P("depth", "height", None, None),
            P(),
            P(),
            P(),
            P("depth", "height", None, None),
        ),
        out_specs=(
            P("depth", "height", None, None),
            P("depth", None, None, "height"),
            P("depth", "height", None, None),
            P(None, None, None, "height", "depth"),
            P(None, None, None, "height", "depth"),
            P(None, None, None, "height", "depth"),
        ),
        check_vma=False,
    )
```

```python
import functools
import math

import jax
import jax.numpy as jnp
from jax import lax
from jax.experimental import pallas as pl
from jax.experimental.pallas import tpu as pltpu
from jax.sharding import PartitionSpec as P

MESH = pl.DeviceIdType.MESH
F32 = jnp.float32
BF16 = jnp.bfloat16
GRID9 = [(a, b) for a in range(3) for b in range(3)]
OTHERS = [(a, b) for a in (-1, 0, 1) for b in (-1, 0, 1) if (a, b) != (0, 0)]
NT = (((1,), (1,)), ((), ()))
PARITY_SHIFT = {0: (1, 1), 1: (0, 0), 2: (1, 0)}


def round_up(value, unit):
    return -(-value // unit) * unit


def remote(src, dst, send, recv, target):
    return pltpu.make_async_remote_copy(
        src_ref=src, dst_ref=dst, send_sem=send, recv_sem=recv, device_id=target, device_id_type=MESH
    )


class Spread:
    def __init__(self, log, me, count, target, source, slot, send, recv, steps=None):
        self.me, self.count, self.target = me, count, target
        self.source, self.slot, self.send, self.recv = source, slot, send, recv
        self.steps = steps or (1, count)
        self.arrived, self.log = False, log

    def each(self, act):
        def step(j, carry):
            act(j)
            return carry

        lax.fori_loop(*self.steps, step, 0)

    def outgoing(self, j):
        peer = lax.rem(self.me + j, self.count)
        return remote(
            self.source(peer), self.slot(self.me), self.send.at[peer], self.recv.at[self.me], self.target(peer)
        )

    def incoming(self, j):
        peer = lax.rem(self.me + self.count - j, self.count)
        return remote(
            self.source(peer), self.slot(peer), self.send.at[peer], self.recv.at[peer], self.target(peer)
        )

    def start(self):
        self.log.append(self)
        self.each(lambda j: self.outgoing(j).start())

    def wait_recv(self):
        self.arrived = True
        self.each(lambda j: self.incoming(j).wait_recv())

    def wait_send(self):
        self.each(lambda j: self.outgoing(j).wait_send())


class Halo:
    def __init__(self, log, there, copy, directions):
        self.there, self.copy, self.directions = there, copy, directions
        self.arrived, self.log = False, log

    def each(self, sign, act):
        for dd, dh in self.directions:
            @pl.when(self.there(sign * dd, sign * dh))
            def _(dd=dd, dh=dh):
                act(self.copy(dd, dh))

    def start(self):
        self.log.append(self)
        self.each(1, lambda copy: copy.start())

    def wait_recv(self):
        self.arrived = True
        self.each(-1, lambda copy: copy.wait_recv())

    def wait_send(self):
        self.each(1, lambda copy: copy.wait_send())


def shift_rows(value, by, period):
    rows = value.shape[0]
    row = lax.broadcasted_iota(jnp.int32, value.shape, 0) % period
    edge = 0 if by > 0 else period - 1
    return jnp.where(row == edge, 0.0, pltpu.roll(value, by % rows, 0))


def shift_lanes(value, by, period):
    lanes = value.shape[1]
    lane = lax.broadcasted_iota(jnp.int32, value.shape, 1) % period
    edge = 0 if by > 0 else period - 1
    return jnp.where(lane == edge, 0.0, pltpu.roll(value, by % lanes, 1))


def slope(values):
    sig = jax.nn.sigmoid(values)
    return sig * (1.0 + values * (1.0 - sig))


def dot(a, b, dims=(((1,), (0,)), ((), ()))):
    return lax.dot_general(a, b, dims, preferred_element_type=F32)


def body(
    nd, nh, factor,
    bottom, skip, upw_hbm, w1_hbm, w2_hbm, cot_hbm,
    result, gskip, cgrows, sumup, sumfirst, sumsecond,
    upw, w1, w2, cot, bott, bsend, brecv, near, bg, up32, joined, jg, fp, hid, hg, e2, e1, et2s, et2r, et1s, et1r,
    bu32, bu, buts, butr, cgs, cgr, acc1, acc2, px2, pr2, px1, pr1, pxu, pru, gs2, gr2, gs1, gr1, gsu, gru,
    ssem, rsem, hs, hr, loc,
):
    d = lax.axis_index("depth")
    h = lax.axis_index("height")
    pair, core = d // 2, lax.rem(d, 2)
    partner = d + 1 - 2 * core
    npair = nd // 2
    cb, rows_all, cw = bottom.shape
    cu = upw.shape[2]
    cin = upw.shape[1]
    no = cu // nd
    both = 2 * no

    weights = [
        pltpu.make_async_copy(upw_hbm, upw, loc.at[0]),
        pltpu.make_async_copy(w1_hbm, w1, loc.at[1]),
        pltpu.make_async_copy(w2_hbm, w2, loc.at[2]),
        pltpu.make_async_copy(cot_hbm, cot, loc.at[3]),
    ]
    own_skip = pltpu.make_async_copy(skip, joined.at[pl.ds(1, 2), pl.ds(1, 2), :, pl.ds(cu, cu)], loc.at[4])

    joined[...] = jnp.zeros_like(joined)
    hid[...] = jnp.zeros_like(hid)
    e2[...] = jnp.zeros_like(e2)
    e1[...] = jnp.zeros_like(e1)
    bu[...] = jnp.zeros_like(bu)

    own_skip.start()
    for copy in weights:
        copy.start()

    barrier = pltpu.get_barrier_semaphore()

    def greet_line(count, target):
        def step(j, carry):
            pl.semaphore_signal(barrier, inc=1, device_id=target(j), device_id_type=MESH)
            return carry

        lax.fori_loop(1, count, step, 0)

    greet_line(nh, lambda j: (d, lax.rem(h + j, nh)))
    greet_line(npair, lambda j: (2 * lax.rem(pair + j, npair) + core, h))

    def there(dd, dh):
        ok = None
        for pos, step, count in ((d, dd, nd), (h, dh, nh)):
            if step:
                cond = pos > 0 if step < 0 else pos < count - 1
                ok = cond if ok is None else jnp.logical_and(ok, cond)
        return ok

    for dd in (-1, 1):
        for dh in (-1, 0, 1):
            target = (lax.rem(d + dd + nd, nd), lax.rem(h + dh + nh, nh))
            pl.semaphore_signal(barrier, inc=1, device_id=target, device_id_type=MESH)

    bott[...] = bottom[...].astype(F32).reshape(cb * rows_all, cw)
    lines = [bott[pl.ds(r, cb, stride=rows_all), :] for r in range(rows_all)]
    blank = jnp.zeros((cb, cw), F32)
    rest = jnp.zeros((cb, 128 - 3 * cw), F32)
    pad = jnp.zeros((bsend.shape[1] - cb, 128), F32)
    for p in range(nh):
        before = lines[p - 1] if p > 0 else blank
        after = lines[p + 1] if p < nh - 1 else blank
        window = jnp.concatenate([before, lines[p], after, rest], axis=1)
        bsend[p] = jnp.concatenate([window, pad], axis=0).astype(BF16)
    brecv[h] = bsend[h]
    pl.semaphore_wait(barrier, nh + npair + 4)

    def src_part(step):
        return {0: pl.ds(1, 2), 1: pl.ds(2, 1), -1: pl.ds(1, 1)}[step]

    def own_part(step):
        return {0: pl.ds(0, 2), 1: pl.ds(1, 1), -1: pl.ds(0, 1)}[step]

    def dst_part(step):
        return {0: pl.ds(1, 2), 1: pl.ds(0, 1), -1: pl.ds(3, 1)}[step]

    log = []

    def halo(phase, copy_of, directions=OTHERS):
        def copy(dd, dh):
            slot = (dd + 1) * 3 + dh + 1
            src, dst = copy_of(dd, dh)
            return remote(src, dst, hs.at[phase, slot], hr.at[phase, slot], (d + dd, h + dh))

        return Halo(log, there, copy, directions)

    def field_halo(phase, field):
        return halo(
            phase,
            lambda dd, dh: (
                field.at[src_part(dd), src_part(dh)],
                field.at[dst_part(dd), dst_part(dh)],
            ),
        )

    def line_h(phase, source, slot):
        return Spread(log, h, nh, lambda p: (d, p), source, slot, ssem.at[phase], rsem.at[phase])

    def line_d(phase, source, slot, steps):
        return Spread(log, d, nd, lambda p: (p, h), source, slot, ssem.at[phase], rsem.at[phase], steps)

    def line_p(phase, source, slot):
        return Spread(
            log, pair, npair, lambda p: (2 * p + core, h), source, slot, ssem.at[phase], rsem.at[phase]
        )

    rows_out = line_h(0, lambda p: bsend.at[p], lambda s: brecv.at[s])
    rows_out.start()
    skip_halo = halo(
        0,
        lambda dd, dh: (
            skip.at[own_part(dd), own_part(dh)],
            joined.at[dst_part(dd), dst_part(dh), :, pl.ds(cu, cu)],
        ),
    )
    skip_halo.start()
    rows_out.wait_recv()
    stack = [brecv[c].astype(F32)[:cb] for c in range(nh)]
    wide = near.shape[3]
    if wide > cin:
        stack.append(jnp.zeros((wide - cin, 128), F32))
    near[1] = jnp.concatenate(stack, axis=0).T[: 3 * cw].reshape(3, cw, wide).astype(BF16)

    plane_next = line_d(1, lambda p: near.at[1], lambda s: near.at[0], (1, 2))
    plane_prev = line_d(2, lambda p: near.at[1], lambda s: near.at[2], (nd - 1, nd))
    plane_next.start()
    plane_prev.start()
    weights[0].wait()
    plane_next.wait_recv()
    plane_prev.wait_recv()

    coarse = []
    for s in range(3):
        plane = d - 1 + s
        here = jnp.logical_and(plane >= 0, plane < nd)
        value = near[s, :, :, 0:cin]
        coarse.append(jnp.where(here, value, jnp.zeros_like(value)))
    coarse = jnp.stack(coarse)
    bg[pair] = jnp.stack([near[1, 1:3], jnp.where(d < nd - 1, near[2, 1:3], jnp.zeros_like(near[2, 1:3]))])
    first_of = {0: 1, 1: 1, 2: 0}
    for gd in range(2):
        for gh in range(2):
            total = None
            for kd in ((1,), (0, 2))[gd]:
                for kh in ((1,), (0, 2))[gh]:
                    a, b = first_of[kd], first_of[kh]
                    lhs = coarse[a : a + 2, b : b + 2].reshape(4 * cw, -1)
                    t = kd * 9 + kh * 3
                    rhs = jnp.concatenate([upw[t], upw[t + 1], upw[t + 2]], axis=1)
                    part = dot(lhs, rhs)
                    total = part if total is None else total + part
            even = total[:, cu : 2 * cu]
            odd = total[:, 2 * cu :] + shift_rows(total[:, :cu], -1, cw)
            for i in range(2):
                for j in range(2):
                    at = (i * 2 + j) * cw
                    fd, fh = 2 * i + 1 - gd, 2 * j + 1 - gh
                    up32[fd, fh, pl.ds(0, cw, stride=2), :] = even[at : at + cw]
                    up32[fd, fh, pl.ds(1, cw, stride=2), :] = odd[at : at + cw]
    for fd in range(4):
        for fh in range(4):
            inside = None
            for pos, f, count in ((d, fd, nd), (h, fh, nh)):
                cond = None
                if f == 0:
                    cond = pos > 0
                if f == 3:
                    cond = pos < count - 1
                if cond is not None:
                    inside = cond if inside is None else jnp.logical_and(inside, cond)
            value = up32[fd, fh]
            if inside is not None:
                value = jnp.where(inside, value, 0.0)
            joined[fd, fh, :, 0:cu] = value.astype(BF16)

    own_skip.wait()
    skip_halo.wait_recv()
    weights[1].wait()
    cells = 4 * 2 * cw

    def conv(field, weight):
        chans = field.shape[3]
        lhs = jnp.concatenate(
            [field[a : a + 2, b : b + 2].reshape(cells, chans) for a, b in GRID9], axis=1
        )
        rhs = jnp.concatenate(
            [
                jnp.concatenate([weight[(a * 3 + b) * 3 + c] for c in range(3)], axis=1)
                for a, b in GRID9
            ],
            axis=0,
        )
        y = dot(lhs, rhs)
        n = weight.shape[2]
        return shift_rows(y[:, :n], 1, 2 * cw) + y[:, n : 2 * n] + shift_rows(y[:, 2 * n :], -1, 2 * cw)

    def conv_back(field, weight):
        chans = field.shape[3]
        lhs = jnp.concatenate(
            [field[2 - a : 4 - a, 2 - b : 4 - b].reshape(cells, chans) for a, b in GRID9], axis=1
        )
        rhs = jnp.concatenate(
            [
                jnp.concatenate([weight[(a * 3 + b) * 3 + c] for a, b in GRID9], axis=1)
                for c in range(3)
            ],
            axis=0,
        )
        y = dot(lhs, rhs, NT)
        n = weight.shape[1]
        return shift_rows(y[:, :n], -1, 2 * cw) + y[:, n : 2 * n] + shift_rows(y[:, 2 * n :], 1, 2 * cw)

    first_pre = conv(joined, w1)
    fp[...] = first_pre
    hidden = (first_pre * jax.nn.sigmoid(first_pre)).astype(BF16)
    hid[1:3, 1:3] = hidden.reshape(2, 2, 2 * cw, cu)
    hid_halo = field_halo(2, hid)
    hid_halo.start()
    hg[pair] = hidden
    jg[pair] = joined[1:3, 1:3].reshape(cells, 2 * cu)
    joined_out = line_p(4, lambda p: jg.at[pair], lambda s: jg.at[s])
    joined_out.start()

    weights[2].wait()
    weights[3].wait()
    hid_halo.wait_recv()
    second_pre = conv(hid, w2)
    result[...] = (second_pre * jax.nn.sigmoid(second_pre)).astype(BF16).reshape(2, 2, 2 * cw, cu)
    err2 = (cot[...].reshape(cells, cu).astype(F32) * slope(second_pre)).astype(BF16)
    e2[1:3, 1:3] = err2.reshape(2, 2, 2 * cw, cu)
    e2_halo = field_halo(3, e2)
    e2_halo.start()
    hid_out = line_p(3, lambda p: hg.at[pair], lambda s: hg.at[s])
    hid_out.start()

    e2_halo.wait_recv()
    err1 = (conv_back(e2, w2) * slope(fp[...])).astype(BF16)
    e1[1:3, 1:3] = err1.reshape(2, 2, 2 * cw, cu)
    e1_halo = field_halo(4, e1)
    e1_halo.start()

    def part_of(p):
        return pl.ds(pl.multiple_of(p * both, both), both)

    def flip(value, phase, out, into):
        out[...] = value.astype(F32).T.astype(BF16)
        into[pair] = out[part_of(pair)]
        spread = line_p(phase, lambda p: out.at[part_of(p)], lambda s: into.at[s])
        spread.start()
        return spread

    e2_out = flip(e2[...].reshape(4 * cells, cu), 5, et2s, et2r)
    planes_out = line_p(6, lambda p: bg.at[pair], lambda s: bg.at[s])
    planes_out.start()

    e1_halo.wait_recv()
    back = conv_back(e1, w1)
    bu32[...] = back[:, :cu].reshape(2, 2, 2 * cw, cu)
    for i in range(2):
        for j in range(2):
            for par in range(2):
                bu[1 + i, 1 + j, par] = bu32[i, j, pl.ds(par, cw, stride=2), :].astype(BF16)
    bu_halo = halo(
        5,
        lambda dd, dh: (
            bu.at[pl.ds(2, 1) if dd else pl.ds(1, 2), pl.ds(2, 1) if dh else pl.ds(1, 2)],
            bu.at[pl.ds(0, 1) if dd else pl.ds(1, 2), pl.ds(0, 1) if dh else pl.ds(1, 2)],
        ),
        [(1, 0), (0, 1), (1, 1)],
    )
    bu_halo.start()
    bu_out = flip(bu[1:3, 1:3].reshape(cells, cu), 7, buts, butr)
    e1_out = flip(e1[...].reshape(4 * cells, cu), 8, et1s, et1r)
    gskip[...] = back[:, cu:].astype(BF16).reshape(2, 2, 2 * cw, cu)

    def weight_grad(into, gathered, acc):
        acc[...] = jnp.zeros_like(acc)
        half = 2 * cw
        per_plane = 4 * half
        lane = lax.broadcasted_iota(jnp.int32, (both, 128), 1)

        def step(j, carry):
            shifted = []
            for plane in range(4):
                at = plane * per_plane
                low = into[j, :, at : at + 128].astype(F32)
                high = into[j, :, at + 128 : at + 256].astype(F32)
                mid = jnp.where(lane < half, pltpu.roll(low, half, 1), pltpu.roll(high, half, 1))
                shifted.append(
                    [
                        rows if kw == 1 else shift_lanes(rows, kw - 1, half)
                        for rows in (high, mid, low)
                        for kw in range(3)
                    ]
                )
            lhs = []
            for c in range(2):
                for kd in range(3):
                    for k in range(9):
                        pieces = [shifted[2 - kd + q][k][c * no : (c + 1) * no] for q in range(2)]
                        lhs.append(jnp.concatenate(pieces, axis=1))
            acc[...] += dot(jnp.concatenate(lhs, axis=0).astype(BF16), gathered[j])
            return carry

        lax.fori_loop(0, npair, step, 0)
        return acc[...]

    def swap(phase, value, out, into):
        half = 27 * no
        halves = [value[:half], value[half:]]
        mine = jnp.where(core == 0, halves[0], halves[1])
        out[...] = jnp.where(core == 0, halves[1], halves[0])
        copy = line_d(phase, lambda p: out, lambda s: into, (1, 2))
        copy.target = lambda p: (partner, h)
        copy.outgoing = copy.incoming = lambda j: remote(
            out, into, ssem.at[phase, 0], rsem.at[phase, 0], (partner, h)
        )
        copy.start()
        return copy, mine

    def flipped(value):
        rows, lanes = value.shape
        tall, wide = round_up(rows, 128), round_up(lanes, 128)
        if tall > rows:
            value = jnp.concatenate([value, jnp.zeros((tall - rows, lanes), F32)], axis=0)
        if wide > lanes:
            value = jnp.concatenate([value, jnp.zeros((tall, wide - lanes), F32)], axis=1)
        return value.T

    def scatter_rows(phase, swapped, arriving, chunk, out, into):
        copy, mine = swapped
        copy.wait_recv()
        turned = flipped((mine + arriving[...]) * factor)
        fill = out.shape[1] - chunk
        for c in range(nh):
            piece = turned[c * chunk : (c + 1) * chunk]
            if fill:
                piece = jnp.concatenate([piece, jnp.zeros((fill, piece.shape[1]), F32)], axis=0)
            out[c] = piece.astype(out.dtype)
        into[h] = out[h]
        spread = line_h(phase, lambda p: out.at[p], lambda s: into.at[s])
        spread.start()
        return spread

    e2_out.wait_recv()
    hid_out.wait_recv()
    swap2 = swap(9, weight_grad(et2r, hg, acc2), px2, pr2)

    bu_halo.wait_recv()
    around = lambda par: [bu[a, b, par].reshape(cw, cu) for a, b in GRID9]
    lhs = jnp.concatenate(around(0) + around(1), axis=1)
    rhs = jnp.concatenate(
        [upw[(a * 3 + b) * 3 + 1] for a, b in GRID9] + [upw[(a * 3 + b) * 3 + 2] for a, b in GRID9], axis=1
    )
    same = dot(lhs, rhs, NT)
    lhs = jnp.concatenate(around(1), axis=1)
    rhs = jnp.concatenate([upw[(a * 3 + b) * 3] for a, b in GRID9], axis=1)
    block_grad = flipped(same + shift_rows(dot(lhs, rhs, NT), 1, cw))
    for c in range(nh):
        cgs[c, 0:cb] = block_grad[c * cb : (c + 1) * cb]
    cgr[h] = cgs[h]
    cg_out = line_h(10, lambda p: cgs.at[p], lambda s: cgr.at[s])
    cg_out.start()
    g2_out = scatter_rows(11, swap2, pr2, cu // nh, gs2, gr2)

    bu_out.wait_recv()
    per = 128 // cw
    span = npair * cw
    group = min(per, npair)
    lane = lax.broadcasted_iota(jnp.int32, (both, 128), 1) // cw
    phases = {}
    for pd in range(2):
        for p in range(per):
            groups = []
            for g in range(npair // group):
                total = None
                for s in range(group):
                    piece = butr[g * group + s, :, pd * 128 : (pd + 1) * 128].astype(F32)
                    turn = ((s - p) * cw) % 128
                    piece = pltpu.roll(piece, turn, 1) if turn else piece
                    total = piece if total is None else jnp.where(lane == s, piece, total)
                groups.append(total)
            value = jnp.concatenate(groups, axis=1) if len(groups) > 1 else groups[0]
            phases[pd, p // 2, p % 2] = value[:, :span]

    def tap_rows(kd, kh, kw):
        pw, sw = PARITY_SHIFT[kw]
        value = phases[PARITY_SHIFT[kd][0], PARITY_SHIFT[kh][0], pw]
        return shift_lanes(value, 1, cw) if sw else value

    planes_out.wait_recv()
    products = {}
    for sd, kds in ((0, (1, 2)), (1, (0,))):
        for sh, khs in ((0, (1, 2)), (1, (0,))):
            order = [(kd, kh, kw) for kd in kds for kh in khs for kw in range(3)]
            lhs = jnp.concatenate([tap_rows(*k) for k in order], axis=0).astype(BF16)
            rhs = bg[:, sd, sh].reshape(span, -1)
            value = dot(lhs, rhs)
            for i, k in enumerate(order):
                for c in range(2):
                    at = (i * 2 + c) * no
                    products[(c,) + k] = value[at : at + no]
    grad_up = jnp.concatenate(
        [products[c, a, b, e] for c in range(2) for a, b in GRID9 for e in range(3)], axis=0
    )
    swapu = swap(12, grad_up, pxu, pru)

    e1_out.wait_recv()
    joined_out.wait_recv()
    swap1 = swap(13, weight_grad(et1r, jg, acc1), px1, pr1)
    gu_out = scatter_rows(14, swapu, pru, cb, gsu, gru)
    g1_out = scatter_rows(15, swap1, pr1, 2 * cu // nh, gs1, gr1)

    def finish(spread, into, out):
        spread.wait_recv()
        total = into[0].astype(F32)
        for s in range(1, nh):
            total = total + into[s].astype(F32)
        out[...] = total[: out.shape[0]]

    finish(g2_out, gr2, sumsecond)
    cg_out.wait_recv()
    cgrows[...] = cgr[...]
    finish(gu_out, gru, sumup)
    finish(g1_out, gr1, sumfirst)

    for part in log:
        if not part.arrived:
            part.wait_recv()
        part.wait_send()


def closing(nh, result, gskip, cgrows, sumup, sumfirst, sumsecond, out0, out1, out2, out3, out4, out5, sems):
    whole = [pltpu.make_async_copy(result, out0, sems.at[0]), pltpu.make_async_copy(gskip, out2, sems.at[1])]
    for copy in whole:
        copy.start()
    cb = out1.shape[0]
    tall = cgrows.shape[0] // nh
    for c in range(cb):
        out1[c] = cgrows[pl.ds(c, nh, stride=tall), 0 : out1.shape[2]].astype(BF16)
    no = out3.shape[1]
    for total, out in ((sumup, out3), (sumfirst, out4)):
        n = out.shape[2]
        turned = total[...]
        if turned.shape[0] < 128:
            fill = jnp.zeros((128 - turned.shape[0], turned.shape[1]), F32)
            turned = jnp.concatenate([turned, fill], axis=0)
        out[...] = turned.T[: 27 * no, :n].reshape(27, no, n)
    total = sumsecond[...]
    for t in range(27):
        out5[t] = total[: out5.shape[1], t * no : (t + 1) * no]
    for copy in whole:
        copy.wait()


def per_device(nd, nh, bottom, skip, upconv_kernel, w_first, w_second, cotangent):
    cb, cw = bottom.shape[3], bottom.shape[2]
    cin, cu = upconv_kernel.shape[3:]
    fw = skip.shape[2]
    cj = w_first.shape[3]
    no = cu // nd
    both, npair = 2 * no, nd // 2
    rows = skip.shape[:2]
    factor = 1.0 / math.sqrt(rows[0] * nd * rows[1] * nh * fw)
    taps = round_up(27 * no, 128)
    ncj, nch = cj // nh, cu // nh
    v = pltpu.VMEM
    upw = upconv_kernel.reshape(27, cin, cu)
    w1 = w_first.reshape(27, cj, cu)
    w2 = w_second.reshape(27, cu, cu)
    cells = rows[0] * rows[1] * fw
    line = max(nd, nh)
    wide = round_up(cin, 128)
    part = 27 * no
    scratch = [
        v(upw.shape, BF16), v(w1.shape, BF16), v(w2.shape, BF16), v(cotangent.shape, BF16),
        v((cb * nh, cw), F32),
        v((nh, round_up(cb, 16), 128), BF16), v((nh, round_up(cb, 16), 128), BF16),
        v((3, 3, cw, wide), BF16),
        v((npair, 2, 2, cw, wide), BF16),
        v((4, 4, fw, cu), F32),
        v((4, 4, fw, cj), BF16),
        v((npair, cells, cj), BF16),
        v((cells, cu), F32),
        v((4, 4, fw, cu), BF16),
        v((npair, cells, cu), BF16),
        v((4, 4, fw, cu), BF16),
        v((4, 4, fw, cu), BF16),
        v((cu, 4 * cells), BF16), v((npair, both, 4 * cells), BF16),
        v((cu, 4 * cells), BF16), v((npair, both, 4 * cells), BF16),
        v((2, 2, fw, cu), F32),
        v((3, 3, 2, cw, cu), BF16),
        v((cu, cells), BF16), v((npair, both, cells), BF16),
        v((nh, round_up(cb, 8), 128), F32), v((nh, round_up(cb, 8), 128), F32),
        v((2 * part, cj), F32), v((2 * part, cu), F32),
        v((part, cu), F32), v((part, cu), F32),
        v((part, cj), F32), v((part, cj), F32),
        v((part, wide), F32), v((part, wide), F32),
        v((nh, round_up(nch, 8), taps), F32), v((nh, round_up(nch, 8), taps), F32),
        v((nh, round_up(ncj, 16), taps), BF16), v((nh, round_up(ncj, 16), taps), BF16),
        v((nh, round_up(cb, 16), taps), BF16), v((nh, round_up(cb, 16), taps), BF16),
        pltpu.SemaphoreType.DMA((16, line)), pltpu.SemaphoreType.DMA((16, line)),
        pltpu.SemaphoreType.DMA((6, 9)), pltpu.SemaphoreType.DMA((6, 9)),
        pltpu.SemaphoreType.DMA((6,)),
    ]
    tall = round_up(cb, 8)
    shape = jax.ShapeDtypeStruct
    left = pl.pallas_call(
        functools.partial(body, nd, nh, factor),
        out_shape=[
            shape(skip.shape, BF16),
            shape(skip.shape, BF16),
            shape((nh, tall, 128), F32),
            shape((tall, taps), F32),
            shape((round_up(ncj, 8), taps), F32),
            shape((round_up(nch, 8), taps), F32),
        ],
        in_specs=[pl.BlockSpec(memory_space=pltpu.VMEM)] + [pl.BlockSpec(memory_space=pl.ANY)] * 5,
        out_specs=[pl.BlockSpec(memory_space=pltpu.VMEM)] * 6,
        scratch_shapes=scratch,
        compiler_params=pltpu.CompilerParams(
            collective_id=0, has_side_effects=True, vmem_limit_bytes=56 * 1024 * 1024
        ),
        name="decoder",
    )(bottom[0].transpose(2, 0, 1), skip, upw, w1, w2, cotangent)
    result, gskip, cgrows, sumup, sumfirst, sumsecond = left
    anywhere = pl.BlockSpec(memory_space=pl.ANY)
    inside = pl.BlockSpec(memory_space=pltpu.VMEM)
    outs = pl.pallas_call(
        functools.partial(closing, nh),
        out_shape=[
            shape(skip.shape, BF16),
            shape((cb, nh, cw), BF16),
            shape(skip.shape, BF16),
            shape((27, no, cb), F32),
            shape((27, no, ncj), F32),
            shape((27, nch, no), F32),
        ],
        in_specs=[anywhere] * 2 + [inside] * 4,
        out_specs=[anywhere, inside, anywhere, inside, inside, inside],
        scratch_shapes=[pltpu.SemaphoreType.DMA((2,))],
        name="closing",
    )(result, gskip, cgrows.reshape(nh * tall, 128), sumup, sumfirst, sumsecond)
    return (
        outs[0],
        outs[1].transpose(1, 2, 0)[None],
        outs[2],
        outs[3].reshape(3, 3, 3, no, cb).transpose(0, 1, 2, 4, 3),
        outs[4].reshape(3, 3, 3, no, ncj).transpose(0, 1, 2, 4, 3),
        outs[5].reshape(3, 3, 3, nch, no),
    )


def solution(mesh):
    return jax.shard_map(
        functools.partial(per_device, mesh.shape["depth"], mesh.shape["height"]),
        mesh=mesh,
        in_specs=(
            P("depth", None, None, "height"),
            P("depth", "height", None, None),
            P(),
            P(),
            P(),
            P("depth", "height", None, None),
        ),
        out_specs=(
            P("depth", "height", None, None),
            P("depth", None, None, "height"),
            P("depth", "height", None, None),
            P(None, None, None, "height", "depth"),
            P(None, None, None, "height", "depth"),
            P(None, None, None, "height", "depth"),
        ),
        check_vma=False,
    )
```

```python
import functools
import math

import jax
import jax.numpy as jnp
from jax import lax
from jax.experimental import pallas as pl
from jax.experimental.pallas import tpu as pltpu
from jax.sharding import PartitionSpec as P

MESH = pl.DeviceIdType.MESH
F32 = jnp.float32
BF16 = jnp.bfloat16
GRID9 = [(a, b) for a in range(3) for b in range(3)]
OTHERS = [(a, b) for a in (-1, 0, 1) for b in (-1, 0, 1) if (a, b) != (0, 0)]
NT = (((1,), (1,)), ((), ()))
PARITY_SHIFT = {0: (1, 1), 1: (0, 0), 2: (1, 0)}


def round_up(value, unit):
    return -(-value // unit) * unit


def remote(src, dst, send, recv, target):
    return pltpu.make_async_remote_copy(
        src_ref=src, dst_ref=dst, send_sem=send, recv_sem=recv, device_id=target, device_id_type=MESH
    )


class Spread:
    def __init__(self, log, me, count, target, source, slot, send, recv, steps=None):
        self.me, self.count, self.target = me, count, target
        self.source, self.slot, self.send, self.recv = source, slot, send, recv
        self.steps = steps or (1, count)
        self.arrived, self.log = False, log

    def each(self, act):
        def step(j, carry):
            act(j)
            return carry

        lax.fori_loop(*self.steps, step, 0)

    def outgoing(self, j):
        peer = lax.rem(self.me + j, self.count)
        return remote(
            self.source(peer), self.slot(self.me), self.send.at[peer], self.recv.at[self.me], self.target(peer)
        )

    def incoming(self, j):
        peer = lax.rem(self.me + self.count - j, self.count)
        return remote(
            self.source(peer), self.slot(peer), self.send.at[peer], self.recv.at[peer], self.target(peer)
        )

    def start(self):
        self.log.append(self)
        self.each(lambda j: self.outgoing(j).start())

    def wait_recv(self):
        self.arrived = True
        self.each(lambda j: self.incoming(j).wait_recv())

    def wait_send(self):
        self.each(lambda j: self.outgoing(j).wait_send())


class Halo:
    def __init__(self, log, there, copy, directions):
        self.there, self.copy, self.directions = there, copy, directions
        self.arrived, self.log = False, log

    def each(self, sign, act):
        for dd, dh in self.directions:
            @pl.when(self.there(sign * dd, sign * dh))
            def _(dd=dd, dh=dh):
                act(self.copy(dd, dh))

    def start(self):
        self.log.append(self)
        self.each(1, lambda copy: copy.start())

    def wait_recv(self):
        self.arrived = True
        self.each(-1, lambda copy: copy.wait_recv())

    def wait_send(self):
        self.each(1, lambda copy: copy.wait_send())


def shift_rows(value, by, period):
    rows = value.shape[0]
    row = lax.broadcasted_iota(jnp.int32, value.shape, 0) % period
    edge = 0 if by > 0 else period - 1
    return jnp.where(row == edge, 0.0, pltpu.roll(value, by % rows, 0))


def shift_lanes(value, by, period):
    lanes = value.shape[1]
    lane = lax.broadcasted_iota(jnp.int32, value.shape, 1) % period
    edge = 0 if by > 0 else period - 1
    return jnp.where(lane == edge, 0.0, pltpu.roll(value, by % lanes, 1))


def slope(values):
    sig = jax.nn.sigmoid(values)
    return sig * (1.0 + values * (1.0 - sig))


def dot(a, b, dims=(((1,), (0,)), ((), ()))):
    return lax.dot_general(a, b, dims, preferred_element_type=F32)


def body(
    nd, nh, factor,
    bottom_hbm, skip, upw_hbm, w1_hbm, w2_hbm, cot_hbm,
    result_hbm, gskip_hbm, cgrows, sumup_hbm, sumfirst_hbm, sumsecond_hbm,
    bottom, result, gskip, sumup, sumfirst, sumsecond, upw, w1, w2, cot, bott, bsend, brecv, near, bg, up32, joined, ug, sg, fp, hid, hg, e2, e1, et2s, et2r, et1s, et1r,
    bu32, bu, buts, butr, cgs, cgr, acc1, acc2, px2, pr2, px1, pr1, pxu, pru, gs2, gr2, gs1, gr1, gsu, gru,
    ssem, rsem, hs, hr, loc,
):
    d = lax.axis_index("depth")
    h = lax.axis_index("height")
    pair, core = d // 2, lax.rem(d, 2)
    partner = d + 1 - 2 * core
    npair = nd // 2
    cb, rows_all, cw = bottom.shape
    cu = upw.shape[2]
    cin = upw.shape[1]
    no = cu // nd
    both = 2 * no

    weights = [
        pltpu.make_async_copy(upw_hbm, upw, loc.at[0]),
        pltpu.make_async_copy(w1_hbm, w1, loc.at[1]),
        pltpu.make_async_copy(w2_hbm, w2, loc.at[2]),
        pltpu.make_async_copy(cot_hbm, cot, loc.at[3]),
    ]
    own_skip = pltpu.make_async_copy(skip, joined.at[pl.ds(1, 2), pl.ds(1, 2), :, pl.ds(cu, cu)], loc.at[4])
    own_gathered = pltpu.make_async_copy(skip, sg.at[pair], loc.at[6])

    own_bottom = pltpu.make_async_copy(bottom_hbm, bottom, loc.at[5])
    own_bottom.start()
    for copy in weights:
        copy.start()
    joined[...] = jnp.zeros_like(joined)
    own_skip.start()
    own_gathered.start()
    hid[...] = jnp.zeros_like(hid)
    e2[...] = jnp.zeros_like(e2)
    e1[...] = jnp.zeros_like(e1)
    bu[...] = jnp.zeros_like(bu)


    barrier = pltpu.get_barrier_semaphore()

    def greet_line(count, target):
        def step(j, carry):
            pl.semaphore_signal(barrier, inc=1, device_id=target(j), device_id_type=MESH)
            return carry

        lax.fori_loop(1, count, step, 0)

    greet_line(nh, lambda j: (d, lax.rem(h + j, nh)))
    greet_line(npair, lambda j: (2 * lax.rem(pair + j, npair) + core, h))

    def there(dd, dh):
        ok = None
        for pos, step, count in ((d, dd, nd), (h, dh, nh)):
            if step:
                cond = pos > 0 if step < 0 else pos < count - 1
                ok = cond if ok is None else jnp.logical_and(ok, cond)
        return ok

    for dd in (-1, 1):
        for dh in (-1, 0, 1):
            target = (lax.rem(d + dd + nd, nd), lax.rem(h + dh + nh, nh))
            pl.semaphore_signal(barrier, inc=1, device_id=target, device_id_type=MESH)

    own_bottom.wait()
    bott[...] = bottom[...].astype(F32).reshape(cb * rows_all, cw)
    lines = [bott[pl.ds(r, cb, stride=rows_all), :] for r in range(rows_all)]
    blank = jnp.zeros((cb, cw), F32)
    rest = jnp.zeros((cb, 128 - 3 * cw), F32)
    pad = jnp.zeros((bsend.shape[1] - cb, 128), F32)
    for p in range(nh):
        before = lines[p - 1] if p > 0 else blank
        after = lines[p + 1] if p < nh - 1 else blank
        window = jnp.concatenate([before, lines[p], after, rest], axis=1)
        bsend[p] = jnp.concatenate([window, pad], axis=0).astype(BF16)
    brecv[h] = bsend[h]
    pl.semaphore_wait(barrier, nh + npair + 4)

    def src_part(step):
        return {0: pl.ds(1, 2), 1: pl.ds(2, 1), -1: pl.ds(1, 1)}[step]

    def own_part(step):
        return {0: pl.ds(0, 2), 1: pl.ds(1, 1), -1: pl.ds(0, 1)}[step]

    def dst_part(step):
        return {0: pl.ds(1, 2), 1: pl.ds(0, 1), -1: pl.ds(3, 1)}[step]

    log = []

    def halo(phase, copy_of, directions=OTHERS):
        def copy(dd, dh):
            slot = (dd + 1) * 3 + dh + 1
            src, dst = copy_of(dd, dh)
            return remote(src, dst, hs.at[phase, slot], hr.at[phase, slot], (d + dd, h + dh))

        return Halo(log, there, copy, directions)

    def field_halo(phase, field):
        return halo(
            phase,
            lambda dd, dh: (
                field.at[src_part(dd), src_part(dh)],
                field.at[dst_part(dd), dst_part(dh)],
            ),
        )

    def line_h(phase, source, slot):
        return Spread(log, h, nh, lambda p: (d, p), source, slot, ssem.at[phase], rsem.at[phase])

    def line_d(phase, source, slot, steps):
        return Spread(log, d, nd, lambda p: (p, h), source, slot, ssem.at[phase], rsem.at[phase], steps)

    def line_p(phase, source, slot):
        return Spread(
            log, pair, npair, lambda p: (2 * p + core, h), source, slot, ssem.at[phase], rsem.at[phase]
        )

    rows_out = line_h(0, lambda p: bsend.at[p], lambda s: brecv.at[s])
    rows_out.start()
    skip_halo = halo(
        0,
        lambda dd, dh: (
            skip.at[own_part(dd), own_part(dh)],
            joined.at[dst_part(dd), dst_part(dh), :, pl.ds(cu, cu)],
        ),
    )
    skip_halo.start()
    skip_out = line_p(17, lambda p: skip, lambda s: sg.at[s])
    skip_out.start()
    rows_out.wait_recv()
    stack = [brecv[c].astype(F32)[:cb] for c in range(nh)]
    wide = near.shape[3]
    if wide > cin:
        stack.append(jnp.zeros((wide - cin, 128), F32))
    near[1] = jnp.concatenate(stack, axis=0).T[: 3 * cw].reshape(3, cw, wide).astype(BF16)

    plane_next = line_d(1, lambda p: near.at[1], lambda s: near.at[0], (1, 2))
    plane_prev = line_d(2, lambda p: near.at[1], lambda s: near.at[2], (nd - 1, nd))
    plane_next.start()
    plane_prev.start()
    weights[0].wait()
    plane_next.wait_recv()
    plane_prev.wait_recv()

    coarse = []
    for s in range(3):
        plane = d - 1 + s
        here = jnp.logical_and(plane >= 0, plane < nd)
        value = near[s, :, :, 0:cin]
        coarse.append(jnp.where(here, value, jnp.zeros_like(value)))
    coarse = jnp.stack(coarse)
    bg[pair] = jnp.stack([near[1, 1:3], jnp.where(d < nd - 1, near[2, 1:3], jnp.zeros_like(near[2, 1:3]))])
    first_of = {0: 1, 1: 1, 2: 0}
    for gd in range(2):
        for gh in range(2):
            total = None
            for kd in ((1,), (0, 2))[gd]:
                for kh in ((1,), (0, 2))[gh]:
                    a, b = first_of[kd], first_of[kh]
                    lhs = coarse[a : a + 2, b : b + 2].reshape(4 * cw, -1)
                    t = kd * 9 + kh * 3
                    rhs = jnp.concatenate([upw[t], upw[t + 1], upw[t + 2]], axis=1)
                    part = dot(lhs, rhs)
                    total = part if total is None else total + part
            even = total[:, cu : 2 * cu]
            odd = total[:, 2 * cu :] + shift_rows(total[:, :cu], -1, cw)
            for i in range(2):
                for j in range(2):
                    at = (i * 2 + j) * cw
                    fd, fh = 2 * i + 1 - gd, 2 * j + 1 - gh
                    up32[fd, fh, pl.ds(0, cw, stride=2), :] = even[at : at + cw]
                    up32[fd, fh, pl.ds(1, cw, stride=2), :] = odd[at : at + cw]
    for fd in range(4):
        for fh in range(4):
            inside = None
            for pos, f, count in ((d, fd, nd), (h, fh, nh)):
                cond = None
                if f == 0:
                    cond = pos > 0
                if f == 3:
                    cond = pos < count - 1
                if cond is not None:
                    inside = cond if inside is None else jnp.logical_and(inside, cond)
            value = up32[fd, fh]
            if inside is not None:
                value = jnp.where(inside, value, 0.0)
            joined[fd, fh, :, 0:cu] = value.astype(BF16)

    own_skip.wait()
    skip_halo.wait_recv()
    weights[1].wait()
    cells = 4 * 2 * cw

    def conv(field, weight):
        chans = field.shape[3]
        lhs = jnp.concatenate(
            [field[a : a + 2, b : b + 2].reshape(cells, chans) for a, b in GRID9], axis=1
        )
        rhs = jnp.concatenate(
            [
                jnp.concatenate([weight[(a * 3 + b) * 3 + c] for c in range(3)], axis=1)
                for a, b in GRID9
            ],
            axis=0,
        )
        y = dot(lhs, rhs)
        n = weight.shape[2]
        return shift_rows(y[:, :n], 1, 2 * cw) + y[:, n : 2 * n] + shift_rows(y[:, 2 * n :], -1, 2 * cw)

    def conv_back(field, weight):
        chans = field.shape[3]
        lhs = jnp.concatenate(
            [field[2 - a : 4 - a, 2 - b : 4 - b].reshape(cells, chans) for a, b in GRID9], axis=1
        )
        rhs = jnp.concatenate(
            [
                jnp.concatenate([weight[(a * 3 + b) * 3 + c] for a, b in GRID9], axis=1)
                for c in range(3)
            ],
            axis=0,
        )
        y = dot(lhs, rhs, NT)
        n = weight.shape[1]
        return shift_rows(y[:, :n], -1, 2 * cw) + y[:, n : 2 * n] + shift_rows(y[:, 2 * n :], 1, 2 * cw)

    first_pre = conv(joined, w1)
    fp[...] = first_pre
    hidden = (first_pre * jax.nn.sigmoid(first_pre)).astype(BF16)
    hid[1:3, 1:3] = hidden.reshape(2, 2, 2 * cw, cu)
    hid_halo = field_halo(2, hid)
    hid_halo.start()
    hg[pair] = hidden
    ug[pair] = joined[1:3, 1:3, :, 0:cu].reshape(cells, cu)
    up_out = line_p(4, lambda p: ug.at[pair], lambda s: ug.at[s])
    up_out.start()

    weights[2].wait()
    weights[3].wait()
    hid_halo.wait_recv()
    second_pre = conv(hid, w2)
    result[...] = (second_pre * jax.nn.sigmoid(second_pre)).astype(BF16).reshape(2, 2, 2 * cw, cu)
    err2 = (cot[...].reshape(cells, cu).astype(F32) * slope(second_pre)).astype(BF16)
    e2[1:3, 1:3] = err2.reshape(2, 2, 2 * cw, cu)
    out_result = pltpu.make_async_copy(result, result_hbm, loc.at[7])
    out_result.start()
    e2_halo = field_halo(3, e2)
    e2_halo.start()
    hid_out = line_p(3, lambda p: hg.at[pair], lambda s: hg.at[s])
    hid_out.start()

    e2_halo.wait_recv()
    err1 = (conv_back(e2, w2) * slope(fp[...])).astype(BF16)
    e1[1:3, 1:3] = err1.reshape(2, 2, 2 * cw, cu)
    e1_halo = field_halo(4, e1)
    e1_halo.start()

    def part_of(p):
        return pl.ds(pl.multiple_of(p * both, both), both)

    def flip(value, phase, out, into):
        out[...] = value.astype(F32).T.astype(BF16)
        into[pair] = out[part_of(pair)]
        spread = line_p(phase, lambda p: out.at[part_of(p)], lambda s: into.at[s])
        spread.start()
        return spread

    e2_out = flip(e2[...].reshape(4 * cells, cu), 5, et2s, et2r)
    planes_out = line_p(6, lambda p: bg.at[pair], lambda s: bg.at[s])
    planes_out.start()

    e1_halo.wait_recv()
    back = conv_back(e1, w1)
    bu32[...] = back[:, :cu].reshape(2, 2, 2 * cw, cu)
    for i in range(2):
        for j in range(2):
            for par in range(2):
                bu[1 + i, 1 + j, par] = bu32[i, j, pl.ds(par, cw, stride=2), :].astype(BF16)
    bu_halo = halo(
        5,
        lambda dd, dh: (
            bu.at[pl.ds(2, 1) if dd else pl.ds(1, 2), pl.ds(2, 1) if dh else pl.ds(1, 2)],
            bu.at[pl.ds(0, 1) if dd else pl.ds(1, 2), pl.ds(0, 1) if dh else pl.ds(1, 2)],
        ),
        [(1, 0), (0, 1), (1, 1)],
    )
    bu_halo.start()
    bu_out = flip(bu[1:3, 1:3].reshape(cells, cu), 7, buts, butr)
    e1_out = flip(e1[...].reshape(4 * cells, cu), 8, et1s, et1r)
    gskip[...] = back[:, cu:].astype(BF16).reshape(2, 2, 2 * cw, cu)
    out_gskip = pltpu.make_async_copy(gskip, gskip_hbm, loc.at[8])
    out_gskip.start()

    def weight_grad(into, gathered, acc):
        acc[...] = jnp.zeros_like(acc)
        half = 2 * cw
        per_plane = 4 * half
        lane = lax.broadcasted_iota(jnp.int32, (both, 128), 1)

        def step(j, carry):
            shifted = []
            for plane in range(4):
                at = plane * per_plane
                low = into[j, :, at : at + 128].astype(F32)
                high = into[j, :, at + 128 : at + 256].astype(F32)
                mid = jnp.where(lane < half, pltpu.roll(low, half, 1), pltpu.roll(high, half, 1))
                shifted.append(
                    [
                        rows if kw == 1 else shift_lanes(rows, kw - 1, half)
                        for rows in (high, mid, low)
                        for kw in range(3)
                    ]
                )
            lhs = []
            for c in range(2):
                for kd in range(3):
                    for k in range(9):
                        pieces = [shifted[2 - kd + q][k][c * no : (c + 1) * no] for q in range(2)]
                        lhs.append(jnp.concatenate(pieces, axis=1))
            acc[...] += dot(jnp.concatenate(lhs, axis=0).astype(BF16), gathered(j))
            return carry

        lax.fori_loop(0, npair, step, 0)
        return acc[...]

    def swap(phase, value, out, into):
        half = 27 * no
        halves = [value[:half], value[half:]]
        mine = jnp.where(core == 0, halves[0], halves[1])
        out[...] = jnp.where(core == 0, halves[1], halves[0])
        copy = line_d(phase, lambda p: out, lambda s: into, (1, 2))
        copy.target = lambda p: (partner, h)
        copy.outgoing = copy.incoming = lambda j: remote(
            out, into, ssem.at[phase, 0], rsem.at[phase, 0], (partner, h)
        )
        copy.start()
        return copy, mine

    def flipped(value):
        rows, lanes = value.shape
        tall, wide = round_up(rows, 128), round_up(lanes, 128)
        if tall > rows:
            value = jnp.concatenate([value, jnp.zeros((tall - rows, lanes), F32)], axis=0)
        if wide > lanes:
            value = jnp.concatenate([value, jnp.zeros((tall, wide - lanes), F32)], axis=1)
        return value.T

    def scatter_rows(phase, swapped, arriving, chunk, out, into):
        copy, mine = swapped
        copy.wait_recv()
        turned = flipped((mine + arriving[...]) * factor)
        fill = out.shape[1] - chunk
        for c in range(nh):
            piece = turned[c * chunk : (c + 1) * chunk]
            if fill:
                piece = jnp.concatenate([piece, jnp.zeros((fill, piece.shape[1]), F32)], axis=0)
            out[c] = piece.astype(out.dtype)
        into[h] = out[h]
        spread = line_h(phase, lambda p: out.at[p], lambda s: into.at[s])
        spread.start()
        return spread

    e2_out.wait_recv()
    hid_out.wait_recv()
    swap2 = swap(9, weight_grad(et2r, lambda j: hg[j], acc2), px2, pr2)

    bu_halo.wait_recv()
    around = lambda par: [bu[a, b, par].reshape(cw, cu) for a, b in GRID9]
    lhs = jnp.concatenate(around(0) + around(1), axis=1)
    rhs = jnp.concatenate(
        [upw[(a * 3 + b) * 3 + 1] for a, b in GRID9] + [upw[(a * 3 + b) * 3 + 2] for a, b in GRID9], axis=1
    )
    same = dot(lhs, rhs, NT)
    lhs = jnp.concatenate(around(1), axis=1)
    rhs = jnp.concatenate([upw[(a * 3 + b) * 3] for a, b in GRID9], axis=1)
    block_grad = flipped(same + shift_rows(dot(lhs, rhs, NT), 1, cw))
    share = cb // (128 // cw)
    for c in range(nh):
        groups = [block_grad[c * cb + q : c * cb + q + share, :cw] for q in range(0, cb, share)]
        cgs[c, 0:share] = jnp.concatenate(groups, axis=1)
    cgr[h] = cgs[h]
    cg_out = line_h(10, lambda p: cgs.at[p], lambda s: cgr.at[s])
    cg_out.start()
    g2_out = scatter_rows(11, swap2, pr2, cu // nh, gs2, gr2)

    bu_out.wait_recv()
    per = 128 // cw
    span = npair * cw
    group = min(per, npair)
    lane = lax.broadcasted_iota(jnp.int32, (both, 128), 1) // cw
    phases = {}
    for pd in range(2):
        for p in range(per):
            groups = []
            for g in range(npair // group):
                total = None
                for s in range(group):
                    piece = butr[g * group + s, :, pd * 128 : (pd + 1) * 128].astype(F32)
                    turn = ((s - p) * cw) % 128
                    piece = pltpu.roll(piece, turn, 1) if turn else piece
                    total = piece if total is None else jnp.where(lane == s, piece, total)
                groups.append(total)
            value = jnp.concatenate(groups, axis=1) if len(groups) > 1 else groups[0]
            phases[pd, p // 2, p % 2] = value[:, :span]

    def tap_rows(kd, kh, kw):
        pw, sw = PARITY_SHIFT[kw]
        value = phases[PARITY_SHIFT[kd][0], PARITY_SHIFT[kh][0], pw]
        return shift_lanes(value, 1, cw) if sw else value

    planes_out.wait_recv()
    products = {}
    for sd, kds in ((0, (1, 2)), (1, (0,))):
        for sh, khs in ((0, (1, 2)), (1, (0,))):
            order = [(kd, kh, kw) for kd in kds for kh in khs for kw in range(3)]
            lhs = jnp.concatenate([tap_rows(*k) for k in order], axis=0).astype(BF16)
            rhs = bg[:, sd, sh].reshape(span, -1)
            value = dot(lhs, rhs)
            for i, k in enumerate(order):
                for c in range(2):
                    at = (i * 2 + c) * no
                    products[(c,) + k] = value[at : at + no]
    grad_up = jnp.concatenate(
        [products[c, a, b, e] for c in range(2) for a, b in GRID9 for e in range(3)], axis=0
    )
    swapu = swap(12, grad_up, pxu, pru)

    e1_out.wait_recv()
    up_out.wait_recv()
    skip_out.wait_recv()
    own_gathered.wait()
    swap1 = swap(13, weight_grad(et1r, lambda j: jnp.concatenate([ug[j], sg[j].reshape(cells, cu)], axis=1), acc1), px1, pr1)
    gu_out = scatter_rows(14, swapu, pru, cb, gsu, gru)
    g1_out = scatter_rows(15, swap1, pr1, 2 * cu // nh, gs1, gr1)

    def finish(spread, into, out, hbm, at):
        spread.wait_recv()
        total = into[0].astype(F32)
        for s in range(1, nh):
            total = total + into[s].astype(F32)
        out[...] = total[: out.shape[0]]
        copy = pltpu.make_async_copy(out, hbm, loc.at[at])
        copy.start()
        return copy

    finished = [finish(g2_out, gr2, sumsecond, sumsecond_hbm, 9)]
    cg_out.wait_recv()
    out_cg = pltpu.make_async_copy(cgr, cgrows, loc.at[10])
    out_cg.start()
    finished.append(finish(gu_out, gru, sumup, sumup_hbm, 11))
    finished.append(finish(g1_out, gr1, sumfirst, sumfirst_hbm, 12))
    for copy in finished + [out_cg, out_result, out_gskip]:
        copy.wait()

    for part in log:
        if not part.arrived:
            part.wait_recv()
        part.wait_send()


def closing(nh, *refs):
    (result, gskip, *left), (out0, out1h, out2, *grads), (cgrows, sumup, sumfirst, sumsecond) = (
        refs[:6], refs[6:12], refs[12:16]
    )
    out1, out3, out4, out5, sems = refs[16:]
    stages = (cgrows, sumup, sumfirst, sumsecond)
    into = [pltpu.make_async_copy(src, dst, sems.at[i]) for i, (src, dst) in enumerate(zip(left, stages))]
    whole = [pltpu.make_async_copy(result, out0, sems.at[4]), pltpu.make_async_copy(gskip, out2, sems.at[5])]
    for copy in into + whole:
        copy.start()
    cb, rows, cw = out1.shape
    tall = cgrows.shape[0] // nh
    per = 128 // cw
    share = cb // per
    away = [
        pltpu.make_async_copy(src, dst, sems.at[6 + i])
        for i, (src, dst) in enumerate(zip((out1, out3, out4, out5), [out1h] + grads))
    ]
    into[0].wait()
    for i in range(share):
        line = cgrows[pl.ds(i, nh, stride=tall), :].astype(BF16)
        for q in range(per):
            out1[q * share + i] = line[:, q * cw : (q + 1) * cw]
    away[0].start()
    no = out3.shape[1]
    for k, (total, out) in enumerate(((sumup, out3), (sumfirst, out4))):
        into[1 + k].wait()
        n = out.shape[2]
        turned = total[...]
        if turned.shape[0] < 128:
            fill = jnp.zeros((128 - turned.shape[0], turned.shape[1]), F32)
            turned = jnp.concatenate([turned, fill], axis=0)
        out[...] = turned.T[: 27 * no, :n].reshape(27, no, n)
        away[1 + k].start()
    into[3].wait()
    total = sumsecond[...]
    for t in range(27):
        out5[t] = total[: out5.shape[1], t * no : (t + 1) * no]
    away[3].start()
    for copy in whole + away:
        copy.wait()


def per_device(nd, nh, bottom, skip, upconv_kernel, w_first, w_second, cotangent):
    cb, cw = bottom.shape[3], bottom.shape[2]
    cin, cu = upconv_kernel.shape[3:]
    fw = skip.shape[2]
    cj = w_first.shape[3]
    no = cu // nd
    both, npair = 2 * no, nd // 2
    rows = skip.shape[:2]
    factor = 1.0 / math.sqrt(rows[0] * nd * rows[1] * nh * fw)
    taps = round_up(27 * no, 128)
    ncj, nch = cj // nh, cu // nh
    v = pltpu.VMEM
    upw = upconv_kernel.reshape(27, cin, cu)
    w1 = w_first.reshape(27, cj, cu)
    w2 = w_second.reshape(27, cu, cu)
    cells = rows[0] * rows[1] * fw
    line = max(nd, nh)
    wide = round_up(cin, 128)
    part = 27 * no
    tall = round_up(cb * cw // 128, 8)
    scratch = [
        v((cb, nh, cw), BF16), v(skip.shape, BF16), v(skip.shape, BF16),
        v((round_up(cb, 8), taps), F32), v((round_up(ncj, 8), taps), F32), v((round_up(nch, 8), taps), F32),
        v(upw.shape, BF16), v(w1.shape, BF16), v(w2.shape, BF16), v(cotangent.shape, BF16),
        v((cb * nh, cw), F32),
        v((nh, round_up(cb, 16), 128), BF16), v((nh, round_up(cb, 16), 128), BF16),
        v((3, 3, cw, wide), BF16),
        v((npair, 2, 2, cw, wide), BF16),
        v((4, 4, fw, cu), F32),
        v((4, 4, fw, cj), BF16),
        v((npair, cells, cu), BF16),
        v((npair,) + skip.shape, BF16),
        v((cells, cu), F32),
        v((4, 4, fw, cu), BF16),
        v((npair, cells, cu), BF16),
        v((4, 4, fw, cu), BF16),
        v((4, 4, fw, cu), BF16),
        v((cu, 4 * cells), BF16), v((npair, both, 4 * cells), BF16),
        v((cu, 4 * cells), BF16), v((npair, both, 4 * cells), BF16),
        v((2, 2, fw, cu), F32),
        v((3, 3, 2, cw, cu), BF16),
        v((cu, cells), BF16), v((npair, both, cells), BF16),
        v((nh, tall, 128), F32), v((nh, tall, 128), F32),
        v((2 * part, cj), F32), v((2 * part, cu), F32),
        v((part, cu), F32), v((part, cu), F32),
        v((part, cj), F32), v((part, cj), F32),
        v((part, wide), F32), v((part, wide), F32),
        v((nh, round_up(nch, 8), taps), F32), v((nh, round_up(nch, 8), taps), F32),
        v((nh, round_up(ncj, 16), taps), BF16), v((nh, round_up(ncj, 16), taps), BF16),
        v((nh, round_up(cb, 16), taps), BF16), v((nh, round_up(cb, 16), taps), BF16),
        pltpu.SemaphoreType.DMA((18, line)), pltpu.SemaphoreType.DMA((18, line)),
        pltpu.SemaphoreType.DMA((6, 9)), pltpu.SemaphoreType.DMA((6, 9)),
        pltpu.SemaphoreType.DMA((13,)),
    ]
    shape = jax.ShapeDtypeStruct
    anywhere = pl.BlockSpec(memory_space=pl.ANY)
    tops = [
        shape((nh, tall, 128), F32),
        shape((round_up(cb, 8), taps), F32),
        shape((round_up(ncj, 8), taps), F32),
        shape((round_up(nch, 8), taps), F32),
    ]
    left = pl.pallas_call(
        functools.partial(body, nd, nh, factor),
        out_shape=[shape(skip.shape, BF16), shape(skip.shape, BF16)] + tops,
        in_specs=[anywhere] * 6,
        out_specs=[anywhere] * 6,
        scratch_shapes=scratch,
        compiler_params=pltpu.CompilerParams(
            collective_id=0, has_side_effects=True, vmem_limit_bytes=56 * 1024 * 1024
        ),
        name="decoder",
    )(bottom[0].transpose(2, 0, 1), skip, upw, w1, w2, cotangent)
    tops[0] = shape((nh * tall, 128), F32)
    ends = [shape((cb, nh, cw), BF16), shape((27, no, cb), F32), shape((27, no, ncj), F32), shape((27, nch, no), F32)]
    outs = pl.pallas_call(
        functools.partial(closing, nh),
        out_shape=[shape(skip.shape, BF16), ends[0], shape(skip.shape, BF16)] + ends[1:],
        in_specs=[anywhere] * 6,
        out_specs=[anywhere] * 6,
        scratch_shapes=[v(one.shape, one.dtype) for one in tops + ends] + [pltpu.SemaphoreType.DMA((10,))],
        name="closing",
    )(*left[:2], left[2].reshape(nh * tall, 128), *left[3:])
    return (
        outs[0],
        outs[1].transpose(1, 2, 0)[None],
        outs[2],
        outs[3].reshape(3, 3, 3, no, cb).transpose(0, 1, 2, 4, 3),
        outs[4].reshape(3, 3, 3, no, ncj).transpose(0, 1, 2, 4, 3),
        outs[5].reshape(3, 3, 3, nch, no),
    )


def solution(mesh):
    return jax.shard_map(
        functools.partial(per_device, mesh.shape["depth"], mesh.shape["height"]),
        mesh=mesh,
        in_specs=(
            P("depth", None, None, "height"),
            P("depth", "height", None, None),
            P(),
            P(),
            P(),
            P("depth", "height", None, None),
        ),
        out_specs=(
            P("depth", "height", None, None),
            P("depth", None, None, "height"),
            P("depth", "height", None, None),
            P(None, None, None, "height", "depth"),
            P(None, None, None, "height", "depth"),
            P(None, None, None, "height", "depth"),
        ),
        check_vma=False,
    )
```

```python
import functools
import math

import jax
import jax.numpy as jnp
from jax import lax
from jax.experimental import pallas as pl
from jax.experimental.pallas import tpu as pltpu
from jax.sharding import PartitionSpec as P

MESH = pl.DeviceIdType.MESH
F32 = jnp.float32
BF16 = jnp.bfloat16
GRID9 = [(a, b) for a in range(3) for b in range(3)]
OTHERS = [(a, b) for a in (-1, 0, 1) for b in (-1, 0, 1) if (a, b) != (0, 0)]
NT = (((1,), (1,)), ((), ()))
PARITY_SHIFT = {0: (1, 1), 1: (0, 0), 2: (1, 0)}


def round_up(value, unit):
    return -(-value // unit) * unit


def remote(src, dst, send, recv, target):
    return pltpu.make_async_remote_copy(
        src_ref=src, dst_ref=dst, send_sem=send, recv_sem=recv, device_id=target, device_id_type=MESH
    )


class Spread:
    def __init__(self, log, me, count, target, source, slot, send, recv, steps=None):
        self.me, self.count, self.target = me, count, target
        self.source, self.slot, self.send, self.recv = source, slot, send, recv
        self.steps = steps or (1, count)
        self.arrived, self.log = False, log

    def each(self, act):
        def step(j, carry):
            act(j)
            return carry

        lax.fori_loop(*self.steps, step, 0)

    def outgoing(self, j):
        peer = lax.rem(self.me + j, self.count)
        return remote(
            self.source(peer), self.slot(self.me), self.send.at[peer], self.recv.at[self.me], self.target(peer)
        )

    def incoming(self, j):
        peer = lax.rem(self.me + self.count - j, self.count)
        return remote(
            self.source(peer), self.slot(peer), self.send.at[peer], self.recv.at[peer], self.target(peer)
        )

    def start(self):
        self.log.append(self)
        self.each(lambda j: self.outgoing(j).start())

    def wait_recv(self):
        self.arrived = True
        self.each(lambda j: self.incoming(j).wait_recv())

    def wait_send(self):
        self.each(lambda j: self.outgoing(j).wait_send())


class Halo:
    def __init__(self, log, there, copy, directions):
        self.there, self.copy, self.directions = there, copy, directions
        self.arrived, self.log = False, log

    def each(self, sign, act):
        for dd, dh in self.directions:
            @pl.when(self.there(sign * dd, sign * dh))
            def _(dd=dd, dh=dh):
                act(self.copy(dd, dh))

    def start(self):
        self.log.append(self)
        self.each(1, lambda copy: copy.start())

    def wait_recv(self):
        self.arrived = True
        self.each(-1, lambda copy: copy.wait_recv())

    def wait_send(self):
        self.each(1, lambda copy: copy.wait_send())


def shift_rows(value, by, period):
    rows = value.shape[0]
    row = lax.broadcasted_iota(jnp.int32, value.shape, 0) % period
    edge = 0 if by > 0 else period - 1
    return jnp.where(row == edge, 0.0, pltpu.roll(value, by % rows, 0))


def shift_lanes(value, by, period):
    lanes = value.shape[1]
    lane = lax.broadcasted_iota(jnp.int32, value.shape, 1) % period
    edge = 0 if by > 0 else period - 1
    return jnp.where(lane == edge, 0.0, pltpu.roll(value, by % lanes, 1))


def slope(values):
    sig = jax.nn.sigmoid(values)
    return sig * (1.0 + values * (1.0 - sig))


def dot(a, b, dims=(((1,), (0,)), ((), ()))):
    return lax.dot_general(a, b, dims, preferred_element_type=F32)


def body(
    nd, nh, factor,
    bottom_hbm, skip, upw_hbm, w1_hbm, w2_hbm, cot_hbm,
    result_hbm, gskip_hbm, cgrows, sumup_hbm, sumfirst_hbm, sumsecond_hbm,
    bottom, result, gskip, sumup, sumfirst, sumsecond, upw, w1, w2, cot, bott, bsend, brecv, near, bg, up32, joined, ug, sg, fp, hid, hg, e2, e1, et2s, et2r, et1s, et1r,
    bu32, bu, buts, butr, cgs, cgr, acc1, acc2, px2, pr2, px1, pr1, pxu, pru, gs2, gr2, gs1, gr1, gsu, gru,
    ssem, rsem, hs, hr, loc,
):
    d = lax.axis_index("depth")
    h = lax.axis_index("height")
    pair, core = d // 2, lax.rem(d, 2)
    partner = d + 1 - 2 * core
    npair = nd // 2
    cb, rows_all, cw = bottom.shape
    cu = upw.shape[2]
    cin = upw.shape[1]
    no = cu // nd
    both = 2 * no

    weights = [
        pltpu.make_async_copy(upw_hbm, upw, loc.at[0]),
        pltpu.make_async_copy(w1_hbm, w1, loc.at[1]),
        pltpu.make_async_copy(w2_hbm, w2, loc.at[2]),
        pltpu.make_async_copy(cot_hbm, cot, loc.at[3]),
    ]
    own_skip = pltpu.make_async_copy(skip, joined.at[pl.ds(1, 2), pl.ds(1, 2), :, pl.ds(cu, cu)], loc.at[4])
    own_gathered = pltpu.make_async_copy(skip, sg.at[pair], loc.at[6])

    own_bottom = pltpu.make_async_copy(bottom_hbm, bottom, loc.at[5])
    own_bottom.start()
    for copy in weights:
        copy.start()
    joined[...] = jnp.zeros_like(joined)
    own_skip.start()
    own_gathered.start()
    hid[...] = jnp.zeros_like(hid)
    e2[...] = jnp.zeros_like(e2)
    e1[...] = jnp.zeros_like(e1)
    bu[...] = jnp.zeros_like(bu)


    barrier = pltpu.get_barrier_semaphore()

    def greet_line(count, target):
        def step(j, carry):
            pl.semaphore_signal(barrier, inc=1, device_id=target(j), device_id_type=MESH)
            return carry

        lax.fori_loop(1, count, step, 0)

    greet_line(nh, lambda j: (d, lax.rem(h + j, nh)))
    greet_line(npair, lambda j: (2 * lax.rem(pair + j, npair) + core, h))

    def there(dd, dh):
        ok = None
        for pos, step, count in ((d, dd, nd), (h, dh, nh)):
            if step:
                cond = pos > 0 if step < 0 else pos < count - 1
                ok = cond if ok is None else jnp.logical_and(ok, cond)
        return ok

    for dd in (-1, 1):
        for dh in (-1, 0, 1):
            target = (lax.rem(d + dd + nd, nd), lax.rem(h + dh + nh, nh))
            pl.semaphore_signal(barrier, inc=1, device_id=target, device_id_type=MESH)

    own_bottom.wait()
    bott[...] = bottom[...].astype(F32).reshape(cb * rows_all, cw)
    lines = [bott[pl.ds(r, cb, stride=rows_all), :] for r in range(rows_all)]
    blank = jnp.zeros((cb, cw), F32)
    rest = jnp.zeros((cb, 128 - 3 * cw), F32)
    pad = jnp.zeros((bsend.shape[1] - cb, 128), F32)
    for p in range(nh):
        before = lines[p - 1] if p > 0 else blank
        after = lines[p + 1] if p < nh - 1 else blank
        window = jnp.concatenate([before, lines[p], after, rest], axis=1)
        bsend[p] = jnp.concatenate([window, pad], axis=0).astype(BF16)
    brecv[h] = bsend[h]
    pl.semaphore_wait(barrier, nh + npair + 4)

    def src_part(step):
        return {0: pl.ds(1, 2), 1: pl.ds(2, 1), -1: pl.ds(1, 1)}[step]

    def own_part(step):
        return {0: pl.ds(0, 2), 1: pl.ds(1, 1), -1: pl.ds(0, 1)}[step]

    def dst_part(step):
        return {0: pl.ds(1, 2), 1: pl.ds(0, 1), -1: pl.ds(3, 1)}[step]

    log = []

    def halo(phase, copy_of, directions=OTHERS):
        def copy(dd, dh):
            slot = (dd + 1) * 3 + dh + 1
            src, dst = copy_of(dd, dh)
            return remote(src, dst, hs.at[phase, slot], hr.at[phase, slot], (d + dd, h + dh))

        return Halo(log, there, copy, directions)

    def field_halo(phase, field):
        return halo(
            phase,
            lambda dd, dh: (
                field.at[src_part(dd), src_part(dh)],
                field.at[dst_part(dd), dst_part(dh)],
            ),
        )

    def line_h(phase, source, slot):
        return Spread(log, h, nh, lambda p: (d, p), source, slot, ssem.at[phase], rsem.at[phase])

    def line_d(phase, source, slot, steps):
        return Spread(log, d, nd, lambda p: (p, h), source, slot, ssem.at[phase], rsem.at[phase], steps)

    def line_p(phase, source, slot):
        return Spread(
            log, pair, npair, lambda p: (2 * p + core, h), source, slot, ssem.at[phase], rsem.at[phase]
        )

    rows_out = line_h(0, lambda p: bsend.at[p], lambda s: brecv.at[s])
    rows_out.start()
    skip_halo = halo(
        0,
        lambda dd, dh: (
            skip.at[own_part(dd), own_part(dh)],
            joined.at[dst_part(dd), dst_part(dh), :, pl.ds(cu, cu)],
        ),
    )
    skip_halo.start()
    skip_out = line_p(17, lambda p: sg.at[pair], lambda s: sg.at[s])
    own_gathered.wait()
    skip_out.start()
    rows_out.wait_recv()
    stack = [brecv[c].astype(F32)[:cb] for c in range(nh)]
    wide = near.shape[3]
    if wide > cin:
        stack.append(jnp.zeros((wide - cin, 128), F32))
    near[1] = jnp.concatenate(stack, axis=0).T[: 3 * cw].reshape(3, cw, wide).astype(BF16)

    plane_next = line_d(1, lambda p: near.at[1], lambda s: near.at[0], (1, 2))
    plane_prev = line_d(2, lambda p: near.at[1], lambda s: near.at[2], (nd - 1, nd))
    plane_next.start()
    plane_prev.start()
    bg[core, pair] = near[1, 1:3]
    bg[0, npair] = jnp.zeros_like(near[1, 1:3])
    planes_out = line_p(6, lambda p: bg.at[core, pair], lambda s: bg.at[core, s])
    planes_out.start()
    weights[0].wait()
    plane_next.wait_recv()
    plane_prev.wait_recv()

    coarse = []
    for s in range(3):
        plane = d - 1 + s
        here = jnp.logical_and(plane >= 0, plane < nd)
        value = near[s, :, :, 0:cin]
        coarse.append(jnp.where(here, value, jnp.zeros_like(value)))
    coarse = jnp.stack(coarse)
    first_of = {0: 1, 1: 1, 2: 0}
    for gd in range(2):
        for gh in range(2):
            total = None
            for kd in ((1,), (0, 2))[gd]:
                for kh in ((1,), (0, 2))[gh]:
                    a, b = first_of[kd], first_of[kh]
                    lhs = coarse[a : a + 2, b : b + 2].reshape(4 * cw, -1)
                    t = kd * 9 + kh * 3
                    rhs = jnp.concatenate([upw[t], upw[t + 1], upw[t + 2]], axis=1)
                    part = dot(lhs, rhs)
                    total = part if total is None else total + part
            even = total[:, cu : 2 * cu]
            odd = total[:, 2 * cu :] + shift_rows(total[:, :cu], -1, cw)
            for i in range(2):
                for j in range(2):
                    at = (i * 2 + j) * cw
                    fd, fh = 2 * i + 1 - gd, 2 * j + 1 - gh
                    up32[fd, fh, pl.ds(0, cw, stride=2), :] = even[at : at + cw]
                    up32[fd, fh, pl.ds(1, cw, stride=2), :] = odd[at : at + cw]
    for fd in range(4):
        for fh in range(4):
            inside = None
            for pos, f, count in ((d, fd, nd), (h, fh, nh)):
                cond = None
                if f == 0:
                    cond = pos > 0
                if f == 3:
                    cond = pos < count - 1
                if cond is not None:
                    inside = cond if inside is None else jnp.logical_and(inside, cond)
            value = up32[fd, fh]
            if inside is not None:
                value = jnp.where(inside, value, 0.0)
            joined[fd, fh, :, 0:cu] = value.astype(BF16)

    own_skip.wait()
    skip_halo.wait_recv()
    weights[1].wait()
    cells = 4 * 2 * cw

    def conv(field, weight):
        chans = field.shape[3]
        lhs = jnp.concatenate(
            [field[a : a + 2, b : b + 2].reshape(cells, chans) for a, b in GRID9], axis=1
        )
        rhs = jnp.concatenate(
            [
                jnp.concatenate([weight[(a * 3 + b) * 3 + c] for c in range(3)], axis=1)
                for a, b in GRID9
            ],
            axis=0,
        )
        y = dot(lhs, rhs)
        n = weight.shape[2]
        return shift_rows(y[:, :n], 1, 2 * cw) + y[:, n : 2 * n] + shift_rows(y[:, 2 * n :], -1, 2 * cw)

    def conv_back(field, weight):
        chans = field.shape[3]
        lhs = jnp.concatenate(
            [field[2 - a : 4 - a, 2 - b : 4 - b].reshape(cells, chans) for a, b in GRID9], axis=1
        )
        rhs = jnp.concatenate(
            [
                jnp.concatenate([weight[(a * 3 + b) * 3 + c] for a, b in GRID9], axis=1)
                for c in range(3)
            ],
            axis=0,
        )
        y = dot(lhs, rhs, NT)
        n = weight.shape[1]
        return shift_rows(y[:, :n], -1, 2 * cw) + y[:, n : 2 * n] + shift_rows(y[:, 2 * n :], 1, 2 * cw)

    first_pre = conv(joined, w1)
    fp[...] = first_pre
    hidden = (first_pre * jax.nn.sigmoid(first_pre)).astype(BF16)
    hid[1:3, 1:3] = hidden.reshape(2, 2, 2 * cw, cu)
    hid_halo = field_halo(2, hid)
    hid_halo.start()
    hg[pair] = hidden
    ug[pair] = joined[1:3, 1:3, :, 0:cu].reshape(cells, cu)
    up_out = line_p(4, lambda p: ug.at[pair], lambda s: ug.at[s])
    up_out.start()

    weights[2].wait()
    weights[3].wait()
    hid_halo.wait_recv()
    second_pre = conv(hid, w2)
    result[...] = (second_pre * jax.nn.sigmoid(second_pre)).astype(BF16).reshape(2, 2, 2 * cw, cu)
    err2 = (cot[...].reshape(cells, cu).astype(F32) * slope(second_pre)).astype(BF16)
    e2[1:3, 1:3] = err2.reshape(2, 2, 2 * cw, cu)
    out_result = pltpu.make_async_copy(result, result_hbm, loc.at[7])
    out_result.start()
    e2_halo = field_halo(3, e2)
    e2_halo.start()
    hid_out = line_p(3, lambda p: hg.at[pair], lambda s: hg.at[s])
    hid_out.start()

    e2_halo.wait_recv()
    err1 = (conv_back(e2, w2) * slope(fp[...])).astype(BF16)
    e1[1:3, 1:3] = err1.reshape(2, 2, 2 * cw, cu)
    e1_halo = field_halo(4, e1)
    e1_halo.start()

    def part_of(p):
        return pl.ds(pl.multiple_of(p * both, both), both)

    def flip(value, phase, out, into):
        out[...] = value.astype(F32).T.astype(BF16)
        into[pair] = out[part_of(pair)]
        spread = line_p(phase, lambda p: out.at[part_of(p)], lambda s: into.at[s])
        spread.start()
        return spread

    e2_out = flip(e2[...].reshape(4 * cells, cu), 5, et2s, et2r)

    def swap_copy(phase, src, dst, arriving):
        copy = Spread(log, 0, 2, None, None, None, None, None)
        sems = ssem.at[phase, 0], rsem.at[phase, 0]
        copy.outgoing = lambda j: remote(src, dst, *sems, (partner, h))
        copy.incoming = lambda j: remote(src, arriving, *sems, (partner, h))
        return copy

    e1_halo.wait_recv()
    back = conv_back(e1, w1)
    bu32[...] = back[:, :cu].reshape(2, 2, 2 * cw, cu)
    for i in range(2):
        for j in range(2):
            for par in range(2):
                bu[1 + i, 1 + j, par] = bu32[i, j, pl.ds(par, cw, stride=2), :].astype(BF16)
    bu_halo = halo(
        5,
        lambda dd, dh: (
            bu.at[pl.ds(2, 1) if dd else pl.ds(1, 2), pl.ds(2, 1) if dh else pl.ds(1, 2)],
            bu.at[pl.ds(0, 1) if dd else pl.ds(1, 2), pl.ds(0, 1) if dh else pl.ds(1, 2)],
        ),
        [(1, 0), (0, 1), (1, 1)],
    )
    bu_halo.start()
    bu_out = flip(bu[1:3, 1:3].reshape(cells, cu), 7, buts, butr)
    e1_out = flip(e1[...].reshape(4 * cells, cu), 8, et1s, et1r)
    planes_out.wait_recv()
    planes_swap = swap_copy(16, bg.at[core, pl.ds(0, npair)], bg.at[core, pl.ds(0, npair)], bg.at[1 - core, pl.ds(0, npair)])
    planes_swap.start()
    gskip[...] = back[:, cu:].astype(BF16).reshape(2, 2, 2 * cw, cu)
    out_gskip = pltpu.make_async_copy(gskip, gskip_hbm, loc.at[8])
    out_gskip.start()

    def weight_grad(into, gathered, acc):
        acc[...] = jnp.zeros_like(acc)
        half = 2 * cw
        per_plane = 4 * half
        lane = lax.broadcasted_iota(jnp.int32, (both, 128), 1)

        def step(j, carry):
            shifted = []
            for plane in range(4):
                at = plane * per_plane
                low = into[j, :, at : at + 128].astype(F32)
                high = into[j, :, at + 128 : at + 256].astype(F32)
                mid = jnp.where(lane < half, pltpu.roll(low, half, 1), pltpu.roll(high, half, 1))
                shifted.append(
                    [
                        rows if kw == 1 else shift_lanes(rows, kw - 1, half)
                        for rows in (high, mid, low)
                        for kw in range(3)
                    ]
                )
            lhs = []
            for c in range(2):
                for kd in range(3):
                    for k in range(9):
                        pieces = [shifted[2 - kd + q][k][c * no : (c + 1) * no] for q in range(2)]
                        lhs.append(jnp.concatenate(pieces, axis=1))
            acc[...] += dot(jnp.concatenate(lhs, axis=0).astype(BF16), gathered(j))
            return carry

        lax.fori_loop(0, npair, step, 0)
        return acc[...]

    def swap(phase, value, out, into):
        half = 27 * no
        halves = [value[:half], value[half:]]
        mine = jnp.where(core == 0, halves[0], halves[1])
        out[...] = jnp.where(core == 0, halves[1], halves[0])
        copy = swap_copy(phase, out, into, into)
        copy.start()
        return copy, mine

    def flipped(value):
        rows, lanes = value.shape
        tall, wide = round_up(rows, 128), round_up(lanes, 128)
        if tall > rows:
            value = jnp.concatenate([value, jnp.zeros((tall - rows, lanes), F32)], axis=0)
        if wide > lanes:
            value = jnp.concatenate([value, jnp.zeros((tall, wide - lanes), F32)], axis=1)
        return value.T

    def scatter_rows(phase, swapped, arriving, chunk, out, into):
        copy, mine = swapped
        copy.wait_recv()
        turned = flipped((mine + arriving[...]) * factor)
        fill = out.shape[1] - chunk
        for c in range(nh):
            piece = turned[c * chunk : (c + 1) * chunk]
            if fill:
                piece = jnp.concatenate([piece, jnp.zeros((fill, piece.shape[1]), F32)], axis=0)
            out[c] = piece.astype(out.dtype)
        into[h] = out[h]
        spread = line_h(phase, lambda p: out.at[p], lambda s: into.at[s])
        spread.start()
        return spread

    e2_out.wait_recv()
    hid_out.wait_recv()
    swap2 = swap(9, weight_grad(et2r, lambda j: hg[j], acc2), px2, pr2)

    bu_halo.wait_recv()
    around = lambda par: [bu[a, b, par].reshape(cw, cu) for a, b in GRID9]
    lhs = jnp.concatenate(around(0) + around(1), axis=1)
    rhs = jnp.concatenate(
        [upw[(a * 3 + b) * 3 + 1] for a, b in GRID9] + [upw[(a * 3 + b) * 3 + 2] for a, b in GRID9], axis=1
    )
    same = dot(lhs, rhs, NT)
    lhs = jnp.concatenate(around(1), axis=1)
    rhs = jnp.concatenate([upw[(a * 3 + b) * 3] for a, b in GRID9], axis=1)
    block_grad = flipped(same + shift_rows(dot(lhs, rhs, NT), 1, cw))
    share = cb // (128 // cw)
    for c in range(nh):
        groups = [block_grad[c * cb + q : c * cb + q + share, :cw] for q in range(0, cb, share)]
        cgs[c, 0:share] = jnp.concatenate(groups, axis=1)
    cgr[h] = cgs[h]
    cg_out = line_h(10, lambda p: cgs.at[p], lambda s: cgr.at[s])
    cg_out.start()
    g2_out = scatter_rows(11, swap2, pr2, cu // nh, gs2, gr2)

    bu_out.wait_recv()
    per = 128 // cw
    span = npair * cw
    group = min(per, npair)
    lane = lax.broadcasted_iota(jnp.int32, (both, 128), 1) // cw
    phases = {}
    for pd in range(2):
        for p in range(per):
            groups = []
            for g in range(npair // group):
                total = None
                for s in range(group):
                    piece = butr[g * group + s, :, pd * 128 : (pd + 1) * 128].astype(F32)
                    turn = ((s - p) * cw) % 128
                    piece = pltpu.roll(piece, turn, 1) if turn else piece
                    total = piece if total is None else jnp.where(lane == s, piece, total)
                groups.append(total)
            value = jnp.concatenate(groups, axis=1) if len(groups) > 1 else groups[0]
            phases[pd, p // 2, p % 2] = value[:, :span]

    def tap_rows(kd, kh, kw):
        pw, sw = PARITY_SHIFT[kw]
        value = phases[PARITY_SHIFT[kd][0], PARITY_SHIFT[kh][0], pw]
        return shift_lanes(value, 1, cw) if sw else value

    planes_swap.wait_recv()
    products = {}
    for sd, kds in ((0, (1, 2)), (1, (0,))):
        for sh, khs in ((0, (1, 2)), (1, (0,))):
            order = [(kd, kh, kw) for kd in kds for kh in khs for kw in range(3)]
            lhs = jnp.concatenate([tap_rows(*k) for k in order], axis=0).astype(BF16)
            odd_one = lax.rem(core + sd, 2)
            first = core * sd
            rhs = bg[odd_one, pl.ds(first, npair), sh].reshape(span, -1)
            value = dot(lhs, rhs)
            for i, k in enumerate(order):
                for c in range(2):
                    at = (i * 2 + c) * no
                    products[(c,) + k] = value[at : at + no]
    grad_up = jnp.concatenate(
        [products[c, a, b, e] for c in range(2) for a, b in GRID9 for e in range(3)], axis=0
    )
    swapu = swap(12, grad_up, pxu, pru)

    e1_out.wait_recv()
    up_out.wait_recv()
    skip_out.wait_recv()
    swap1 = swap(13, weight_grad(et1r, lambda j: jnp.concatenate([ug[j], sg[j].reshape(cells, cu)], axis=1), acc1), px1, pr1)
    gu_out = scatter_rows(14, swapu, pru, cb, gsu, gru)
    g1_out = scatter_rows(15, swap1, pr1, 2 * cu // nh, gs1, gr1)

    def finish(spread, into, out, hbm, at):
        spread.wait_recv()
        total = into[0].astype(F32)
        for s in range(1, nh):
            total = total + into[s].astype(F32)
        out[...] = total[: out.shape[0]]
        copy = pltpu.make_async_copy(out, hbm, loc.at[at])
        copy.start()
        return copy

    finished = [finish(g2_out, gr2, sumsecond, sumsecond_hbm, 9)]
    cg_out.wait_recv()
    out_cg = pltpu.make_async_copy(cgr, cgrows, loc.at[10])
    out_cg.start()
    finished.append(finish(gu_out, gru, sumup, sumup_hbm, 11))
    finished.append(finish(g1_out, gr1, sumfirst, sumfirst_hbm, 12))
    for copy in finished + [out_cg, out_result, out_gskip]:
        copy.wait()

    for part in log:
        if not part.arrived:
            part.wait_recv()
        part.wait_send()


def closing(nh, *refs):
    (result, gskip, *left), (out0, out1h, out2, *grads), (cgrows, sumup, sumfirst, sumsecond) = (
        refs[:6], refs[6:12], refs[12:16]
    )
    out1, out3, out4, out5, pass0, pass1, sems = refs[16:]
    stages = (cgrows, sumup, sumfirst, sumsecond)
    into = [pltpu.make_async_copy(src, dst, sems.at[i]) for i, (src, dst) in enumerate(zip(left, stages))]
    through = [pltpu.make_async_copy(result, pass0, sems.at[4]), pltpu.make_async_copy(gskip, pass1, sems.at[5])]
    whole = [pltpu.make_async_copy(pass0, out0, sems.at[10]), pltpu.make_async_copy(pass1, out2, sems.at[11])]
    for copy in into + through:
        copy.start()
    cb, rows, cw = out1.shape
    tall = cgrows.shape[0] // nh
    per = 128 // cw
    share = cb // per
    away = [
        pltpu.make_async_copy(src, dst, sems.at[6 + i])
        for i, (src, dst) in enumerate(zip((out1, out3, out4, out5), [out1h] + grads))
    ]
    into[0].wait()
    for i in range(share):
        line = cgrows[pl.ds(i, nh, stride=tall), :].astype(BF16)
        for q in range(per):
            out1[q * share + i] = line[:, q * cw : (q + 1) * cw]
    away[0].start()
    for arriving, leaving in zip(through, whole):
        arriving.wait()
        leaving.start()
    no = out3.shape[1]
    for k, (total, out) in enumerate(((sumup, out3), (sumfirst, out4))):
        into[1 + k].wait()
        n = out.shape[2]
        turned = total[...]
        if turned.shape[0] < 128:
            fill = jnp.zeros((128 - turned.shape[0], turned.shape[1]), F32)
            turned = jnp.concatenate([turned, fill], axis=0)
        out[...] = turned.T[: 27 * no, :n].reshape(27, no, n)
        away[1 + k].start()
    into[3].wait()
    total = sumsecond[...]
    for t in range(27):
        out5[t] = total[: out5.shape[1], t * no : (t + 1) * no]
    away[3].start()
    for copy in whole + away:
        copy.wait()


def per_device(nd, nh, bottom, skip, upconv_kernel, w_first, w_second, cotangent):
    cb, cw = bottom.shape[3], bottom.shape[2]
    cin, cu = upconv_kernel.shape[3:]
    fw = skip.shape[2]
    cj = w_first.shape[3]
    no = cu // nd
    both, npair = 2 * no, nd // 2
    rows = skip.shape[:2]
    factor = 1.0 / math.sqrt(rows[0] * nd * rows[1] * nh * fw)
    taps = round_up(27 * no, 128)
    ncj, nch = cj // nh, cu // nh
    v = pltpu.VMEM
    upw = upconv_kernel.reshape(27, cin, cu)
    w1 = w_first.reshape(27, cj, cu)
    w2 = w_second.reshape(27, cu, cu)
    cells = rows[0] * rows[1] * fw
    line = max(nd, nh)
    wide = round_up(cin, 128)
    part = 27 * no
    tall = round_up(cb * cw // 128, 8)
    scratch = [
        v((cb, nh, cw), BF16), v(skip.shape, BF16), v(skip.shape, BF16),
        v((round_up(cb, 8), taps), F32), v((round_up(ncj, 8), taps), F32), v((round_up(nch, 8), taps), F32),
        v(upw.shape, BF16), v(w1.shape, BF16), v(w2.shape, BF16), v(cotangent.shape, BF16),
        v((cb * nh, cw), F32),
        v((nh, round_up(cb, 16), 128), BF16), v((nh, round_up(cb, 16), 128), BF16),
        v((3, 3, cw, wide), BF16),
        v((2, npair + 1, 2, cw, wide), BF16),
        v((4, 4, fw, cu), F32),
        v((4, 4, fw, cj), BF16),
        v((npair, cells, cu), BF16),
        v((npair,) + skip.shape, BF16),
        v((cells, cu), F32),
        v((4, 4, fw, cu), BF16),
        v((npair, cells, cu), BF16),
        v((4, 4, fw, cu), BF16),
        v((4, 4, fw, cu), BF16),
        v((cu, 4 * cells), BF16), v((npair, both, 4 * cells), BF16),
        v((cu, 4 * cells), BF16), v((npair, both, 4 * cells), BF16),
        v((2, 2, fw, cu), F32),
        v((3, 3, 2, cw, cu), BF16),
        v((cu, cells), BF16), v((npair, both, cells), BF16),
        v((nh, tall, 128), F32), v((nh, tall, 128), F32),
        v((2 * part, cj), F32), v((2 * part, cu), F32),
        v((part, cu), F32), v((part, cu), F32),
        v((part, cj), F32), v((part, cj), F32),
        v((part, wide), F32), v((part, wide), F32),
        v((nh, round_up(nch, 8), taps), F32), v((nh, round_up(nch, 8), taps), F32),
        v((nh, round_up(ncj, 16), taps), BF16), v((nh, round_up(ncj, 16), taps), BF16),
        v((nh, round_up(cb, 16), taps), BF16), v((nh, round_up(cb, 16), taps), BF16),
        pltpu.SemaphoreType.DMA((18, line)), pltpu.SemaphoreType.DMA((18, line)),
        pltpu.SemaphoreType.DMA((6, 9)), pltpu.SemaphoreType.DMA((6, 9)),
        pltpu.SemaphoreType.DMA((13,)),
    ]
    shape = jax.ShapeDtypeStruct
    anywhere = pl.BlockSpec(memory_space=pl.ANY)
    tops = [
        shape((nh, tall, 128), F32),
        shape((round_up(cb, 8), taps), F32),
        shape((round_up(ncj, 8), taps), F32),
        shape((round_up(nch, 8), taps), F32),
    ]
    left = pl.pallas_call(
        functools.partial(body, nd, nh, factor),
        out_shape=[shape(skip.shape, BF16), shape(skip.shape, BF16)] + tops,
        in_specs=[anywhere] * 6,
        out_specs=[anywhere] * 6,
        scratch_shapes=scratch,
        compiler_params=pltpu.CompilerParams(
            collective_id=0, has_side_effects=True, vmem_limit_bytes=56 * 1024 * 1024
        ),
        name="decoder",
    )(bottom[0].transpose(2, 0, 1), skip, upw, w1, w2, cotangent)
    tops[0] = shape((nh * tall, 128), F32)
    ends = [shape((cb, nh, cw), BF16), shape((27, no, cb), F32), shape((27, no, ncj), F32), shape((27, nch, no), F32)]
    outs = pl.pallas_call(
        functools.partial(closing, nh),
        out_shape=[shape(skip.shape, BF16), ends[0], shape(skip.shape, BF16)] + ends[1:],
        in_specs=[anywhere] * 6,
        out_specs=[anywhere] * 6,
        scratch_shapes=[v(one.shape, one.dtype) for one in tops + ends]
        + [v(skip.shape, BF16), v(skip.shape, BF16), pltpu.SemaphoreType.DMA((12,))],
        name="closing",
    )(*left[:2], left[2].reshape(nh * tall, 128), *left[3:])
    return (
        outs[0],
        outs[1].transpose(1, 2, 0)[None],
        outs[2],
        outs[3].reshape(3, 3, 3, no, cb).transpose(0, 1, 2, 4, 3),
        outs[4].reshape(3, 3, 3, no, ncj).transpose(0, 1, 2, 4, 3),
        outs[5].reshape(3, 3, 3, nch, no),
    )


def solution(mesh):
    return jax.shard_map(
        functools.partial(per_device, mesh.shape["depth"], mesh.shape["height"]),
        mesh=mesh,
        in_specs=(
            P("depth", None, None, "height"),
            P("depth", "height", None, None),
            P(),
            P(),
            P(),
            P("depth", "height", None, None),
        ),
        out_specs=(
            P("depth", "height", None, None),
            P("depth", None, None, "height"),
            P("depth", "height", None, None),
            P(None, None, None, "height", "depth"),
            P(None, None, None, "height", "depth"),
            P(None, None, None, "height", "depth"),
        ),
        check_vma=False,
    )
```

```python
import functools
import math

import jax
import jax.numpy as jnp
from jax import lax
from jax.experimental import pallas as pl
from jax.experimental.pallas import tpu as pltpu
from jax.sharding import PartitionSpec as P

MESH = pl.DeviceIdType.MESH
F32 = jnp.float32
BF16 = jnp.bfloat16
GRID9 = [(a, b) for a in range(3) for b in range(3)]
OTHERS = [(a, b) for a in (-1, 0, 1) for b in (-1, 0, 1) if (a, b) != (0, 0)]
NT = (((1,), (1,)), ((), ()))
PARITY_SHIFT = {0: (1, 1), 1: (0, 0), 2: (1, 0)}


def round_up(value, unit):
    return -(-value // unit) * unit


def remote(src, dst, send, recv, target):
    return pltpu.make_async_remote_copy(
        src_ref=src, dst_ref=dst, send_sem=send, recv_sem=recv, device_id=target, device_id_type=MESH
    )


class Spread:
    def __init__(self, log, me, count, target, source, slot, bulk, send, recv):
        self.me, self.count, self.target = me, count, target
        self.source, self.slot, self.bulk, self.send, self.recv = source, slot, bulk, send, recv
        self.arrived, self.log = False, log

    def start(self):
        self.log.append(self)

        def step(j, carry):
            peer = lax.rem(self.me + j, self.count)
            remote(self.source(peer), self.slot(self.me), self.send, self.recv, self.target(peer)).start()
            return carry

        lax.fori_loop(1, self.count, step, 0)

    def whole(self):
        peer = lax.rem(self.me + 1, self.count)
        return remote(self.bulk, self.bulk, self.send, self.recv, self.target(peer))

    def wait_recv(self):
        self.arrived = True
        self.whole().wait_recv()

    def wait_send(self):
        self.whole().wait_send()


class Single:
    def __init__(self, log, out, into):
        self.out, self.into = out, into
        self.arrived, self.log = False, log

    def start(self):
        self.log.append(self)
        self.out.start()

    def wait_recv(self):
        self.arrived = True
        self.into.wait_recv()

    def wait_send(self):
        self.out.wait_send()


class Halo:
    def __init__(self, log, there, copy, directions):
        self.there, self.copy, self.directions = there, copy, directions
        self.arrived, self.log = False, log

    def each(self, sign, act):
        for dd, dh in self.directions:
            @pl.when(self.there(sign * dd, sign * dh))
            def _(dd=dd, dh=dh):
                act(self.copy(dd, dh))

    def start(self):
        self.log.append(self)
        self.each(1, lambda copy: copy.start())

    def wait_recv(self):
        self.arrived = True
        self.each(-1, lambda copy: copy.wait_recv())

    def wait_send(self):
        self.each(1, lambda copy: copy.wait_send())


def shift_rows(value, by, period):
    rows = value.shape[0]
    row = lax.broadcasted_iota(jnp.int32, value.shape, 0) % period
    edge = 0 if by > 0 else period - 1
    return jnp.where(row == edge, 0.0, pltpu.roll(value, by % rows, 0))


def shift_lanes(value, by, period):
    lanes = value.shape[1]
    lane = lax.broadcasted_iota(jnp.int32, value.shape, 1) % period
    edge = 0 if by > 0 else period - 1
    return jnp.where(lane == edge, 0.0, pltpu.roll(value, by % lanes, 1))


def slope(values):
    sig = jax.nn.sigmoid(values)
    return sig * (1.0 + values * (1.0 - sig))


def dot(a, b, dims=(((1,), (0,)), ((), ()))):
    return lax.dot_general(a, b, dims, preferred_element_type=F32)


def body(
    nd, nh, factor,
    bottom_hbm, skip, upw_hbm, w1_hbm, w2_hbm, cot_hbm,
    result_hbm, gskip_hbm, cgrows, sumup_hbm, sumfirst_hbm, sumsecond_hbm,
    bottom, result, gskip, sumup, sumfirst, sumsecond, upw, w1, w2, cot, bott, bsend, brecv, near, bg, up32, joined, ug, sg, fp, hid, hg, e2, e1, et2s, et2r, et1s, et1r,
    bu32, bu, buts, butr, cgr, acc1, acc2, px2, pr2, px1, pr1, pxu, pru, gs2, gr2, gs1, gr1, gsu, gru,
    ssem, rsem, hs, hr, loc,
):
    d = lax.axis_index("depth")
    h = lax.axis_index("height")
    pair, core = d // 2, lax.rem(d, 2)
    partner = d + 1 - 2 * core
    npair = nd // 2
    cb, rows_all, cw = bottom.shape
    cu = upw.shape[2]
    cin = upw.shape[1]
    no = cu // nd
    both = 2 * no

    weights = [
        pltpu.make_async_copy(upw_hbm, upw, loc.at[0]),
        pltpu.make_async_copy(w1_hbm, w1, loc.at[1]),
        pltpu.make_async_copy(w2_hbm, w2, loc.at[2]),
        pltpu.make_async_copy(cot_hbm, cot, loc.at[3]),
    ]
    own_skip = pltpu.make_async_copy(skip, joined.at[pl.ds(1, 2), pl.ds(1, 2), :, pl.ds(cu, cu)], loc.at[4])
    own_gathered = pltpu.make_async_copy(skip, sg.at[pair], loc.at[6])

    own_bottom = pltpu.make_async_copy(bottom_hbm, bottom, loc.at[5])
    own_bottom.start()
    for copy in weights:
        copy.start()
    joined[...] = jnp.zeros_like(joined)
    own_skip.start()
    own_gathered.start()
    hid[...] = jnp.zeros_like(hid)
    e2[...] = jnp.zeros_like(e2)
    e1[...] = jnp.zeros_like(e1)
    bu[...] = jnp.zeros_like(bu)


    barrier = pltpu.get_barrier_semaphore()

    def greet_line(count, target):
        def step(j, carry):
            pl.semaphore_signal(barrier, inc=1, device_id=target(j), device_id_type=MESH)
            return carry

        lax.fori_loop(1, count, step, 0)

    greet_line(nh, lambda j: (d, lax.rem(h + j, nh)))
    greet_line(npair, lambda j: (2 * lax.rem(pair + j, npair) + core, h))

    def there(dd, dh):
        ok = None
        for pos, step, count in ((d, dd, nd), (h, dh, nh)):
            if step:
                cond = pos > 0 if step < 0 else pos < count - 1
                ok = cond if ok is None else jnp.logical_and(ok, cond)
        return ok

    for dd in (-1, 1):
        for dh in (-1, 0, 1):
            target = (lax.rem(d + dd + nd, nd), lax.rem(h + dh + nh, nh))
            pl.semaphore_signal(barrier, inc=1, device_id=target, device_id_type=MESH)

    own_bottom.wait()
    bott[...] = bottom[...].astype(F32).reshape(cb * rows_all, cw)
    lines = [bott[pl.ds(r, cb, stride=rows_all), :] for r in range(rows_all)]
    blank = jnp.zeros((cb, cw), F32)
    rest = jnp.zeros((cb, 128 - 3 * cw), F32)
    pad = jnp.zeros((bsend.shape[1] - cb, 128), F32)
    for p in range(nh):
        before = lines[p - 1] if p > 0 else blank
        after = lines[p + 1] if p < nh - 1 else blank
        window = jnp.concatenate([before, lines[p], after, rest], axis=1)
        bsend[p] = jnp.concatenate([window, pad], axis=0).astype(BF16)
    brecv[h] = bsend[h]
    pl.semaphore_wait(barrier, nh + npair + 4)

    def src_part(step):
        return {0: pl.ds(1, 2), 1: pl.ds(2, 1), -1: pl.ds(1, 1)}[step]

    def own_part(step):
        return {0: pl.ds(0, 2), 1: pl.ds(1, 1), -1: pl.ds(0, 1)}[step]

    def dst_part(step):
        return {0: pl.ds(1, 2), 1: pl.ds(0, 1), -1: pl.ds(3, 1)}[step]

    log = []

    def halo(phase, copy_of, directions=OTHERS):
        def copy(dd, dh):
            slot = (dd + 1) * 3 + dh + 1
            src, dst = copy_of(dd, dh)
            return remote(src, dst, hs.at[phase, slot], hr.at[phase, slot], (d + dd, h + dh))

        return Halo(log, there, copy, directions)

    def field_halo(phase, field):
        return halo(
            phase,
            lambda dd, dh: (
                field.at[src_part(dd), src_part(dh)],
                field.at[dst_part(dd), dst_part(dh)],
            ),
        )

    def line_h(phase, source, into):
        return Spread(
            log, h, nh, lambda p: (d, p), source, lambda s: into.at[s], into.at[pl.ds(0, nh - 1)],
            ssem.at[phase], rsem.at[phase],
        )

    def line_p(phase, source, into):
        return Spread(
            log, pair, npair, lambda p: (2 * p + core, h), source, lambda s: into.at[s],
            into.at[pl.ds(0, npair - 1)], ssem.at[phase], rsem.at[phase],
        )

    def single(phase, src, dst, target, arriving):
        sems = ssem.at[phase], rsem.at[phase]
        return Single(log, remote(src, dst, *sems, target), remote(src, arriving, *sems, target))

    rows_out = line_h(0, lambda p: bsend.at[p], brecv)
    rows_out.start()
    skip_halo = halo(
        0,
        lambda dd, dh: (
            skip.at[own_part(dd), own_part(dh)],
            joined.at[dst_part(dd), dst_part(dh), :, pl.ds(cu, cu)],
        ),
    )
    skip_halo.start()
    skip_out = line_p(17, lambda p: sg.at[pair], sg)
    own_gathered.wait()
    skip_out.start()
    rows_out.wait_recv()
    stack = [brecv[c].astype(F32)[:cb] for c in range(nh)]
    wide = near.shape[3]
    if wide > cin:
        stack.append(jnp.zeros((wide - cin, 128), F32))
    near[1] = jnp.concatenate(stack, axis=0).T[: 3 * cw].reshape(3, cw, wide).astype(BF16)

    plane_next = single(1, near.at[1], near.at[0], (lax.rem(d + 1, nd), h), near.at[0])
    plane_prev = single(2, near.at[1], near.at[2], (lax.rem(d + nd - 1, nd), h), near.at[2])
    plane_next.start()
    plane_prev.start()
    bg[core, pair] = near[1, 1:3]
    bg[0, npair] = jnp.zeros_like(near[1, 1:3])
    planes_out = line_p(6, lambda p: bg.at[core, pair], bg.at[core])
    planes_out.start()
    weights[0].wait()
    plane_next.wait_recv()
    plane_prev.wait_recv()

    coarse = []
    for s in range(3):
        plane = d - 1 + s
        here = jnp.logical_and(plane >= 0, plane < nd)
        value = near[s, :, :, 0:cin]
        coarse.append(jnp.where(here, value, jnp.zeros_like(value)))
    coarse = jnp.stack(coarse)
    first_of = {0: 1, 1: 1, 2: 0}
    for gd in range(2):
        for gh in range(2):
            total = None
            for kd in ((1,), (0, 2))[gd]:
                for kh in ((1,), (0, 2))[gh]:
                    a, b = first_of[kd], first_of[kh]
                    lhs = coarse[a : a + 2, b : b + 2].reshape(4 * cw, -1)
                    t = kd * 9 + kh * 3
                    rhs = jnp.concatenate([upw[t], upw[t + 1], upw[t + 2]], axis=1)
                    part = dot(lhs, rhs)
                    total = part if total is None else total + part
            even = total[:, cu : 2 * cu]
            odd = total[:, 2 * cu :] + shift_rows(total[:, :cu], -1, cw)
            for i in range(2):
                for j in range(2):
                    at = (i * 2 + j) * cw
                    fd, fh = 2 * i + 1 - gd, 2 * j + 1 - gh
                    up32[fd, fh, pl.ds(0, cw, stride=2), :] = even[at : at + cw]
                    up32[fd, fh, pl.ds(1, cw, stride=2), :] = odd[at : at + cw]
    for fd in range(4):
        for fh in range(4):
            inside = None
            for pos, f, count in ((d, fd, nd), (h, fh, nh)):
                cond = None
                if f == 0:
                    cond = pos > 0
                if f == 3:
                    cond = pos < count - 1
                if cond is not None:
                    inside = cond if inside is None else jnp.logical_and(inside, cond)
            value = up32[fd, fh]
            if inside is not None:
                value = jnp.where(inside, value, 0.0)
            joined[fd, fh, :, 0:cu] = value.astype(BF16)

    own_skip.wait()
    skip_halo.wait_recv()
    weights[1].wait()
    cells = 4 * 2 * cw

    def conv(field, weight):
        chans = field.shape[3]
        lhs = jnp.concatenate(
            [field[a : a + 2, b : b + 2].reshape(cells, chans) for a, b in GRID9], axis=1
        )
        rhs = jnp.concatenate(
            [
                jnp.concatenate([weight[(a * 3 + b) * 3 + c] for c in range(3)], axis=1)
                for a, b in GRID9
            ],
            axis=0,
        )
        y = dot(lhs, rhs)
        n = weight.shape[2]
        return shift_rows(y[:, :n], 1, 2 * cw) + y[:, n : 2 * n] + shift_rows(y[:, 2 * n :], -1, 2 * cw)

    def conv_back(field, weight):
        chans = field.shape[3]
        lhs = jnp.concatenate(
            [field[2 - a : 4 - a, 2 - b : 4 - b].reshape(cells, chans) for a, b in GRID9], axis=1
        )
        rhs = jnp.concatenate(
            [
                jnp.concatenate([weight[(a * 3 + b) * 3 + c] for a, b in GRID9], axis=1)
                for c in range(3)
            ],
            axis=0,
        )
        y = dot(lhs, rhs, NT)
        n = weight.shape[1]
        return shift_rows(y[:, :n], -1, 2 * cw) + y[:, n : 2 * n] + shift_rows(y[:, 2 * n :], 1, 2 * cw)

    first_pre = conv(joined, w1)
    fp[...] = first_pre
    hidden = (first_pre * jax.nn.sigmoid(first_pre)).astype(BF16)
    hid[1:3, 1:3] = hidden.reshape(2, 2, 2 * cw, cu)
    hid_halo = field_halo(2, hid)
    hid_halo.start()
    hg[pair] = hidden
    ug[pair] = joined[1:3, 1:3, :, 0:cu].reshape(cells, cu)
    up_out = line_p(4, lambda p: ug.at[pair], ug)
    up_out.start()

    weights[2].wait()
    weights[3].wait()
    hid_halo.wait_recv()
    second_pre = conv(hid, w2)
    result[...] = (second_pre * jax.nn.sigmoid(second_pre)).astype(BF16).reshape(2, 2, 2 * cw, cu)
    err2 = (cot[...].reshape(cells, cu).astype(F32) * slope(second_pre)).astype(BF16)
    e2[1:3, 1:3] = err2.reshape(2, 2, 2 * cw, cu)
    out_result = pltpu.make_async_copy(result, result_hbm, loc.at[7])
    out_result.start()
    e2_halo = field_halo(3, e2)
    e2_halo.start()
    hid_out = line_p(3, lambda p: hg.at[pair], hg)
    hid_out.start()

    def part_of(p):
        return pl.ds(pl.multiple_of(p * both, both), both)

    def flip(value, phase, out, into):
        out[...] = value.astype(F32).T.astype(BF16)
        into[pair] = out[part_of(pair)]
        spread = line_p(phase, lambda p: out.at[part_of(p)], into)
        spread.start()
        return spread

    def weight_grad(into, gathered, acc):
        acc[...] = jnp.zeros_like(acc)
        half = 2 * cw
        per_plane = 4 * half
        lane = lax.broadcasted_iota(jnp.int32, (both, 128), 1)

        def step(j, carry):
            shifted = []
            for plane in range(4):
                at = plane * per_plane
                low = into[j, :, at : at + 128].astype(F32)
                high = into[j, :, at + 128 : at + 256].astype(F32)
                mid = jnp.where(lane < half, pltpu.roll(low, half, 1), pltpu.roll(high, half, 1))
                shifted.append(
                    [
                        rows if kw == 1 else shift_lanes(rows, kw - 1, half)
                        for rows in (high, mid, low)
                        for kw in range(3)
                    ]
                )
            lhs = []
            for c in range(2):
                for kd in range(3):
                    for k in range(9):
                        pieces = [shifted[2 - kd + q][k][c * no : (c + 1) * no] for q in range(2)]
                        lhs.append(jnp.concatenate(pieces, axis=1))
            acc[...] += dot(jnp.concatenate(lhs, axis=0).astype(BF16), gathered(j))
            return carry

        lax.fori_loop(0, npair, step, 0)
        return acc[...]

    def swap(phase, value, out, into):
        half = 27 * no
        halves = [value[:half], value[half:]]
        mine = jnp.where(core == 0, halves[0], halves[1])
        out[...] = jnp.where(core == 0, halves[1], halves[0])
        copy = single(phase, out, into, (partner, h), into)
        copy.start()
        return copy, mine

    def flipped(value):
        rows, lanes = value.shape
        tall, wide = round_up(rows, 128), round_up(lanes, 128)
        if tall > rows:
            value = jnp.concatenate([value, jnp.zeros((tall - rows, lanes), F32)], axis=0)
        if wide > lanes:
            value = jnp.concatenate([value, jnp.zeros((tall, wide - lanes), F32)], axis=1)
        return value.T

    first_taps = 14
    split = first_taps * no
    lanes = round_up(split, 128)

    def scatter_rows(phase, swapped, arriving, chunk, out, into, folded=True, beside=None):
        copy, mine = swapped
        copy.wait_recv()
        turned = flipped((mine + arriving[...]) * factor)
        for c in range(nh):
            piece = turned[c * chunk : (c + 1) * chunk]
            if folded:
                piece = jnp.concatenate([piece[:, :lanes], piece[:, split : split + lanes]], axis=0)
            if beside:
                piece = jnp.concatenate([piece, beside[c]], axis=0)
            fill = out.shape[1] - piece.shape[0]
            if fill:
                piece = jnp.concatenate([piece, jnp.zeros((fill, piece.shape[1]), F32)], axis=0)
            out[c] = piece.astype(BF16)
        into[h] = out[h]
        spread = line_h(phase, lambda p: out.at[p], into)
        spread.start()
        return spread

    e2_halo.wait_recv()
    err1 = (conv_back(e2, w2) * slope(fp[...])).astype(BF16)
    e1[1:3, 1:3] = err1.reshape(2, 2, 2 * cw, cu)
    e1_halo = field_halo(4, e1)
    e1_halo.start()
    e2_out = flip(e2[...].reshape(4 * cells, cu), 5, et2s, et2r)

    e1_halo.wait_recv()
    e1_out = flip(e1[...].reshape(4 * cells, cu), 8, et1s, et1r)
    back = conv_back(e1, w1)
    bu32[...] = back[:, :cu].reshape(2, 2, 2 * cw, cu)
    for i in range(2):
        for j in range(2):
            for par in range(2):
                bu[1 + i, 1 + j, par] = bu32[i, j, pl.ds(par, cw, stride=2), :].astype(BF16)
    bu_halo = halo(
        5,
        lambda dd, dh: (
            bu.at[pl.ds(2, 1) if dd else pl.ds(1, 2), pl.ds(2, 1) if dh else pl.ds(1, 2)],
            bu.at[pl.ds(0, 1) if dd else pl.ds(1, 2), pl.ds(0, 1) if dh else pl.ds(1, 2)],
        ),
        [(1, 0), (0, 1), (1, 1)],
    )
    bu_halo.start()
    bu_out = flip(bu[1:3, 1:3].reshape(cells, cu), 7, buts, butr)
    e2_out.wait_recv()
    hid_out.wait_recv()
    swap2 = swap(9, weight_grad(et2r, lambda j: hg[j], acc2), px2, pr2)
    planes_out.wait_recv()
    planes_swap = single(
        16, bg.at[core, pl.ds(0, npair)], bg.at[core, pl.ds(0, npair)], (partner, h), bg.at[1 - core, pl.ds(0, npair)]
    )
    planes_swap.start()

    e1_out.wait_recv()
    up_out.wait_recv()
    skip_out.wait_recv()
    swap1 = swap(13, weight_grad(et1r, lambda j: jnp.concatenate([ug[j], sg[j].reshape(cells, cu)], axis=1), acc1), px1, pr1)

    g2_out = scatter_rows(11, swap2, pr2, cu // nh, gs2, gr2)

    bu_out.wait_recv()
    per = 128 // cw
    span = npair * cw
    group = min(per, npair)
    lane = lax.broadcasted_iota(jnp.int32, (both, 128), 1) // cw
    phases = {}
    for pd in range(2):
        for p in range(per):
            groups = []
            for g in range(npair // group):
                total = None
                for s in range(group):
                    piece = butr[g * group + s, :, pd * 128 : (pd + 1) * 128].astype(F32)
                    turn = ((s - p) * cw) % 128
                    piece = pltpu.roll(piece, turn, 1) if turn else piece
                    total = piece if total is None else jnp.where(lane == s, piece, total)
                groups.append(total)
            value = jnp.concatenate(groups, axis=1) if len(groups) > 1 else groups[0]
            phases[pd, p // 2, p % 2] = value[:, :span]

    def tap_rows(kd, kh, kw):
        pw, sw = PARITY_SHIFT[kw]
        value = phases[PARITY_SHIFT[kd][0], PARITY_SHIFT[kh][0], pw]
        return shift_lanes(value, 1, cw) if sw else value

    planes_swap.wait_recv()
    products = {}
    for sd, kds in ((0, (1, 2)), (1, (0,))):
        for sh, khs in ((0, (1, 2)), (1, (0,))):
            order = [(kd, kh, kw) for kd in kds for kh in khs for kw in range(3)]
            lhs = jnp.concatenate([tap_rows(*k) for k in order], axis=0).astype(BF16)
            odd_one = lax.rem(core + sd, 2)
            first = core * sd
            rhs = bg[odd_one, pl.ds(first, npair), sh].reshape(span, -1)
            value = dot(lhs, rhs)
            for i, k in enumerate(order):
                for c in range(2):
                    at = (i * 2 + c) * no
                    products[(c,) + k] = value[at : at + no]
    grad_up = jnp.concatenate(
        [products[c, a, b, e] for c in range(2) for a, b in GRID9 for e in range(3)], axis=0
    )
    swapu = swap(12, grad_up, pxu, pru)

    g1_out = scatter_rows(15, swap1, pr1, 2 * cu // nh, gs1, gr1, folded=False)
    bu_halo.wait_recv()
    around = lambda par: [bu[a, b, par].reshape(cw, cu) for a, b in GRID9]
    lhs = jnp.concatenate(around(0) + around(1), axis=1)
    rhs = jnp.concatenate(
        [upw[(a * 3 + b) * 3 + 1] for a, b in GRID9] + [upw[(a * 3 + b) * 3 + 2] for a, b in GRID9], axis=1
    )
    same = dot(lhs, rhs, NT)
    lhs = jnp.concatenate(around(1), axis=1)
    rhs = jnp.concatenate([upw[(a * 3 + b) * 3] for a, b in GRID9], axis=1)
    block_grad = flipped(same + shift_rows(dot(lhs, rhs, NT), 1, cw))
    share = cb // (128 // cw)
    beside = []
    for c in range(nh):
        groups = [block_grad[c * cb + q : c * cb + q + share, :cw] for q in range(0, cb, share)]
        beside.append(jnp.concatenate(groups, axis=1))
    gu_out = scatter_rows(14, swapu, pru, cb, gsu, gru, beside=beside)
    gskip[...] = back[:, cu:].astype(BF16).reshape(2, 2, 2 * cw, cu)
    out_gskip = pltpu.make_async_copy(gskip, gskip_hbm, loc.at[8])
    out_gskip.start()

    def finish(spread, into, out, hbm, at):
        spread.wait_recv()
        total = into[0].astype(F32)
        for s in range(1, nh):
            total = total + into[s].astype(F32)
        out[...] = total[: out.shape[0]]
        copy = pltpu.make_async_copy(out, hbm, loc.at[at])
        copy.start()
        return copy

    finished = [finish(g2_out, gr2, sumsecond, sumsecond_hbm, 9), finish(g1_out, gr1, sumfirst, sumfirst_hbm, 12)]
    sent = len(log) - 1
    for part in log[:sent]:
        part.wait_send()
    finished.append(finish(gu_out, gru, sumup, sumup_hbm, 11))
    base = 2 * cb // 16 * 16
    for s in range(nh):
        cgr[s] = gru[s, base : gru.shape[1]].astype(F32)[2 * cb - base : 2 * cb - base + cgr.shape[1]]
    out_cg = pltpu.make_async_copy(cgr, cgrows, loc.at[10])
    out_cg.start()
    for copy in finished + [out_cg, out_result, out_gskip]:
        copy.wait()

    for part in log[sent:]:
        if not part.arrived:
            part.wait_recv()
        part.wait_send()


def tall_turn(value):
    rows = value.shape[0]
    if rows < 128:
        value = jnp.concatenate([value, jnp.zeros((128 - rows, value.shape[1]), F32)], axis=0)
    return value.T


def closing(nh, *refs):
    (result, gskip, *left), (out0, out1h, out2, *grads), (cgrows, sumup, sumfirst, sumsecond) = (
        refs[:6], refs[6:12], refs[12:16]
    )
    out1, out3, out4, out5, pass0, pass1, sems = refs[16:]
    stages = (cgrows, sumup, sumfirst, sumsecond)
    into = [pltpu.make_async_copy(src, dst, sems.at[i]) for i, (src, dst) in enumerate(zip(left, stages))]
    through = [pltpu.make_async_copy(result, pass0, sems.at[4]), pltpu.make_async_copy(gskip, pass1, sems.at[5])]
    whole = [pltpu.make_async_copy(pass0, out0, sems.at[10]), pltpu.make_async_copy(pass1, out2, sems.at[11])]
    for copy in into + through:
        copy.start()
    cb, rows, cw = out1.shape
    tall = cgrows.shape[0] // nh
    per = 128 // cw
    share = cb // per
    away = [
        pltpu.make_async_copy(src, dst, sems.at[6 + i])
        for i, (src, dst) in enumerate(zip((out1, out3, out4, out5), [out1h] + grads))
    ]
    into[0].wait()
    for i in range(share):
        line = cgrows[pl.ds(i, nh, stride=tall), :].astype(BF16)
        for q in range(per):
            out1[q * share + i] = line[:, q * cw : (q + 1) * cw]
    away[0].start()
    for arriving, leaving in zip(through, whole):
        arriving.wait()
        leaving.start()
    no = out3.shape[1]
    into[2].wait()
    n = out4.shape[2]
    out4[...] = tall_turn(sumfirst[...])[: 27 * no, :n].reshape(27, no, n)
    away[2].start()
    into[1].wait()
    n = out3.shape[2]
    turned = tall_turn(sumup[...])
    out3[:14] = turned[: 14 * no, :n].reshape(14, no, n)
    out3[14:] = turned[: 13 * no, n : 2 * n].reshape(13, no, n)
    away[1].start()
    into[3].wait()
    total = sumsecond[...]
    n = out5.shape[1]
    for t in range(27):
        row, at = (0, t) if t < 14 else (n, t - 14)
        out5[t] = total[row : row + n, at * no : (at + 1) * no]
    away[3].start()
    for copy in whole + away:
        copy.wait()


def per_device(nd, nh, bottom, skip, upconv_kernel, w_first, w_second, cotangent):
    cb, cw = bottom.shape[3], bottom.shape[2]
    cin, cu = upconv_kernel.shape[3:]
    fw = skip.shape[2]
    cj = w_first.shape[3]
    no = cu // nd
    both, npair = 2 * no, nd // 2
    rows = skip.shape[:2]
    factor = 1.0 / math.sqrt(rows[0] * nd * rows[1] * nh * fw)
    taps = round_up(27 * no, 128)
    ncj, nch = cj // nh, cu // nh
    v = pltpu.VMEM
    upw = upconv_kernel.reshape(27, cin, cu)
    w1 = w_first.reshape(27, cj, cu)
    w2 = w_second.reshape(27, cu, cu)
    cells = rows[0] * rows[1] * fw
    wide = round_up(cin, 128)
    part = 27 * no
    tall = round_up(cb * cw // 128, 8)
    lanes = round_up(14 * no, 128)
    scratch = [
        v((cb, nh, cw), BF16), v(skip.shape, BF16), v(skip.shape, BF16),
        v((2 * cb, lanes), F32), v((round_up(ncj, 8), taps), F32), v((2 * nch, lanes), F32),
        v(upw.shape, BF16), v(w1.shape, BF16), v(w2.shape, BF16), v(cotangent.shape, BF16),
        v((cb * nh, cw), F32),
        v((nh, round_up(cb, 16), 128), BF16), v((nh, round_up(cb, 16), 128), BF16),
        v((3, 3, cw, wide), BF16),
        v((2, npair + 1, 2, cw, wide), BF16),
        v((4, 4, fw, cu), F32),
        v((4, 4, fw, cj), BF16),
        v((npair, cells, cu), BF16),
        v((npair,) + skip.shape, BF16),
        v((cells, cu), F32),
        v((4, 4, fw, cu), BF16),
        v((npair, cells, cu), BF16),
        v((4, 4, fw, cu), BF16),
        v((4, 4, fw, cu), BF16),
        v((cu, 4 * cells), BF16), v((npair, both, 4 * cells), BF16),
        v((cu, 4 * cells), BF16), v((npair, both, 4 * cells), BF16),
        v((2, 2, fw, cu), F32),
        v((3, 3, 2, cw, cu), BF16),
        v((cu, cells), BF16), v((npair, both, cells), BF16),
        v((nh, tall, 128), F32),
        v((2 * part, cj), F32), v((2 * part, cu), F32),
        v((part, cu), F32), v((part, cu), F32),
        v((part, cj), F32), v((part, cj), F32),
        v((part, wide), F32), v((part, wide), F32),
        v((nh, round_up(2 * nch, 16), lanes), BF16), v((nh, round_up(2 * nch, 16), lanes), BF16),
        v((nh, round_up(ncj, 16), taps), BF16), v((nh, round_up(ncj, 16), taps), BF16),
        v((nh, round_up(2 * cb + tall, 16), lanes), BF16), v((nh, round_up(2 * cb + tall, 16), lanes), BF16),
        pltpu.SemaphoreType.DMA((18,)), pltpu.SemaphoreType.DMA((18,)),
        pltpu.SemaphoreType.DMA((6, 9)), pltpu.SemaphoreType.DMA((6, 9)),
        pltpu.SemaphoreType.DMA((13,)),
    ]
    shape = jax.ShapeDtypeStruct
    anywhere = pl.BlockSpec(memory_space=pl.ANY)
    tops = [
        shape((nh, tall, 128), F32),
        shape((2 * cb, lanes), F32),
        shape((round_up(ncj, 8), taps), F32),
        shape((2 * nch, lanes), F32),
    ]
    left = pl.pallas_call(
        functools.partial(body, nd, nh, factor),
        out_shape=[shape(skip.shape, BF16), shape(skip.shape, BF16)] + tops,
        in_specs=[anywhere] * 6,
        out_specs=[anywhere] * 6,
        scratch_shapes=scratch,
        compiler_params=pltpu.CompilerParams(
            collective_id=0, has_side_effects=True, vmem_limit_bytes=56 * 1024 * 1024
        ),
        name="decoder",
    )(bottom[0].transpose(2, 0, 1), skip, upw, w1, w2, cotangent)
    tops[0] = shape((nh * tall, 128), F32)
    ends = [shape((cb, nh, cw), BF16), shape((27, no, cb), F32), shape((27, no, ncj), F32), shape((27, nch, no), F32)]
    outs = pl.pallas_call(
        functools.partial(closing, nh),
        out_shape=[shape(skip.shape, BF16), ends[0], shape(skip.shape, BF16)] + ends[1:],
        in_specs=[anywhere] * 6,
        out_specs=[anywhere] * 6,
        scratch_shapes=[v(one.shape, one.dtype) for one in tops + ends]
        + [v(skip.shape, BF16), v(skip.shape, BF16), pltpu.SemaphoreType.DMA((12,))],
        name="closing",
    )(*left[:2], left[2].reshape(nh * tall, 128), *left[3:])
    return (
        outs[0],
        outs[1].transpose(1, 2, 0)[None],
        outs[2],
        outs[3].reshape(3, 3, 3, no, cb).transpose(0, 1, 2, 4, 3),
        outs[4].reshape(3, 3, 3, no, ncj).transpose(0, 1, 2, 4, 3),
        outs[5].reshape(3, 3, 3, nch, no),
    )


def solution(mesh):
    return jax.shard_map(
        functools.partial(per_device, mesh.shape["depth"], mesh.shape["height"]),
        mesh=mesh,
        in_specs=(
            P("depth", None, None, "height"),
            P("depth", "height", None, None),
            P(),
            P(),
            P(),
            P("depth", "height", None, None),
        ),
        out_specs=(
            P("depth", "height", None, None),
            P("depth", None, None, "height"),
            P("depth", "height", None, None),
            P(None, None, None, "height", "depth"),
            P(None, None, None, "height", "depth"),
            P(None, None, None, "height", "depth"),
        ),
        check_vma=False,
    )
```

```python
import functools
import math

import jax
import jax.numpy as jnp
from jax import lax
from jax.experimental import pallas as pl
from jax.experimental.pallas import tpu as pltpu
from jax.sharding import PartitionSpec as P

MESH = pl.DeviceIdType.MESH
F32 = jnp.float32
BF16 = jnp.bfloat16
GRID9 = [(a, b) for a in range(3) for b in range(3)]
OTHERS = [(a, b) for a in (-1, 0, 1) for b in (-1, 0, 1) if (a, b) != (0, 0)]
NT = (((1,), (1,)), ((), ()))
PARITY_SHIFT = {0: (1, 1), 1: (0, 0), 2: (1, 0)}


def round_up(value, unit):
    return -(-value // unit) * unit


def remote(src, dst, send, recv, target):
    return pltpu.make_async_remote_copy(
        src_ref=src, dst_ref=dst, send_sem=send, recv_sem=recv, device_id=target, device_id_type=MESH
    )


class Spread:
    def __init__(self, log, me, count, target, source, slot, bulk, send, recv):
        self.me, self.count, self.target = me, count, target
        self.source, self.slot, self.bulk, self.send, self.recv = source, slot, bulk, send, recv
        self.arrived, self.log = False, log

    def start(self):
        self.log.append(self)

        def step(j, carry):
            peer = lax.rem(self.me + j, self.count)
            remote(self.source(peer), self.slot(self.me), self.send, self.recv, self.target(peer)).start()
            return carry

        lax.fori_loop(1, self.count, step, 0)

    def whole(self):
        peer = lax.rem(self.me + 1, self.count)
        return remote(self.bulk, self.bulk, self.send, self.recv, self.target(peer))

    def wait_recv(self):
        self.arrived = True
        self.whole().wait_recv()

    def wait_send(self):
        self.whole().wait_send()


class Single:
    def __init__(self, log, out, into):
        self.out, self.into = out, into
        self.arrived, self.log = False, log

    def start(self):
        self.log.append(self)
        self.out.start()

    def wait_recv(self):
        self.arrived = True
        self.into.wait_recv()

    def wait_send(self):
        self.out.wait_send()


class Halo:
    def __init__(self, log, there, copy, directions):
        self.there, self.copy, self.directions = there, copy, directions
        self.arrived, self.log = False, log

    def each(self, sign, act):
        for dd, dh in self.directions:
            @pl.when(self.there(sign * dd, sign * dh))
            def _(dd=dd, dh=dh):
                act(self.copy(dd, dh))

    def start(self):
        self.log.append(self)
        self.each(1, lambda copy: copy.start())

    def wait_recv(self):
        self.arrived = True
        self.each(-1, lambda copy: copy.wait_recv())

    def wait_send(self):
        self.each(1, lambda copy: copy.wait_send())


def shift_rows(value, by, period):
    rows = value.shape[0]
    row = lax.broadcasted_iota(jnp.int32, value.shape, 0) % period
    edge = 0 if by > 0 else period - 1
    return jnp.where(row == edge, 0.0, pltpu.roll(value, by % rows, 0))


def shift_lanes(value, by, period):
    lanes = value.shape[1]
    lane = lax.broadcasted_iota(jnp.int32, value.shape, 1) % period
    edge = 0 if by > 0 else period - 1
    return jnp.where(lane == edge, 0.0, pltpu.roll(value, by % lanes, 1))


def slope(values):
    sig = jax.nn.sigmoid(values)
    return sig * (1.0 + values * (1.0 - sig))


def dot(a, b, dims=(((1,), (0,)), ((), ()))):
    return lax.dot_general(a, b, dims, preferred_element_type=F32)


def body(
    nd, nh, factor,
    bottom_hbm, skip, upw_hbm, w1_hbm, w2_hbm, cot_hbm,
    result_hbm, gskip_hbm, cgrows, sumup_hbm, sumfirst_hbm, sumsecond_hbm,
    bottom, result, gskip, sumup, sumfirst, sumsecond, upw, w1, w2, cot, bott, bsend, brecv, near, bg, up32, joined, ug32, ug, sg, fp, hid, hg, e2, e1, et2s, et2r, et1s, et1r,
    bu32, bu, buts, butr, cgr, acc1, acc2, px2, pr2, px1, pr1, pxu, pru, gs2, gr2, gs1, gr1, gsu, gru,
    ssem, rsem, hs, hr, loc,
):
    d = lax.axis_index("depth")
    h = lax.axis_index("height")
    pair, core = d // 2, lax.rem(d, 2)
    partner = d + 1 - 2 * core
    npair = nd // 2
    cb, rows_all, cw = bottom.shape
    cu = upw.shape[2]
    cin = upw.shape[1]
    no = cu // nd
    both = 2 * no

    weights = [
        pltpu.make_async_copy(upw_hbm, upw, loc.at[0]),
        pltpu.make_async_copy(w1_hbm, w1, loc.at[1]),
        pltpu.make_async_copy(w2_hbm, w2, loc.at[2]),
        pltpu.make_async_copy(cot_hbm, cot, loc.at[3]),
    ]
    own_skip = pltpu.make_async_copy(skip, joined.at[pl.ds(1, 2), pl.ds(1, 2), :, pl.ds(cu, cu)], loc.at[4])
    own_gathered = pltpu.make_async_copy(skip, sg.at[pair], loc.at[6])

    own_bottom = pltpu.make_async_copy(bottom_hbm, bottom, loc.at[5])
    own_bottom.start()
    for copy in weights:
        copy.start()
    joined[...] = jnp.zeros_like(joined)
    own_skip.start()
    own_gathered.start()
    hid[...] = jnp.zeros_like(hid)
    e2[...] = jnp.zeros_like(e2)
    e1[...] = jnp.zeros_like(e1)
    bu[...] = jnp.zeros_like(bu)


    barrier = pltpu.get_barrier_semaphore()

    def greet_line(count, target):
        def step(j, carry):
            pl.semaphore_signal(barrier, inc=1, device_id=target(j), device_id_type=MESH)
            return carry

        lax.fori_loop(1, count, step, 0)

    greet_line(nh, lambda j: (d, lax.rem(h + j, nh)))
    greet_line(npair, lambda j: (2 * lax.rem(pair + j, npair) + core, h))

    def there(dd, dh):
        ok = None
        for pos, step, count in ((d, dd, nd), (h, dh, nh)):
            if step:
                cond = pos > 0 if step < 0 else pos < count - 1
                ok = cond if ok is None else jnp.logical_and(ok, cond)
        return ok

    for dd in (-1, 1):
        for dh in (-1, 0, 1):
            target = (lax.rem(d + dd + nd, nd), lax.rem(h + dh + nh, nh))
            pl.semaphore_signal(barrier, inc=1, device_id=target, device_id_type=MESH)

    own_bottom.wait()
    bott[...] = bottom[...].astype(F32).reshape(cb * rows_all, cw)
    lines = [bott[pl.ds(r, cb, stride=rows_all), :] for r in range(rows_all)]
    blank = jnp.zeros((cb, cw), F32)
    rest = jnp.zeros((cb, 128 - 3 * cw), F32)
    pad = jnp.zeros((bsend.shape[1] - cb, 128), F32)
    for p in range(nh):
        before = lines[p - 1] if p > 0 else blank
        after = lines[p + 1] if p < nh - 1 else blank
        window = jnp.concatenate([before, lines[p], after, rest], axis=1)
        bsend[p] = jnp.concatenate([window, pad], axis=0).astype(BF16)
    brecv[h] = bsend[h]
    pl.semaphore_wait(barrier, nh + npair + 4)

    def src_part(step):
        return {0: pl.ds(1, 2), 1: pl.ds(2, 1), -1: pl.ds(1, 1)}[step]

    def own_part(step):
        return {0: pl.ds(0, 2), 1: pl.ds(1, 1), -1: pl.ds(0, 1)}[step]

    def dst_part(step):
        return {0: pl.ds(1, 2), 1: pl.ds(0, 1), -1: pl.ds(3, 1)}[step]

    log = []

    def halo(phase, copy_of, directions=OTHERS):
        def copy(dd, dh):
            slot = (dd + 1) * 3 + dh + 1
            src, dst = copy_of(dd, dh)
            return remote(src, dst, hs.at[phase, slot], hr.at[phase, slot], (d + dd, h + dh))

        return Halo(log, there, copy, directions)

    def field_halo(phase, field):
        return halo(
            phase,
            lambda dd, dh: (
                field.at[src_part(dd), src_part(dh)],
                field.at[dst_part(dd), dst_part(dh)],
            ),
        )

    def line_h(phase, source, into):
        return Spread(
            log, h, nh, lambda p: (d, p), source, lambda s: into.at[s], into.at[pl.ds(0, nh - 1)],
            ssem.at[phase], rsem.at[phase],
        )

    def line_p(phase, source, into):
        return Spread(
            log, pair, npair, lambda p: (2 * p + core, h), source, lambda s: into.at[s],
            into.at[pl.ds(0, npair - 1)], ssem.at[phase], rsem.at[phase],
        )

    def single(phase, src, dst, target, arriving):
        sems = ssem.at[phase], rsem.at[phase]
        return Single(log, remote(src, dst, *sems, target), remote(src, arriving, *sems, target))

    rows_out = line_h(0, lambda p: bsend.at[p], brecv)
    rows_out.start()
    skip_halo = halo(
        0,
        lambda dd, dh: (
            skip.at[own_part(dd), own_part(dh)],
            joined.at[dst_part(dd), dst_part(dh), :, pl.ds(cu, cu)],
        ),
    )
    skip_halo.start()
    skip_out = line_p(17, lambda p: sg.at[pair], sg)
    own_gathered.wait()
    skip_out.start()
    rows_out.wait_recv()
    stack = [brecv[c].astype(F32)[:cb] for c in range(nh)]
    wide = near.shape[3]
    if wide > cin:
        stack.append(jnp.zeros((wide - cin, 128), F32))
    near[1] = jnp.concatenate(stack, axis=0).T[: 3 * cw].reshape(3, cw, wide).astype(BF16)

    plane_next = single(1, near.at[1], near.at[0], (lax.rem(d + 1, nd), h), near.at[0])
    plane_prev = single(2, near.at[1], near.at[2], (lax.rem(d + nd - 1, nd), h), near.at[2])
    plane_next.start()
    plane_prev.start()
    bg[core, pair] = near[1, 1:3]
    bg[0, npair] = jnp.zeros_like(near[1, 1:3])
    planes_out = line_p(6, lambda p: bg.at[core, pair], bg.at[core])
    planes_out.start()
    weights[0].wait()
    plane_next.wait_recv()
    plane_prev.wait_recv()

    coarse = []
    for s in range(3):
        plane = d - 1 + s
        here = jnp.logical_and(plane >= 0, plane < nd)
        value = near[s, :, :, 0:cin]
        coarse.append(jnp.where(here, value, jnp.zeros_like(value)))
    coarse = jnp.stack(coarse)
    first_of = {0: 1, 1: 1, 2: 0}
    for gd in range(2):
        for gh in range(2):
            total = None
            for kd in ((1,), (0, 2))[gd]:
                for kh in ((1,), (0, 2))[gh]:
                    a, b = first_of[kd], first_of[kh]
                    lhs = coarse[a : a + 2, b : b + 2].reshape(4 * cw, -1)
                    t = kd * 9 + kh * 3
                    rhs = jnp.concatenate([upw[t], upw[t + 1], upw[t + 2]], axis=1)
                    part = dot(lhs, rhs)
                    total = part if total is None else total + part
            even = total[:, cu : 2 * cu]
            odd = total[:, 2 * cu :] + shift_rows(total[:, :cu], -1, cw)
            for i in range(2):
                for j in range(2):
                    at = (i * 2 + j) * cw
                    fd, fh = 2 * i + 1 - gd, 2 * j + 1 - gh
                    up32[fd, fh, pl.ds(0, cw, stride=2), :] = even[at : at + cw]
                    up32[fd, fh, pl.ds(1, cw, stride=2), :] = odd[at : at + cw]
    for fd in range(4):
        for fh in range(4):
            inside = None
            for pos, f, count in ((d, fd, nd), (h, fh, nh)):
                cond = None
                if f == 0:
                    cond = pos > 0
                if f == 3:
                    cond = pos < count - 1
                if cond is not None:
                    inside = cond if inside is None else jnp.logical_and(inside, cond)
            value = up32[fd, fh]
            if inside is not None:
                value = jnp.where(inside, value, 0.0)
            joined[fd, fh, :, 0:cu] = value.astype(BF16)

    own_skip.wait()
    skip_halo.wait_recv()
    weights[1].wait()
    cells = 4 * 2 * cw

    def conv(field, weight):
        chans = field.shape[3]
        lhs = jnp.concatenate(
            [field[a : a + 2, b : b + 2].reshape(cells, chans) for a, b in GRID9], axis=1
        )
        rhs = jnp.concatenate(
            [
                jnp.concatenate([weight[(a * 3 + b) * 3 + c] for c in range(3)], axis=1)
                for a, b in GRID9
            ],
            axis=0,
        )
        y = dot(lhs, rhs)
        n = weight.shape[2]
        return shift_rows(y[:, :n], 1, 2 * cw) + y[:, n : 2 * n] + shift_rows(y[:, 2 * n :], -1, 2 * cw)

    def conv_back(field, weight):
        chans = field.shape[3]
        lhs = jnp.concatenate(
            [field[2 - a : 4 - a, 2 - b : 4 - b].reshape(cells, chans) for a, b in GRID9], axis=1
        )
        rhs = jnp.concatenate(
            [
                jnp.concatenate([weight[(a * 3 + b) * 3 + c] for a, b in GRID9], axis=1)
                for c in range(3)
            ],
            axis=0,
        )
        y = dot(lhs, rhs, NT)
        n = weight.shape[1]
        return shift_rows(y[:, :n], -1, 2 * cw) + y[:, n : 2 * n] + shift_rows(y[:, 2 * n :], 1, 2 * cw)

    first_pre = conv(joined, w1)
    fp[...] = first_pre
    hidden = (first_pre * jax.nn.sigmoid(first_pre)).astype(BF16)
    hid[1:3, 1:3] = hidden.reshape(2, 2, 2 * cw, cu)
    hid_halo = field_halo(2, hid)
    hid_halo.start()
    hg[pair] = hidden
    hid_out = line_p(3, lambda p: hg.at[pair], hg)
    hid_out.start()
    planes_out.wait_recv()
    planes_swap = single(
        16, bg.at[core, pl.ds(0, npair)], bg.at[core, pl.ds(0, npair)], (partner, h), bg.at[1 - core, pl.ds(0, npair)]
    )
    planes_swap.start()

    weights[2].wait()
    weights[3].wait()
    hid_halo.wait_recv()
    second_pre = conv(hid, w2)
    result[...] = (second_pre * jax.nn.sigmoid(second_pre)).astype(BF16).reshape(2, 2, 2 * cw, cu)
    err2 = (cot[...].reshape(cells, cu).astype(F32) * slope(second_pre)).astype(BF16)
    e2[1:3, 1:3] = err2.reshape(2, 2, 2 * cw, cu)
    out_result = pltpu.make_async_copy(result, result_hbm, loc.at[7])
    out_result.start()
    e2_halo = field_halo(3, e2)
    e2_halo.start()

    planes_swap.wait_recv()

    def planes_of(sd, sh):
        return bg[lax.rem(core + sd, 2), pl.ds(core * sd, npair), sh].reshape(npair * cw, wide)

    taps_of = (((1, 0),), ((2, 0), (0, 1)))
    for pd in range(2):
        for ph in range(2):
            total = None
            for kd, sd in taps_of[pd]:
                for kh, sh in taps_of[ph]:
                    t = kd * 9 + kh * 3
                    rhs = jnp.concatenate([upw[t], upw[t + 1], upw[t + 2]], axis=1)
                    part = dot(planes_of(sd, sh)[:, :cin], rhs)
                    total = part if total is None else total + part
            even = total[:, cu : 2 * cu]
            odd = total[:, 2 * cu :] + shift_rows(total[:, :cu], -1, cw)
            for k in range(npair):
                ug32[k, pd * 2 + ph, pl.ds(0, cw, stride=2), :] = even[k * cw : (k + 1) * cw]
                ug32[k, pd * 2 + ph, pl.ds(1, cw, stride=2), :] = odd[k * cw : (k + 1) * cw]
    ug[...] = ug32[...].astype(BF16).reshape(npair, cells, cu)

    def part_of(p):
        return pl.ds(pl.multiple_of(p * both, both), both)

    def flip(value, phase, out, into):
        out[...] = value.astype(F32).T.astype(BF16)
        into[pair] = out[part_of(pair)]
        spread = line_p(phase, lambda p: out.at[part_of(p)], into)
        spread.start()
        return spread

    def weight_grad(into, gathered, acc):
        acc[...] = jnp.zeros_like(acc)
        half = 2 * cw
        per_plane = 4 * half
        lane = lax.broadcasted_iota(jnp.int32, (both, 128), 1)

        def step(j, carry):
            shifted = []
            for plane in range(4):
                at = plane * per_plane
                low = into[j, :, at : at + 128].astype(F32)
                high = into[j, :, at + 128 : at + 256].astype(F32)
                mid = jnp.where(lane < half, pltpu.roll(low, half, 1), pltpu.roll(high, half, 1))
                shifted.append(
                    [
                        rows if kw == 1 else shift_lanes(rows, kw - 1, half)
                        for rows in (high, mid, low)
                        for kw in range(3)
                    ]
                )
            lhs = []
            for c in range(2):
                for kd in range(3):
                    for k in range(9):
                        pieces = [shifted[2 - kd + q][k][c * no : (c + 1) * no] for q in range(2)]
                        lhs.append(jnp.concatenate(pieces, axis=1))
            acc[...] += dot(jnp.concatenate(lhs, axis=0).astype(BF16), gathered(j))
            return carry

        lax.fori_loop(0, npair, step, 0)
        return acc[...]

    def swap(phase, value, out, into):
        half = 27 * no
        halves = [value[:half], value[half:]]
        mine = jnp.where(core == 0, halves[0], halves[1])
        out[...] = jnp.where(core == 0, halves[1], halves[0])
        copy = single(phase, out, into, (partner, h), into)
        copy.start()
        return copy, mine

    def flipped(value):
        rows, lanes = value.shape
        tall, wide = round_up(rows, 128), round_up(lanes, 128)
        if tall > rows:
            value = jnp.concatenate([value, jnp.zeros((tall - rows, lanes), F32)], axis=0)
        if wide > lanes:
            value = jnp.concatenate([value, jnp.zeros((tall, wide - lanes), F32)], axis=1)
        return value.T

    first_taps = 14
    split = first_taps * no
    lanes = round_up(split, 128)

    def scatter_rows(phase, swapped, arriving, chunk, out, into, folded=True, beside=None):
        copy, mine = swapped
        copy.wait_recv()
        turned = flipped((mine + arriving[...]) * factor)
        for c in range(nh):
            piece = turned[c * chunk : (c + 1) * chunk]
            if folded:
                piece = jnp.concatenate([piece[:, :lanes], piece[:, split : split + lanes]], axis=0)
            if beside:
                piece = jnp.concatenate([piece, beside[c]], axis=0)
            fill = out.shape[1] - piece.shape[0]
            if fill:
                piece = jnp.concatenate([piece, jnp.zeros((fill, piece.shape[1]), F32)], axis=0)
            out[c] = piece.astype(BF16)
        into[h] = out[h]
        spread = line_h(phase, lambda p: out.at[p], into)
        spread.start()
        return spread

    e2_halo.wait_recv()
    err1 = (conv_back(e2, w2) * slope(fp[...])).astype(BF16)
    e1[1:3, 1:3] = err1.reshape(2, 2, 2 * cw, cu)
    e1_halo = field_halo(4, e1)
    e1_halo.start()
    e2_out = flip(e2[...].reshape(4 * cells, cu), 5, et2s, et2r)

    e1_halo.wait_recv()
    e1_out = flip(e1[...].reshape(4 * cells, cu), 8, et1s, et1r)
    back = conv_back(e1, w1)
    bu32[...] = back[:, :cu].reshape(2, 2, 2 * cw, cu)
    for i in range(2):
        for j in range(2):
            for par in range(2):
                bu[1 + i, 1 + j, par] = bu32[i, j, pl.ds(par, cw, stride=2), :].astype(BF16)
    bu_halo = halo(
        5,
        lambda dd, dh: (
            bu.at[pl.ds(2, 1) if dd else pl.ds(1, 2), pl.ds(2, 1) if dh else pl.ds(1, 2)],
            bu.at[pl.ds(0, 1) if dd else pl.ds(1, 2), pl.ds(0, 1) if dh else pl.ds(1, 2)],
        ),
        [(1, 0), (0, 1), (1, 1)],
    )
    bu_halo.start()
    bu_out = flip(bu[1:3, 1:3].reshape(cells, cu), 7, buts, butr)
    e2_out.wait_recv()
    hid_out.wait_recv()
    swap2 = swap(9, weight_grad(et2r, lambda j: hg[j], acc2), px2, pr2)

    e1_out.wait_recv()
    skip_out.wait_recv()
    swap1 = swap(13, weight_grad(et1r, lambda j: jnp.concatenate([ug[j], sg[j].reshape(cells, cu)], axis=1), acc1), px1, pr1)

    g2_out = scatter_rows(11, swap2, pr2, cu // nh, gs2, gr2)

    bu_out.wait_recv()
    per = 128 // cw
    span = npair * cw
    group = min(per, npair)
    lane = lax.broadcasted_iota(jnp.int32, (both, 128), 1) // cw
    phases = {}
    for pd in range(2):
        for p in range(per):
            groups = []
            for g in range(npair // group):
                total = None
                for s in range(group):
                    piece = butr[g * group + s, :, pd * 128 : (pd + 1) * 128].astype(F32)
                    turn = ((s - p) * cw) % 128
                    piece = pltpu.roll(piece, turn, 1) if turn else piece
                    total = piece if total is None else jnp.where(lane == s, piece, total)
                groups.append(total)
            value = jnp.concatenate(groups, axis=1) if len(groups) > 1 else groups[0]
            phases[pd, p // 2, p % 2] = value[:, :span]

    def tap_rows(kd, kh, kw):
        pw, sw = PARITY_SHIFT[kw]
        value = phases[PARITY_SHIFT[kd][0], PARITY_SHIFT[kh][0], pw]
        return shift_lanes(value, 1, cw) if sw else value

    products = {}
    for sd, kds in ((0, (1, 2)), (1, (0,))):
        for sh, khs in ((0, (1, 2)), (1, (0,))):
            order = [(kd, kh, kw) for kd in kds for kh in khs for kw in range(3)]
            lhs = jnp.concatenate([tap_rows(*k) for k in order], axis=0).astype(BF16)
            rhs = planes_of(sd, sh)
            value = dot(lhs, rhs)
            for i, k in enumerate(order):
                for c in range(2):
                    at = (i * 2 + c) * no
                    products[(c,) + k] = value[at : at + no]
    grad_up = jnp.concatenate(
        [products[c, a, b, e] for c in range(2) for a, b in GRID9 for e in range(3)], axis=0
    )
    swapu = swap(12, grad_up, pxu, pru)

    g1_out = scatter_rows(15, swap1, pr1, 2 * cu // nh, gs1, gr1, folded=False)
    bu_halo.wait_recv()
    around = lambda par: [bu[a, b, par].reshape(cw, cu) for a, b in GRID9]
    lhs = jnp.concatenate(around(0) + around(1), axis=1)
    rhs = jnp.concatenate(
        [upw[(a * 3 + b) * 3 + 1] for a, b in GRID9] + [upw[(a * 3 + b) * 3 + 2] for a, b in GRID9], axis=1
    )
    same = dot(lhs, rhs, NT)
    lhs = jnp.concatenate(around(1), axis=1)
    rhs = jnp.concatenate([upw[(a * 3 + b) * 3] for a, b in GRID9], axis=1)
    block_grad = flipped(same + shift_rows(dot(lhs, rhs, NT), 1, cw))
    share = cb // (128 // cw)
    beside = []
    for c in range(nh):
        groups = [block_grad[c * cb + q : c * cb + q + share, :cw] for q in range(0, cb, share)]
        beside.append(jnp.concatenate(groups, axis=1))
    gu_out = scatter_rows(14, swapu, pru, cb, gsu, gru, beside=beside)
    gskip[...] = back[:, cu:].astype(BF16).reshape(2, 2, 2 * cw, cu)
    out_gskip = pltpu.make_async_copy(gskip, gskip_hbm, loc.at[8])
    out_gskip.start()

    def finish(spread, into, out, hbm, at):
        spread.wait_recv()
        total = into[0].astype(F32)
        for s in range(1, nh):
            total = total + into[s].astype(F32)
        out[...] = total[: out.shape[0]]
        copy = pltpu.make_async_copy(out, hbm, loc.at[at])
        copy.start()
        return copy

    finished = [finish(g2_out, gr2, sumsecond, sumsecond_hbm, 9), finish(g1_out, gr1, sumfirst, sumfirst_hbm, 12)]
    sent = len(log) - 1
    for part in log[:sent]:
        part.wait_send()
    finished.append(finish(gu_out, gru, sumup, sumup_hbm, 11))
    base = 2 * cb // 16 * 16
    for s in range(nh):
        cgr[s] = gru[s, base : gru.shape[1]].astype(F32)[2 * cb - base : 2 * cb - base + cgr.shape[1]]
    out_cg = pltpu.make_async_copy(cgr, cgrows, loc.at[10])
    out_cg.start()
    for copy in finished + [out_cg, out_result, out_gskip]:
        copy.wait()

    for part in log[sent:]:
        if not part.arrived:
            part.wait_recv()
        part.wait_send()


def tall_turn(value):
    rows = value.shape[0]
    if rows < 128:
        value = jnp.concatenate([value, jnp.zeros((128 - rows, value.shape[1]), F32)], axis=0)
    return value.T


def closing(nh, *refs):
    (result, gskip, *left), (out0, out1h, out2, *grads), (cgrows, sumup, sumfirst, sumsecond) = (
        refs[:6], refs[6:12], refs[12:16]
    )
    out1, out3, out4, out5, pass0, pass1, sems = refs[16:]
    stages = (cgrows, sumup, sumfirst, sumsecond)
    into = [pltpu.make_async_copy(src, dst, sems.at[i]) for i, (src, dst) in enumerate(zip(left, stages))]
    through = [pltpu.make_async_copy(result, pass0, sems.at[4]), pltpu.make_async_copy(gskip, pass1, sems.at[5])]
    whole = [pltpu.make_async_copy(pass0, out0, sems.at[10]), pltpu.make_async_copy(pass1, out2, sems.at[11])]
    for copy in into + through:
        copy.start()
    cb, rows, cw = out1.shape
    tall = cgrows.shape[0] // nh
    per = 128 // cw
    share = cb // per
    away = [
        pltpu.make_async_copy(src, dst, sems.at[6 + i])
        for i, (src, dst) in enumerate(zip((out1, out3, out4, out5), [out1h] + grads))
    ]
    into[0].wait()
    for i in range(share):
        line = cgrows[pl.ds(i, nh, stride=tall), :].astype(BF16)
        for q in range(per):
            out1[q * share + i] = line[:, q * cw : (q + 1) * cw]
    away[0].start()
    for arriving, leaving in zip(through, whole):
        arriving.wait()
        leaving.start()
    no = out3.shape[1]
    into[2].wait()
    n = out4.shape[2]
    out4[...] = tall_turn(sumfirst[...])[: 27 * no, :n].reshape(27, no, n)
    away[2].start()
    into[1].wait()
    n = out3.shape[2]
    turned = tall_turn(sumup[...])
    out3[:14] = turned[: 14 * no, :n].reshape(14, no, n)
    out3[14:] = turned[: 13 * no, n : 2 * n].reshape(13, no, n)
    away[1].start()
    into[3].wait()
    total = sumsecond[...]
    n = out5.shape[1]
    for t in range(27):
        row, at = (0, t) if t < 14 else (n, t - 14)
        out5[t] = total[row : row + n, at * no : (at + 1) * no]
    away[3].start()
    for copy in whole + away:
        copy.wait()


def per_device(nd, nh, bottom, skip, upconv_kernel, w_first, w_second, cotangent):
    cb, cw = bottom.shape[3], bottom.shape[2]
    cin, cu = upconv_kernel.shape[3:]
    fw = skip.shape[2]
    cj = w_first.shape[3]
    no = cu // nd
    both, npair = 2 * no, nd // 2
    rows = skip.shape[:2]
    factor = 1.0 / math.sqrt(rows[0] * nd * rows[1] * nh * fw)
    taps = round_up(27 * no, 128)
    ncj, nch = cj // nh, cu // nh
    v = pltpu.VMEM
    upw = upconv_kernel.reshape(27, cin, cu)
    w1 = w_first.reshape(27, cj, cu)
    w2 = w_second.reshape(27, cu, cu)
    cells = rows[0] * rows[1] * fw
    wide = round_up(cin, 128)
    part = 27 * no
    tall = round_up(cb * cw // 128, 8)
    lanes = round_up(14 * no, 128)
    scratch = [
        v((cb, nh, cw), BF16), v(skip.shape, BF16), v(skip.shape, BF16),
        v((2 * cb, lanes), F32), v((round_up(ncj, 8), taps), F32), v((2 * nch, lanes), F32),
        v(upw.shape, BF16), v(w1.shape, BF16), v(w2.shape, BF16), v(cotangent.shape, BF16),
        v((cb * nh, cw), F32),
        v((nh, round_up(cb, 16), 128), BF16), v((nh, round_up(cb, 16), 128), BF16),
        v((3, 3, cw, wide), BF16),
        v((2, npair + 1, 2, cw, wide), BF16),
        v((4, 4, fw, cu), F32),
        v((4, 4, fw, cj), BF16),
        v((npair, 4, fw, cu), F32),
        v((npair, cells, cu), BF16),
        v((npair,) + skip.shape, BF16),
        v((cells, cu), F32),
        v((4, 4, fw, cu), BF16),
        v((npair, cells, cu), BF16),
        v((4, 4, fw, cu), BF16),
        v((4, 4, fw, cu), BF16),
        v((cu, 4 * cells), BF16), v((npair, both, 4 * cells), BF16),
        v((cu, 4 * cells), BF16), v((npair, both, 4 * cells), BF16),
        v((2, 2, fw, cu), F32),
        v((3, 3, 2, cw, cu), BF16),
        v((cu, cells), BF16), v((npair, both, cells), BF16),
        v((nh, tall, 128), F32),
        v((2 * part, cj), F32), v((2 * part, cu), F32),
        v((part, cu), F32), v((part, cu), F32),
        v((part, cj), F32), v((part, cj), F32),
        v((part, wide), F32), v((part, wide), F32),
        v((nh, round_up(2 * nch, 16), lanes), BF16), v((nh, round_up(2 * nch, 16), lanes), BF16),
        v((nh, round_up(ncj, 16), taps), BF16), v((nh, round_up(ncj, 16), taps), BF16),
        v((nh, round_up(2 * cb + tall, 16), lanes), BF16), v((nh, round_up(2 * cb + tall, 16), lanes), BF16),
        pltpu.SemaphoreType.DMA((18,)), pltpu.SemaphoreType.DMA((18,)),
        pltpu.SemaphoreType.DMA((6, 9)), pltpu.SemaphoreType.DMA((6, 9)),
        pltpu.SemaphoreType.DMA((13,)),
    ]
    shape = jax.ShapeDtypeStruct
    anywhere = pl.BlockSpec(memory_space=pl.ANY)
    tops = [
        shape((nh, tall, 128), F32),
        shape((2 * cb, lanes), F32),
        shape((round_up(ncj, 8), taps), F32),
        shape((2 * nch, lanes), F32),
    ]
    left = pl.pallas_call(
        functools.partial(body, nd, nh, factor),
        out_shape=[shape(skip.shape, BF16), shape(skip.shape, BF16)] + tops,
        in_specs=[anywhere] * 6,
        out_specs=[anywhere] * 6,
        scratch_shapes=scratch,
        compiler_params=pltpu.CompilerParams(
            collective_id=0, has_side_effects=True, vmem_limit_bytes=56 * 1024 * 1024
        ),
        name="decoder",
    )(bottom[0].transpose(2, 0, 1), skip, upw, w1, w2, cotangent)
    tops[0] = shape((nh * tall, 128), F32)
    ends = [shape((cb, nh, cw), BF16), shape((27, no, cb), F32), shape((27, no, ncj), F32), shape((27, nch, no), F32)]
    outs = pl.pallas_call(
        functools.partial(closing, nh),
        out_shape=[shape(skip.shape, BF16), ends[0], shape(skip.shape, BF16)] + ends[1:],
        in_specs=[anywhere] * 6,
        out_specs=[anywhere] * 6,
        scratch_shapes=[v(one.shape, one.dtype) for one in tops + ends]
        + [v(skip.shape, BF16), v(skip.shape, BF16), pltpu.SemaphoreType.DMA((12,))],
        name="closing",
    )(*left[:2], left[2].reshape(nh * tall, 128), *left[3:])
    return (
        outs[0],
        outs[1].transpose(1, 2, 0)[None],
        outs[2],
        outs[3].reshape(3, 3, 3, no, cb).transpose(0, 1, 2, 4, 3),
        outs[4].reshape(3, 3, 3, no, ncj).transpose(0, 1, 2, 4, 3),
        outs[5].reshape(3, 3, 3, nch, no),
    )


def solution(mesh):
    return jax.shard_map(
        functools.partial(per_device, mesh.shape["depth"], mesh.shape["height"]),
        mesh=mesh,
        in_specs=(
            P("depth", None, None, "height"),
            P("depth", "height", None, None),
            P(),
            P(),
            P(),
            P("depth", "height", None, None),
        ),
        out_specs=(
            P("depth", "height", None, None),
            P("depth", None, None, "height"),
            P("depth", "height", None, None),
            P(None, None, None, "height", "depth"),
            P(None, None, None, "height", "depth"),
            P(None, None, None, "height", "depth"),
        ),
        check_vma=False,
    )
```

```python
import functools
import math

import jax
import jax.numpy as jnp
from jax import lax
from jax.experimental import pallas as pl
from jax.experimental.pallas import tpu as pltpu
from jax.sharding import PartitionSpec as P

MESH = pl.DeviceIdType.MESH
F32 = jnp.float32
BF16 = jnp.bfloat16
GRID9 = [(a, b) for a in range(3) for b in range(3)]
OTHERS = [(a, b) for a in (-1, 0, 1) for b in (-1, 0, 1) if (a, b) != (0, 0)]
NT = (((1,), (1,)), ((), ()))
PARITY_SHIFT = {0: (1, 1), 1: (0, 0), 2: (1, 0)}


def round_up(value, unit):
    return -(-value // unit) * unit


def remote(src, dst, send, recv, target):
    return pltpu.make_async_remote_copy(
        src_ref=src, dst_ref=dst, send_sem=send, recv_sem=recv, device_id=target, device_id_type=MESH
    )


class Spread:
    def __init__(self, log, me, count, target, source, slot, bulk, send, recv):
        self.me, self.count, self.target = me, count, target
        self.source, self.slot, self.bulk, self.send, self.recv = source, slot, bulk, send, recv
        self.arrived, self.log = False, log

    def start(self):
        self.log.append(self)

        def step(j, carry):
            peer = lax.rem(self.me + j, self.count)
            remote(self.source(peer), self.slot(self.me), self.send, self.recv, self.target(peer)).start()
            return carry

        lax.fori_loop(1, self.count, step, 0)

    def whole(self):
        peer = lax.rem(self.me + 1, self.count)
        return remote(self.bulk, self.bulk, self.send, self.recv, self.target(peer))

    def wait_recv(self):
        self.arrived = True
        self.whole().wait_recv()

    def wait_send(self):
        self.whole().wait_send()


class Single:
    def __init__(self, log, out, into):
        self.out, self.into = out, into
        self.arrived, self.log = False, log

    def start(self):
        self.log.append(self)
        self.out.start()

    def wait_recv(self):
        self.arrived = True
        self.into.wait_recv()

    def wait_send(self):
        self.out.wait_send()


class Halo:
    def __init__(self, log, there, copy, directions):
        self.there, self.copy, self.directions = there, copy, directions
        self.arrived, self.log = False, log

    def each(self, sign, act):
        for dd, dh in self.directions:
            @pl.when(self.there(sign * dd, sign * dh))
            def _(dd=dd, dh=dh):
                act(self.copy(dd, dh))

    def start(self):
        self.log.append(self)
        self.each(1, lambda copy: copy.start())

    def wait_recv(self):
        self.arrived = True
        self.each(-1, lambda copy: copy.wait_recv())

    def wait_send(self):
        self.each(1, lambda copy: copy.wait_send())


def shift_rows(value, by, period):
    rows = value.shape[0]
    row = lax.broadcasted_iota(jnp.int32, value.shape, 0) % period
    edge = 0 if by > 0 else period - 1
    return jnp.where(row == edge, 0.0, pltpu.roll(value, by % rows, 0))


def shift_lanes(value, by, period):
    lanes = value.shape[1]
    lane = lax.broadcasted_iota(jnp.int32, value.shape, 1) % period
    edge = 0 if by > 0 else period - 1
    return jnp.where(lane == edge, 0.0, pltpu.roll(value, by % lanes, 1))


def slope(values):
    sig = jax.nn.sigmoid(values)
    return sig * (1.0 + values * (1.0 - sig))


def dot(a, b, dims=(((1,), (0,)), ((), ()))):
    return lax.dot_general(a, b, dims, preferred_element_type=F32)


def body(
    nd, nh, factor,
    bottom_hbm, skip, upw_hbm, w1_hbm, w2_hbm, cot_hbm,
    result_hbm, gskip_hbm, cgrows, sumup_hbm, sumfirst_hbm, sumsecond_hbm,
    bottom, result, gskip, sumup, sumfirst, sumsecond, upw, w1, w2, cot, bott, bsend, brecv, near, bg, up32, joined, ug32, ug, sg, fp, hid, hg, e2, e1, et2s, et2r, et1s, et1r,
    bu32, bu, buts, butr, cgr, acc1, acc2, px2, pr2, px1, pr1, pxu, pru, gs2, gr2, gs1, gr1, gsu, gru,
    ssem, rsem, hs, hr, loc,
):
    d = lax.axis_index("depth")
    h = lax.axis_index("height")
    pair, core = d // 2, lax.rem(d, 2)
    partner = d + 1 - 2 * core
    npair = nd // 2
    cb, rows_all, cw = bottom.shape
    cu = upw.shape[2]
    cin = upw.shape[1]
    no = cu // nd
    both = 2 * no

    weights = [
        pltpu.make_async_copy(upw_hbm, upw, loc.at[0]),
        pltpu.make_async_copy(w1_hbm, w1, loc.at[1]),
        pltpu.make_async_copy(w2_hbm, w2, loc.at[2]),
        pltpu.make_async_copy(cot_hbm, cot, loc.at[3]),
    ]
    own_skip = pltpu.make_async_copy(skip, joined.at[pl.ds(1, 2), pl.ds(1, 2), :, pl.ds(cu, cu)], loc.at[4])
    own_gathered = pltpu.make_async_copy(skip, sg.at[pair], loc.at[6])

    own_bottom = pltpu.make_async_copy(bottom_hbm, bottom, loc.at[5])
    own_bottom.start()
    for copy in weights:
        copy.start()
    joined[...] = jnp.zeros_like(joined)
    own_skip.start()
    own_gathered.start()
    hid[...] = jnp.zeros_like(hid)
    e2[...] = jnp.zeros_like(e2)
    e1[...] = jnp.zeros_like(e1)
    bu[...] = jnp.zeros_like(bu)


    barrier = pltpu.get_barrier_semaphore()

    def greet_line(count, target):
        def step(j, carry):
            pl.semaphore_signal(barrier, inc=1, device_id=target(j), device_id_type=MESH)
            return carry

        lax.fori_loop(1, count, step, 0)

    greet_line(nh, lambda j: (d, lax.rem(h + j, nh)))
    greet_line(npair, lambda j: (2 * lax.rem(pair + j, npair) + core, h))

    def there(dd, dh):
        ok = None
        for pos, step, count in ((d, dd, nd), (h, dh, nh)):
            if step:
                cond = pos > 0 if step < 0 else pos < count - 1
                ok = cond if ok is None else jnp.logical_and(ok, cond)
        return ok

    for dd in (-1, 1):
        for dh in (-1, 0, 1):
            target = (lax.rem(d + dd + nd, nd), lax.rem(h + dh + nh, nh))
            pl.semaphore_signal(barrier, inc=1, device_id=target, device_id_type=MESH)

    own_bottom.wait()
    bott[...] = bottom[...].astype(F32).reshape(cb * rows_all, cw)
    lines = [bott[pl.ds(r, cb, stride=rows_all), :] for r in range(rows_all)]
    blank = jnp.zeros((cb, cw), F32)
    rest = jnp.zeros((cb, 128 - 3 * cw), F32)
    pad = jnp.zeros((bsend.shape[1] - cb, 128), F32)
    for p in range(nh):
        before = lines[p - 1] if p > 0 else blank
        after = lines[p + 1] if p < nh - 1 else blank
        window = jnp.concatenate([before, lines[p], after, rest], axis=1)
        bsend[p] = jnp.concatenate([window, pad], axis=0).astype(BF16)
    brecv[h] = bsend[h]
    pl.semaphore_wait(barrier, nh + npair + 4)

    def src_part(step):
        return {0: pl.ds(1, 2), 1: pl.ds(2, 1), -1: pl.ds(1, 1)}[step]

    def own_part(step):
        return {0: pl.ds(0, 2), 1: pl.ds(1, 1), -1: pl.ds(0, 1)}[step]

    def dst_part(step):
        return {0: pl.ds(1, 2), 1: pl.ds(0, 1), -1: pl.ds(3, 1)}[step]

    log = []

    def halo(phase, copy_of, directions=OTHERS):
        def copy(dd, dh):
            slot = (dd + 1) * 3 + dh + 1
            src, dst = copy_of(dd, dh)
            return remote(src, dst, hs.at[phase, slot], hr.at[phase, slot], (d + dd, h + dh))

        return Halo(log, there, copy, directions)

    def field_halo(phase, field):
        return halo(
            phase,
            lambda dd, dh: (
                field.at[src_part(dd), src_part(dh)],
                field.at[dst_part(dd), dst_part(dh)],
            ),
        )

    def line_h(phase, source, into):
        return Spread(
            log, h, nh, lambda p: (d, p), source, lambda s: into.at[s], into.at[pl.ds(0, nh - 1)],
            ssem.at[phase], rsem.at[phase],
        )

    def line_p(phase, source, into):
        return Spread(
            log, pair, npair, lambda p: (2 * p + core, h), source, lambda s: into.at[s],
            into.at[pl.ds(0, npair - 1)], ssem.at[phase], rsem.at[phase],
        )

    def single(phase, src, dst, target, arriving):
        sems = ssem.at[phase], rsem.at[phase]
        return Single(log, remote(src, dst, *sems, target), remote(src, arriving, *sems, target))

    rows_out = line_h(0, lambda p: bsend.at[p], brecv)
    rows_out.start()
    skip_halo = halo(
        0,
        lambda dd, dh: (
            skip.at[own_part(dd), own_part(dh)],
            joined.at[dst_part(dd), dst_part(dh), :, pl.ds(cu, cu)],
        ),
    )
    skip_halo.start()
    skip_out = line_p(17, lambda p: sg.at[pair], sg)
    own_gathered.wait()
    skip_out.start()
    rows_out.wait_recv()
    stack = [brecv[c].astype(F32)[:cb] for c in range(nh)]
    wide = near.shape[3]
    if wide > cin:
        stack.append(jnp.zeros((wide - cin, 128), F32))
    near[1] = jnp.concatenate(stack, axis=0).T[: 3 * cw].reshape(3, cw, wide).astype(BF16)

    plane_next = single(1, near.at[1], near.at[0], (lax.rem(d + 1, nd), h), near.at[0])
    plane_prev = single(2, near.at[1], near.at[2], (lax.rem(d + nd - 1, nd), h), near.at[2])
    plane_next.start()
    plane_prev.start()
    bg[core, pair] = near[1, 1:3]
    bg[0, npair] = jnp.zeros_like(near[1, 1:3])
    planes_out = line_p(6, lambda p: bg.at[core, pair], bg.at[core])
    planes_out.start()
    weights[0].wait()
    plane_next.wait_recv()
    plane_prev.wait_recv()

    coarse = []
    for s in range(3):
        plane = d - 1 + s
        here = jnp.logical_and(plane >= 0, plane < nd)
        value = near[s, :, :, 0:cin]
        coarse.append(jnp.where(here, value, jnp.zeros_like(value)))
    coarse = jnp.stack(coarse)
    first_of = {0: 1, 1: 1, 2: 0}
    for gd in range(2):
        for gh in range(2):
            total = None
            for kd in ((1,), (0, 2))[gd]:
                for kh in ((1,), (0, 2))[gh]:
                    a, b = first_of[kd], first_of[kh]
                    lhs = coarse[a : a + 2, b : b + 2].reshape(4 * cw, -1)
                    t = kd * 9 + kh * 3
                    rhs = jnp.concatenate([upw[t], upw[t + 1], upw[t + 2]], axis=1)
                    part = dot(lhs, rhs)
                    total = part if total is None else total + part
            even = total[:, cu : 2 * cu]
            odd = total[:, 2 * cu :] + shift_rows(total[:, :cu], -1, cw)
            for i in range(2):
                for j in range(2):
                    at = (i * 2 + j) * cw
                    fd, fh = 2 * i + 1 - gd, 2 * j + 1 - gh
                    up32[fd, fh, pl.ds(0, cw, stride=2), :] = even[at : at + cw]
                    up32[fd, fh, pl.ds(1, cw, stride=2), :] = odd[at : at + cw]
    for fd in range(4):
        for fh in range(4):
            inside = None
            for pos, f, count in ((d, fd, nd), (h, fh, nh)):
                cond = None
                if f == 0:
                    cond = pos > 0
                if f == 3:
                    cond = pos < count - 1
                if cond is not None:
                    inside = cond if inside is None else jnp.logical_and(inside, cond)
            value = up32[fd, fh]
            if inside is not None:
                value = jnp.where(inside, value, 0.0)
            joined[fd, fh, :, 0:cu] = value.astype(BF16)

    own_skip.wait()
    skip_halo.wait_recv()
    weights[1].wait()
    cells = 4 * 2 * cw

    def conv(field, weight):
        chans = field.shape[3]
        lhs = jnp.concatenate(
            [field[a : a + 2, b : b + 2].reshape(cells, chans) for a, b in GRID9], axis=1
        )
        rhs = jnp.concatenate(
            [
                jnp.concatenate([weight[(a * 3 + b) * 3 + c] for c in range(3)], axis=1)
                for a, b in GRID9
            ],
            axis=0,
        )
        y = dot(lhs, rhs)
        n = weight.shape[2]
        return shift_rows(y[:, :n], 1, 2 * cw) + y[:, n : 2 * n] + shift_rows(y[:, 2 * n :], -1, 2 * cw)

    def conv_back(field, weight):
        chans = field.shape[3]
        lhs = jnp.concatenate(
            [field[2 - a : 4 - a, 2 - b : 4 - b].reshape(cells, chans) for a, b in GRID9], axis=1
        )
        rhs = jnp.concatenate(
            [
                jnp.concatenate([weight[(a * 3 + b) * 3 + c] for a, b in GRID9], axis=1)
                for c in range(3)
            ],
            axis=0,
        )
        y = dot(lhs, rhs, NT)
        n = weight.shape[1]
        return shift_rows(y[:, :n], -1, 2 * cw) + y[:, n : 2 * n] + shift_rows(y[:, 2 * n :], 1, 2 * cw)

    first_pre = conv(joined, w1)
    fp[...] = first_pre
    hidden = (first_pre * jax.nn.sigmoid(first_pre)).astype(BF16)
    hid[1:3, 1:3] = hidden.reshape(2, 2, 2 * cw, cu)
    hid_halo = field_halo(2, hid)
    hid_halo.start()
    hg[pair] = hidden
    hid_out = line_p(3, lambda p: hg.at[pair], hg)
    hid_out.start()
    planes_out.wait_recv()
    planes_swap = single(
        16, bg.at[core, pl.ds(0, npair)], bg.at[core, pl.ds(0, npair)], (partner, h), bg.at[1 - core, pl.ds(0, npair)]
    )
    planes_swap.start()

    weights[2].wait()
    weights[3].wait()
    hid_halo.wait_recv()
    second_pre = conv(hid, w2)
    result[...] = (second_pre * jax.nn.sigmoid(second_pre)).astype(BF16).reshape(2, 2, 2 * cw, cu)
    err2 = (cot[...].reshape(cells, cu).astype(F32) * slope(second_pre)).astype(BF16)
    e2[1:3, 1:3] = err2.reshape(2, 2, 2 * cw, cu)
    out_result = pltpu.make_async_copy(result, result_hbm, loc.at[7])
    out_result.start()
    e2_halo = field_halo(3, e2)
    e2_halo.start()

    planes_swap.wait_recv()

    def planes_of(sd, sh):
        return bg[lax.rem(core + sd, 2), pl.ds(core * sd, npair), sh].reshape(npair * cw, wide)

    taps_of = (((1, 0),), ((2, 0), (0, 1)))
    for pd in range(2):
        for ph in range(2):
            total = None
            for kd, sd in taps_of[pd]:
                for kh, sh in taps_of[ph]:
                    t = kd * 9 + kh * 3
                    rhs = jnp.concatenate([upw[t], upw[t + 1], upw[t + 2]], axis=1)
                    part = dot(planes_of(sd, sh)[:, :cin], rhs)
                    total = part if total is None else total + part
            even = total[:, cu : 2 * cu]
            odd = total[:, 2 * cu :] + shift_rows(total[:, :cu], -1, cw)
            for k in range(npair):
                ug32[k, pd * 2 + ph, pl.ds(0, cw, stride=2), :] = even[k * cw : (k + 1) * cw]
                ug32[k, pd * 2 + ph, pl.ds(1, cw, stride=2), :] = odd[k * cw : (k + 1) * cw]
    ug[...] = ug32[...].astype(BF16).reshape(npair, cells, cu)

    def part_of(p):
        return pl.ds(pl.multiple_of(p * both, both), both)

    def flip(value, phase, out, into):
        out[...] = value.astype(F32).T.astype(BF16)
        into[pair] = out[part_of(pair)]
        spread = line_p(phase, lambda p: out.at[part_of(p)], into)
        spread.start()
        return spread

    def weight_grad(into, gathered, acc):
        acc[...] = jnp.zeros_like(acc)
        half = 2 * cw
        per_plane = 4 * half
        lane = lax.broadcasted_iota(jnp.int32, (both, 128), 1)

        def step(j, carry):
            shifted = []
            for plane in range(4):
                at = plane * per_plane
                low = into[j, :, at : at + 128].astype(F32)
                high = into[j, :, at + 128 : at + 256].astype(F32)
                mid = jnp.where(lane < half, pltpu.roll(low, half, 1), pltpu.roll(high, half, 1))
                shifted.append(
                    [
                        rows if kw == 1 else shift_lanes(rows, kw - 1, half)
                        for rows in (high, mid, low)
                        for kw in range(3)
                    ]
                )
            lhs = []
            for c in range(2):
                for kd in range(3):
                    for k in range(9):
                        pieces = [shifted[2 - kd + q][k][c * no : (c + 1) * no] for q in range(2)]
                        lhs.append(jnp.concatenate(pieces, axis=1))
            acc[...] += dot(jnp.concatenate(lhs, axis=0).astype(BF16), gathered(j))
            return carry

        lax.fori_loop(0, npair, step, 0)
        return acc[...]

    def swap(phase, value, out, into):
        half = 27 * no
        halves = [value[:half], value[half:]]
        mine = jnp.where(core == 0, halves[0], halves[1])
        theirs = jnp.where(core == 0, halves[1], halves[0])
        fill = out.shape[0] - half
        if fill:
            theirs = jnp.concatenate([theirs, jnp.zeros((fill, theirs.shape[1]), F32)], axis=0)
        out[...] = theirs.astype(BF16)
        copy = single(phase, out, into, (partner, h), into)
        copy.start()
        return copy, mine

    def flipped(value):
        rows, lanes = value.shape
        tall, wide = round_up(rows, 128), round_up(lanes, 128)
        if tall > rows:
            value = jnp.concatenate([value, jnp.zeros((tall - rows, lanes), F32)], axis=0)
        if wide > lanes:
            value = jnp.concatenate([value, jnp.zeros((tall, wide - lanes), F32)], axis=1)
        return value.T

    first_taps = 14
    split = first_taps * no
    lanes = round_up(split, 128)

    def scatter_rows(phase, swapped, arriving, chunk, out, into, folded=True, beside=None):
        copy, mine = swapped
        copy.wait_recv()
        turned = flipped((mine + arriving[...].astype(F32)[: mine.shape[0]]) * factor)
        for c in range(nh):
            piece = turned[c * chunk : (c + 1) * chunk]
            if folded:
                piece = jnp.concatenate([piece[:, :lanes], piece[:, split : split + lanes]], axis=0)
            if beside:
                piece = jnp.concatenate([piece, beside[c]], axis=0)
            fill = out.shape[1] - piece.shape[0]
            if fill:
                piece = jnp.concatenate([piece, jnp.zeros((fill, piece.shape[1]), F32)], axis=0)
            out[c] = piece.astype(BF16)
        into[h] = out[h]
        spread = line_h(phase, lambda p: out.at[p], into)
        spread.start()
        return spread

    e2_halo.wait_recv()
    err1 = (conv_back(e2, w2) * slope(fp[...])).astype(BF16)
    e1[1:3, 1:3] = err1.reshape(2, 2, 2 * cw, cu)
    e1_halo = field_halo(4, e1)
    e1_halo.start()
    e2_out = flip(e2[...].reshape(4 * cells, cu), 5, et2s, et2r)

    e1_halo.wait_recv()
    e1_out = flip(e1[...].reshape(4 * cells, cu), 8, et1s, et1r)
    back = conv_back(e1, w1)
    bu32[...] = back[:, :cu].reshape(2, 2, 2 * cw, cu)
    for i in range(2):
        for j in range(2):
            for par in range(2):
                bu[1 + i, 1 + j, par] = bu32[i, j, pl.ds(par, cw, stride=2), :].astype(BF16)
    bu_halo = halo(
        5,
        lambda dd, dh: (
            bu.at[pl.ds(2, 1) if dd else pl.ds(1, 2), pl.ds(2, 1) if dh else pl.ds(1, 2)],
            bu.at[pl.ds(0, 1) if dd else pl.ds(1, 2), pl.ds(0, 1) if dh else pl.ds(1, 2)],
        ),
        [(1, 0), (0, 1), (1, 1)],
    )
    bu_halo.start()
    bu_out = flip(bu[1:3, 1:3].reshape(cells, cu), 7, buts, butr)
    e2_out.wait_recv()
    hid_out.wait_recv()
    swap2 = swap(9, weight_grad(et2r, lambda j: hg[j], acc2), px2, pr2)

    e1_out.wait_recv()
    skip_out.wait_recv()
    swap1 = swap(13, weight_grad(et1r, lambda j: jnp.concatenate([ug[j], sg[j].reshape(cells, cu)], axis=1), acc1), px1, pr1)

    g2_out = scatter_rows(11, swap2, pr2, cu // nh, gs2, gr2)

    bu_out.wait_recv()
    per = 128 // cw
    span = npair * cw
    group = min(per, npair)
    lane = lax.broadcasted_iota(jnp.int32, (both, 128), 1) // cw
    phases = {}
    for pd in range(2):
        for p in range(per):
            groups = []
            for g in range(npair // group):
                total = None
                for s in range(group):
                    piece = butr[g * group + s, :, pd * 128 : (pd + 1) * 128].astype(F32)
                    turn = ((s - p) * cw) % 128
                    piece = pltpu.roll(piece, turn, 1) if turn else piece
                    total = piece if total is None else jnp.where(lane == s, piece, total)
                groups.append(total)
            value = jnp.concatenate(groups, axis=1) if len(groups) > 1 else groups[0]
            phases[pd, p // 2, p % 2] = value[:, :span]

    def tap_rows(kd, kh, kw):
        pw, sw = PARITY_SHIFT[kw]
        value = phases[PARITY_SHIFT[kd][0], PARITY_SHIFT[kh][0], pw]
        return shift_lanes(value, 1, cw) if sw else value

    products = {}
    for sd, kds in ((0, (1, 2)), (1, (0,))):
        for sh, khs in ((0, (1, 2)), (1, (0,))):
            order = [(kd, kh, kw) for kd in kds for kh in khs for kw in range(3)]
            lhs = jnp.concatenate([tap_rows(*k) for k in order], axis=0).astype(BF16)
            rhs = planes_of(sd, sh)
            value = dot(lhs, rhs)
            for i, k in enumerate(order):
                for c in range(2):
                    at = (i * 2 + c) * no
                    products[(c,) + k] = value[at : at + no]
    grad_up = jnp.concatenate(
        [products[c, a, b, e] for c in range(2) for a, b in GRID9 for e in range(3)], axis=0
    )
    swapu = swap(12, grad_up, pxu, pru)

    g1_out = scatter_rows(15, swap1, pr1, 2 * cu // nh, gs1, gr1, folded=False)
    bu_halo.wait_recv()
    around = lambda par: [bu[a, b, par].reshape(cw, cu) for a, b in GRID9]
    lhs = jnp.concatenate(around(0) + around(1), axis=1)
    rhs = jnp.concatenate(
        [upw[(a * 3 + b) * 3 + 1] for a, b in GRID9] + [upw[(a * 3 + b) * 3 + 2] for a, b in GRID9], axis=1
    )
    same = dot(lhs, rhs, NT)
    lhs = jnp.concatenate(around(1), axis=1)
    rhs = jnp.concatenate([upw[(a * 3 + b) * 3] for a, b in GRID9], axis=1)
    block_grad = flipped(same + shift_rows(dot(lhs, rhs, NT), 1, cw))
    share = cb // (128 // cw)
    beside = []
    for c in range(nh):
        groups = [block_grad[c * cb + q : c * cb + q + share, :cw] for q in range(0, cb, share)]
        beside.append(jnp.concatenate(groups, axis=1))
    gu_out = scatter_rows(14, swapu, pru, cb, gsu, gru, beside=beside)
    gskip[...] = back[:, cu:].astype(BF16).reshape(2, 2, 2 * cw, cu)
    out_gskip = pltpu.make_async_copy(gskip, gskip_hbm, loc.at[8])
    out_gskip.start()

    def finish(spread, into, out, hbm, at):
        spread.wait_recv()
        total = into[0].astype(F32)
        for s in range(1, nh):
            total = total + into[s].astype(F32)
        out[...] = total[: out.shape[0]]
        copy = pltpu.make_async_copy(out, hbm, loc.at[at])
        copy.start()
        return copy

    finished = [finish(g2_out, gr2, sumsecond, sumsecond_hbm, 9), finish(g1_out, gr1, sumfirst, sumfirst_hbm, 12)]
    sent = len(log) - 1
    for part in log[:sent]:
        part.wait_send()
    finished.append(finish(gu_out, gru, sumup, sumup_hbm, 11))
    base = 2 * cb // 16 * 16
    for s in range(nh):
        cgr[s] = gru[s, base : gru.shape[1]].astype(F32)[2 * cb - base : 2 * cb - base + cgr.shape[1]]
    out_cg = pltpu.make_async_copy(cgr, cgrows, loc.at[10])
    out_cg.start()
    for copy in finished + [out_cg, out_result, out_gskip]:
        copy.wait()

    for part in log[sent:]:
        if not part.arrived:
            part.wait_recv()
        part.wait_send()


def tall_turn(value):
    rows = value.shape[0]
    if rows < 128:
        value = jnp.concatenate([value, jnp.zeros((128 - rows, value.shape[1]), F32)], axis=0)
    return value.T


def closing(nh, *refs):
    (result, gskip, *left), (out0, out1h, out2, *grads), (cgrows, sumup, sumfirst, sumsecond) = (
        refs[:6], refs[6:12], refs[12:16]
    )
    out1, out3, out4, out5, pass0, pass1, sems = refs[16:]
    stages = (cgrows, sumup, sumfirst, sumsecond)
    into = [pltpu.make_async_copy(src, dst, sems.at[i]) for i, (src, dst) in enumerate(zip(left, stages))]
    through = [pltpu.make_async_copy(result, pass0, sems.at[4]), pltpu.make_async_copy(gskip, pass1, sems.at[5])]
    whole = [pltpu.make_async_copy(pass0, out0, sems.at[10]), pltpu.make_async_copy(pass1, out2, sems.at[11])]
    for copy in into + through:
        copy.start()
    cb, rows, cw = out1.shape
    tall = cgrows.shape[0] // nh
    per = 128 // cw
    share = cb // per
    away = [
        pltpu.make_async_copy(src, dst, sems.at[6 + i])
        for i, (src, dst) in enumerate(zip((out1, out3, out4, out5), [out1h] + grads))
    ]
    into[0].wait()
    for i in range(share):
        line = cgrows[pl.ds(i, nh, stride=tall), :].astype(BF16)
        for q in range(per):
            out1[q * share + i] = line[:, q * cw : (q + 1) * cw]
    away[0].start()
    for arriving, leaving in zip(through, whole):
        arriving.wait()
        leaving.start()
    no = out3.shape[1]
    into[2].wait()
    n = out4.shape[2]
    out4[...] = tall_turn(sumfirst[...])[: 27 * no, :n].reshape(27, no, n)
    away[2].start()
    into[1].wait()
    n = out3.shape[2]
    turned = tall_turn(sumup[...])
    out3[:14] = turned[: 14 * no, :n].reshape(14, no, n)
    out3[14:] = turned[: 13 * no, n : 2 * n].reshape(13, no, n)
    away[1].start()
    into[3].wait()
    total = sumsecond[...]
    n = out5.shape[1]
    for t in range(27):
        row, at = (0, t) if t < 14 else (n, t - 14)
        out5[t] = total[row : row + n, at * no : (at + 1) * no]
    away[3].start()
    for copy in whole + away:
        copy.wait()


def per_device(nd, nh, bottom, skip, upconv_kernel, w_first, w_second, cotangent):
    cb, cw = bottom.shape[3], bottom.shape[2]
    cin, cu = upconv_kernel.shape[3:]
    fw = skip.shape[2]
    cj = w_first.shape[3]
    no = cu // nd
    both, npair = 2 * no, nd // 2
    rows = skip.shape[:2]
    factor = 1.0 / math.sqrt(rows[0] * nd * rows[1] * nh * fw)
    taps = round_up(27 * no, 128)
    ncj, nch = cj // nh, cu // nh
    v = pltpu.VMEM
    upw = upconv_kernel.reshape(27, cin, cu)
    w1 = w_first.reshape(27, cj, cu)
    w2 = w_second.reshape(27, cu, cu)
    cells = rows[0] * rows[1] * fw
    wide = round_up(cin, 128)
    part = 27 * no
    tall = round_up(cb * cw // 128, 8)
    lanes = round_up(14 * no, 128)
    scratch = [
        v((cb, nh, cw), BF16), v(skip.shape, BF16), v(skip.shape, BF16),
        v((2 * cb, lanes), F32), v((round_up(ncj, 8), taps), F32), v((2 * nch, lanes), F32),
        v(upw.shape, BF16), v(w1.shape, BF16), v(w2.shape, BF16), v(cotangent.shape, BF16),
        v((cb * nh, cw), F32),
        v((nh, round_up(cb, 16), 128), BF16), v((nh, round_up(cb, 16), 128), BF16),
        v((3, 3, cw, wide), BF16),
        v((2, npair + 1, 2, cw, wide), BF16),
        v((4, 4, fw, cu), F32),
        v((4, 4, fw, cj), BF16),
        v((npair, 4, fw, cu), F32),
        v((npair, cells, cu), BF16),
        v((npair,) + skip.shape, BF16),
        v((cells, cu), F32),
        v((4, 4, fw, cu), BF16),
        v((npair, cells, cu), BF16),
        v((4, 4, fw, cu), BF16),
        v((4, 4, fw, cu), BF16),
        v((cu, 4 * cells), BF16), v((npair, both, 4 * cells), BF16),
        v((cu, 4 * cells), BF16), v((npair, both, 4 * cells), BF16),
        v((2, 2, fw, cu), F32),
        v((3, 3, 2, cw, cu), BF16),
        v((cu, cells), BF16), v((npair, both, cells), BF16),
        v((nh, tall, 128), F32),
        v((2 * part, cj), F32), v((2 * part, cu), F32),
        v((round_up(part, 16), cu), BF16), v((round_up(part, 16), cu), BF16),
        v((round_up(part, 16), cj), BF16), v((round_up(part, 16), cj), BF16),
        v((round_up(part, 16), wide), BF16), v((round_up(part, 16), wide), BF16),
        v((nh, round_up(2 * nch, 16), lanes), BF16), v((nh, round_up(2 * nch, 16), lanes), BF16),
        v((nh, round_up(ncj, 16), taps), BF16), v((nh, round_up(ncj, 16), taps), BF16),
        v((nh, round_up(2 * cb + tall, 16), lanes), BF16), v((nh, round_up(2 * cb + tall, 16), lanes), BF16),
        pltpu.SemaphoreType.DMA((18,)), pltpu.SemaphoreType.DMA((18,)),
        pltpu.SemaphoreType.DMA((6, 9)), pltpu.SemaphoreType.DMA((6, 9)),
        pltpu.SemaphoreType.DMA((13,)),
    ]
    shape = jax.ShapeDtypeStruct
    anywhere = pl.BlockSpec(memory_space=pl.ANY)
    tops = [
        shape((nh, tall, 128), F32),
        shape((2 * cb, lanes), F32),
        shape((round_up(ncj, 8), taps), F32),
        shape((2 * nch, lanes), F32),
    ]
    left = pl.pallas_call(
        functools.partial(body, nd, nh, factor),
        out_shape=[shape(skip.shape, BF16), shape(skip.shape, BF16)] + tops,
        in_specs=[anywhere] * 6,
        out_specs=[anywhere] * 6,
        scratch_shapes=scratch,
        compiler_params=pltpu.CompilerParams(
            collective_id=0, has_side_effects=True, vmem_limit_bytes=56 * 1024 * 1024
        ),
        name="decoder",
    )(bottom[0].transpose(2, 0, 1), skip, upw, w1, w2, cotangent)
    tops[0] = shape((nh * tall, 128), F32)
    ends = [shape((cb, nh, cw), BF16), shape((27, no, cb), F32), shape((27, no, ncj), F32), shape((27, nch, no), F32)]
    outs = pl.pallas_call(
        functools.partial(closing, nh),
        out_shape=[shape(skip.shape, BF16), ends[0], shape(skip.shape, BF16)] + ends[1:],
        in_specs=[anywhere] * 6,
        out_specs=[anywhere] * 6,
        scratch_shapes=[v(one.shape, one.dtype) for one in tops + ends]
        + [v(skip.shape, BF16), v(skip.shape, BF16), pltpu.SemaphoreType.DMA((12,))],
        name="closing",
    )(*left[:2], left[2].reshape(nh * tall, 128), *left[3:])
    return (
        outs[0],
        outs[1].transpose(1, 2, 0)[None],
        outs[2],
        outs[3].reshape(3, 3, 3, no, cb).transpose(0, 1, 2, 4, 3),
        outs[4].reshape(3, 3, 3, no, ncj).transpose(0, 1, 2, 4, 3),
        outs[5].reshape(3, 3, 3, nch, no),
    )


def solution(mesh):
    return jax.shard_map(
        functools.partial(per_device, mesh.shape["depth"], mesh.shape["height"]),
        mesh=mesh,
        in_specs=(
            P("depth", None, None, "height"),
            P("depth", "height", None, None),
            P(),
            P(),
            P(),
            P("depth", "height", None, None),
        ),
        out_specs=(
            P("depth", "height", None, None),
            P("depth", None, None, "height"),
            P("depth", "height", None, None),
            P(None, None, None, "height", "depth"),
            P(None, None, None, "height", "depth"),
            P(None, None, None, "height", "depth"),
        ),
        check_vma=False,
    )
```
